32 devices in a mesh: seg: 4 (over x, core), chan: 8 (over z, y).
Axes of the slice: x: 2, y: 2, z: 4, core: 2. Of those that a mesh axis runs over, the one named last changes fastest.
Arguments:
- traces: bfloat16 [32, 1024, 4096], P('seg', 'chan'), may hold values from -6 to 6
- channel_mask: int32 [1024], P('chan'), may hold values 0 or 1
- owner_ids: int32 [8, 64, 1], P('chan'), may hold values from 0 to 7; in each aligned block of 64 rows (0 to 63, 64 to 127, ..., all dimensions but the last counted through in order) at most 16 rows name the same one
- local_bins: int32 [8, 64], P('chan'), may hold values from 0 to 7
Outputs:
- stacks: float32 [64, 2048], P('chan')
The draws below stay inside these ranges and needn't reach their ends.
Inputs may be any that keep to these rules, and one draw needn't show every extreme that they name: `owner_ids`: among the 64 tiles of one block no owner is named more than 16 times, a bound that some block reaches.
All inputs are finite; a program needn't handle non-finite values. No bound on the sum of `channel_mask` on one device may be relied on, other than what follows from the above.
Results may differ from the reference program's by a relative error of at most 0.0053.
Values may be sent and summed in bfloat16 or wider, within the bound.
No kernel may reach another device: no remote copies, remote signals or barrier semaphores. Data moves between devices by JAX's collectives and lax.ppermute only.
A program may use at most 192 MiB of HBM per device.

```python
import math
import jax
import jax.numpy as jnp
import numpy as np
from jax import lax

CB = 128
NT = 4096
DEC = 2
K0 = 8
HW = 64
R = 4
G = 16
BIN_DEV = 8
NB = 1024
NLAG = 2048
TILES = 64
SEGS = 32
NBLK = 8
CHANNELS = 1024
NBIN = 64
CAP = 16
N_CHAN = 8


def with_ends(values, rng, least, high):
    index_at = [jax.random.randint(jax.random.fold_in(rng, axis), (), 0, length) for axis, length in enumerate(values.shape)]
    main_axis = values.shape.index(max(values.shape))
    neighbour = index_at[:main_axis] + [(index_at[main_axis] + 1) % values.shape[main_axis]] + index_at[main_axis + 1:]
    return values.at[tuple(index_at)].set(least).at[tuple(neighbour)].set(high)


def level_of(own_key, dims, split, low, high):
    loudness, own = 1.0, jax.random.fold_in(own_key, 6)
    for dim, shards_of in split:
        steps = jnp.exp(jax.random.uniform(jax.random.fold_in(own, dim), (shards_of,), jnp.float32, low / len(split), high / len(split)))
        loudness = loudness * jnp.repeat(steps, dims[dim] // shards_of).reshape([-1 if axis == dim else 1 for axis in range(len(dims))])
    return loudness


def deal_out(rng, own, number, rows, count, top, most, slope):
    ranking = jax.random.permutation(rng, count)
    heavy_load, usual = portions_of(count, rows * top, most, slope, True), portions_of(count, rows * top, most, slope, False)
    places = jnp.arange(count)

    def named(lengths, offset_by):
        used = int((lengths > 0).sum())
        fixed = max(1, used // 4)
        shifted = fixed + (places - fixed + offset_by * (used - fixed)) % max(1, count - fixed)
        return jnp.zeros((count,), jnp.int32).at[ranking[jnp.where(places < fixed, places, shifted)]].set(jnp.asarray(lengths, jnp.int32))

    lengths = jnp.where(number % 4 == 0, named(heavy_load, number // 4), named(usual, number - number // 4 - 1))
    mixed = jax.random.permutation(jax.random.fold_in(own, 3), count)
    source_of, receiver = mixed[0:count // 2 * 2:2], mixed[1:count // 2 * 2:2]
    slack = jnp.minimum(lengths[source_of] - 1, most - lengths[receiver]) // 2
    slack = jnp.where((source_of == ranking[0]) | (receiver == ranking[0]) | (lengths[receiver] == 0), 0, jnp.maximum(slack, 0))
    shifted = jax.random.randint(jax.random.fold_in(own, 4), (count // 2,), 0, 1 << 20) % (slack + 1)
    lengths = lengths.at[source_of].add(-shifted).at[receiver].add(shifted)
    items = jnp.searchsorted(jnp.cumsum(lengths), jnp.arange(rows * top), side="right").astype(jnp.int32)
    table = items.reshape(top, rows).T
    table = table[jax.random.permutation(jax.random.fold_in(own, 1), rows)]
    offset_by = jax.random.randint(jax.random.fold_in(own, 2), (rows, 1), 0, top)
    return jnp.take_along_axis(table, (jnp.arange(top)[None, :] + offset_by) % top, axis=1)


def portions_of(count, total, reach, lean, full):
    weights = [(1 << 20) // math.isqrt(rank ** lean) + 1 for rank in range(1, count + 1)]
    largest = reach if full else min(reach, max(-(-total // count), total * weights[0] // sum(weights)))
    least = 1 if total - largest >= count - 1 else 0
    given, spare = [largest] + [least] * (count - 1), total - largest - least * (count - 1)
    while spare > 0:
        movable = [i for i in range(1, count) if given[i] < largest] or [i for i in range(1, count) if given[i] < reach]
        whole, budget = sum([weights[i] for i in movable]), spare
        for i in movable:
            extra = min(reach - given[i], max(1, budget * weights[i] // whole), spare)
            given[i] = given[i] + extra
            spare = spare - extra
    return np.array(given)


def noise(rng, dims, spread, reach, cuts=(), held_as=jnp.bfloat16):
    gain = level_of(rng, dims, cuts, -0.22, 0.18) if cuts else 1.0
    values = jax.random.normal(rng, dims, jnp.float32) * spread * gain
    return jnp.minimum(jnp.maximum(values, -reach), reach).astype(held_as)


def setup_inputs(seed: int = 0) -> dict:
    arg_keys = jax.random.split(jax.random.key(seed), 5)
    traces = noise(arg_keys[0], (SEGS, CHANNELS, NT), 1.0, 6.0, ((0, 4), (1, 8)))
    channel_mask = with_ends((jax.random.randint(arg_keys[1], (CHANNELS,), 0, 4) < 3).astype(jnp.int32), jax.random.fold_in(arg_keys[1], 1), 0, 1)
    owner_ids_keys = jax.random.split(jax.random.fold_in(arg_keys[2], 1), NBLK * TILES // TILES)
    owner_ids_turns = jax.random.permutation(jax.random.fold_in(arg_keys[2], 3), NBLK * TILES // TILES)
    owner_ids = jax.vmap(lambda own, number: deal_out(jax.random.fold_in(arg_keys[2], 2), own, number, TILES, N_CHAN, 1, CAP, 2))(owner_ids_keys, owner_ids_turns).reshape((NBLK, TILES, 1))
    local_bins = with_ends(jax.random.randint(arg_keys[3], (NBLK, TILES), 0, BIN_DEV), jax.random.fold_in(arg_keys[3], 1), 0, BIN_DEV - 1).astype(jnp.int32)
    return {"traces": traces, "channel_mask": channel_mask, "owner_ids": owner_ids, "local_bins": local_bins}


EPSILON = 1e-06

def forward_table():
    samples = jnp.arange(NT, dtype=jnp.int32)
    freqs = K0 + jnp.arange(NB, dtype=jnp.int32)
    phase = samples[:, None] * freqs[None, :] % NT
    angle = phase.astype(jnp.float32) * (2.0 * math.pi / NT)
    return jnp.concatenate([jnp.cos(angle), -jnp.sin(angle)], axis=1).astype(jnp.bfloat16)

def band_table():
    freqs = jnp.arange(NB, dtype=jnp.int32)
    return (jnp.abs(freqs[:, None] - freqs[None, :]) <= HW).astype(jnp.float32)

def inverse_table():
    freqs = K0 + jnp.arange(NB, dtype=jnp.int32)
    delays = (jnp.arange(NLAG, dtype=jnp.int32) - NLAG // 2) * DEC
    phase = jnp.mod(freqs[:, None] * delays[None, :], NT)
    angle = phase.astype(jnp.float32) * (2.0 * math.pi / NT)
    scale = 1.0 / math.sqrt(NB)
    return jnp.concatenate([jnp.cos(angle) * scale, -jnp.sin(angle) * scale], axis=0)

def whiten(block, mask_float, table, band):
    segs, chans, length = block.shape
    spectrum = jnp.dot(block.reshape(segs * chans, length), table, preferred_element_type=jnp.float32)
    half = spectrum.shape[1] // 2
    real_part = spectrum[:, :half]
    imag_part = spectrum[:, half:]
    power = real_part * real_part + imag_part * imag_part
    counts = lax.optimization_barrier(jnp.sum(band, axis=0))
    level = jnp.sqrt(jnp.dot(power, band, precision=lax.Precision.HIGHEST) / counts + EPSILON)
    weight = jnp.tile(mask_float, segs)[:, None] / level
    result = jnp.concatenate([real_part * weight, imag_part * weight], axis=1)
    return result.astype(jnp.bfloat16).reshape(segs, chans, 2 * half)

def cross(source, source_mask, target, target_mask, total_segs):
    half = source.shape[-1] // 2
    source_float = source.astype(jnp.float32)
    target_float = target.astype(jnp.float32)
    source_real = source_float[..., :half]
    source_imag = source_float[..., half:]
    target_real = target_float[..., :half]
    target_imag = target_float[..., half:]
    real_sum = lax.optimization_barrier(jnp.sum(source_real * target_real + source_imag * target_imag, axis=0))
    imag_sum = lax.optimization_barrier(jnp.sum(source_imag * target_real - source_real * target_imag, axis=0))
    chans = real_sum.shape[0]
    real_groups = real_sum.reshape(G, chans // G, half).sum(axis=1)
    imag_groups = imag_sum.reshape(G, chans // G, half).sum(axis=1)
    counts = (source_mask * target_mask).reshape(G, chans // G).sum(axis=1)
    scale = 1.0 / (total_segs * jnp.maximum(counts, 1.0))
    return jnp.concatenate([real_groups, imag_groups], axis=1) * scale[:, None]

def reference(traces, channel_mask, owner_ids, local_bins):
    table = forward_table()
    band = band_table()
    masks = channel_mask.astype(jnp.float32).reshape(NBLK, CB)

    def whiten_block(index):
        block = lax.dynamic_slice_in_dim(traces, index * CB, CB, 1)
        row_mask = lax.dynamic_index_in_dim(masks, index, 0, keepdims=False)
        return whiten(block, row_mask, table, band)
    whitened = lax.map(whiten_block, jnp.arange(NBLK, dtype=jnp.int32))
    padded = jnp.concatenate([whitened, jnp.zeros((R,) + whitened.shape[1:], jnp.bfloat16)], axis=0)
    padded_masks = jnp.concatenate([masks, jnp.zeros((R, CB), jnp.float32)], axis=0)

    def block_tiles(index):
        source = lax.dynamic_index_in_dim(padded, index, 0, keepdims=False)
        source_mask = lax.dynamic_index_in_dim(padded_masks, index, 0, keepdims=False)
        pieces = []
        for offset in range(1, R + 1):
            target = lax.dynamic_index_in_dim(padded, index + offset, 0, keepdims=False)
            target_mask = lax.dynamic_index_in_dim(padded_masks, index + offset, 0, keepdims=False)
            pieces.append(cross(source, source_mask, target, target_mask, SEGS))
        return jnp.concatenate(pieces, axis=0)
    tiles = lax.map(block_tiles, jnp.arange(NBLK, dtype=jnp.int32))
    lags = jnp.dot(tiles.reshape(NBLK * TILES, 2 * NB), inverse_table(), precision=lax.Precision.HIGHEST)
    labels = (owner_ids.reshape(-1) * BIN_DEV + local_bins.reshape(-1)).astype(jnp.int32)
    return jax.ops.segment_sum(lags, labels, num_segments=NBIN)
```

```python
import functools
import math

import jax
import jax.numpy as jnp
import ml_dtypes
import numpy as np
from jax import lax
from jax.experimental import pallas as pl
from jax.experimental.pallas import tpu as pltpu
from jax.sharding import PartitionSpec as P

NT = 4096
DEC = 2
K0 = 8
HW = 64
R = 4
G = 16
BIN_DEV = 8
NB = 1024
NLAG = 2048
EPSILON = 1e-06

LANES = 128
SLICES = NB // LANES
FOLD = 4
CLASS = NB // FOLD
QUARTER = NT // FOLD
LAGQ = NLAG // FOLD
VMEM = 56 * 1024 * 1024


ORDER = np.arange(NB).reshape(CLASS, FOLD).T.reshape(-1)


def forward_tables():
    samples = np.arange(NT // 2, dtype=np.int64)
    freqs = K0 + ORDER.astype(np.int64)
    phase = samples[:, None] * freqs[None, :] % NT
    angle = (phase.astype(np.float32) * np.float32(2.0 * math.pi / NT)).astype(np.float64)
    cos = np.cos(angle).astype(np.float32).astype(ml_dtypes.bfloat16)
    sin = (-np.sin(angle)).astype(np.float32).astype(ml_dtypes.bfloat16)

    def part(which, rows):
        columns = slice(which * CLASS, (which + 1) * CLASS)
        return [cos[:rows, columns], sin[:rows, columns]]

    zero = np.concatenate(part(0, QUARTER), axis=1)
    two = np.concatenate(part(2, QUARTER), axis=1)
    odd = np.concatenate(part(1, 2 * QUARTER) + part(3, 2 * QUARTER), axis=1)
    return zero, two, odd


def band_tables():
    band = np.abs(ORDER[:, None] - ORDER[None, :]) <= HW
    counts = band.sum(axis=0).astype(np.float32)
    return band.astype(ml_dtypes.bfloat16), (1.0 / counts)[None, :].astype(np.float32)


def inverse_tables():
    freqs = K0 + ORDER.astype(np.int64)
    delays = (np.arange(2 * LAGQ, dtype=np.int64) - NLAG // 2) * DEC
    phase = np.mod(freqs[:, None] * delays[None, :], NT)
    angle = phase.astype(np.float64) * (2.0 * math.pi / NT)
    scale = 1.0 / math.sqrt(NB)
    real = (np.cos(angle) * scale).reshape(SLICES, 1, LANES, 2 * LAGQ)
    imag = (-np.sin(angle) * scale).reshape(SLICES, 1, LANES, 2 * LAGQ)
    rows = np.concatenate([real, imag], axis=1).reshape(FOLD, 2 * CLASS, 2 * LAGQ)
    zero = rows[0][:, :LAGQ]
    two = rows[2][:, :LAGQ]
    odd = np.concatenate([rows[1], rows[3]], axis=0)
    return [table.astype(np.float32).astype(ml_dtypes.bfloat16) for table in (zero, two, odd)]


def spectra_kernel(x_ref, mask_ref, zero_ref, two_ref, odd_ref, band_ref, inverse_ref, out_ref, hold):
    f32, bf16 = jnp.float32, jnp.bfloat16
    x = [x_ref[:, m * QUARTER:(m + 1) * QUARTER].astype(f32) for m in range(FOLD)]
    even, odd = x[0] + x[2], x[1] + x[3]
    first = jnp.dot((even + odd).astype(bf16), zero_ref[...], preferred_element_type=f32)
    third = jnp.dot((even - odd).astype(bf16), two_ref[...], preferred_element_type=f32)
    others = jnp.dot((x[0] - x[2]).astype(bf16), odd_ref[:QUARTER], preferred_element_type=f32)
    others += jnp.dot((x[1] - x[3]).astype(bf16), odd_ref[QUARTER:], preferred_element_type=f32)
    parts = [first, others[:, :2 * CLASS], third, others[:, 2 * CLASS:]]
    power = [part[:, :CLASS] * part[:, :CLASS] + part[:, CLASS:] * part[:, CLASS:] for part in parts]
    power = jnp.concatenate(power, axis=1).astype(bf16)
    mean = jnp.dot(power, band_ref[...], preferred_element_type=f32) * inverse_ref[...]
    weight = mask_ref[...] * lax.rsqrt(mean + EPSILON)
    rows = x_ref.shape[0]
    per_group = LANES // G
    for piece in range(SLICES):
        part, start = parts[piece // 2], (piece % 2) * LANES
        scale = weight[:, piece * LANES:(piece + 1) * LANES]
        hold[0] = part[:, start:start + LANES] * scale
        hold[1] = part[:, CLASS + start:CLASS + start + LANES] * scale
        for seg in range(rows // LANES):
            for j in range(per_group):
                at = seg * LANES + j * G
                for half in range(2):
                    taken = hold[half, pl.ds(seg * LANES + j, G, stride=per_group), :]
                    out_ref[piece, at:at + G, half * LANES:(half + 1) * LANES] = taken.astype(bf16)


def spectra(traces, mask_column, first_row, rows, block):
    tables = forward_tables() + band_tables()
    whole = [pl.BlockSpec(table.shape, lambda i: (0, 0)) for table in tables]
    skip = first_row // block
    return pl.pallas_call(
        spectra_kernel,
        grid=(rows // block,),
        in_specs=[
            pl.BlockSpec((block, NT), lambda i: (i + skip, 0)),
            pl.BlockSpec((block, 1), lambda i: (0, 0)),
        ] + whole,
        out_specs=pl.BlockSpec((SLICES, block, 2 * LANES), lambda i: (0, i, 0)),
        out_shape=jax.ShapeDtypeStruct((SLICES, rows, 2 * LANES), jnp.bfloat16),
        scratch_shapes=[pltpu.VMEM((2, block, LANES), jnp.float32)],
        compiler_params=pltpu.CompilerParams(vmem_limit_bytes=VMEM),
        cost_estimate=pl.CostEstimate(
            flops=8 * rows * NB * NB, bytes_accessed=rows * NT * 3 + 8 * NB * NB, transcendentals=rows * NB
        ),
        name="spectra",
    )(traces, mask_column, *[jnp.asarray(table) for table in tables])


def cross_kernel(blocks, steps, wide_ref, selector_ref, out_ref, tiles):
    f32 = jnp.float32
    tiles[...] = jnp.zeros_like(tiles)
    for source in range(0, blocks, 2):
        pairs = [
            (b, b + d) for b in (source, source + 1) for d in range(1, R + 1) if b + d < blocks and b < blocks
        ]
        if not pairs:
            continue
        needed = sorted({b for pair in pairs for b in pair})

        def body(step, sums):
            at = pl.ds(pl.multiple_of(step * G, G), G)
            real = {b: wide_ref[b, at, :LANES].astype(f32) for b in needed}
            imag = {b: wide_ref[b, at, LANES:].astype(f32) for b in needed}
            new = []
            for (a, b), (re, im) in zip(pairs, sums):
                re = re + (real[a] * real[b] + imag[a] * imag[b])
                im = im + (imag[a] * real[b] - real[a] * imag[b])
                new.append((re, im))
            return tuple(new)

        zero = jnp.zeros((G, LANES), f32)
        sums = lax.fori_loop(0, steps, body, tuple((zero, zero) for _ in pairs))
        for (a, b), (re, im) in zip(pairs, sums):
            row = a * R * G + (b - a - 1) * G
            tiles[row:row + G, :LANES] = re
            tiles[row:row + G, LANES:] = im
    stacked = jnp.dot(
        selector_ref[...], tiles[...], precision=lax.Precision.HIGHEST, preferred_element_type=f32
    ).astype(out_ref.dtype)
    for copy in range(out_ref.shape[0]):
        out_ref[copy] = stacked


def cross_stacks(wide, selector, copies):
    blocks, rows, width = wide.shape
    return pl.pallas_call(
        functools.partial(cross_kernel, blocks, rows // G),
        out_shape=jax.ShapeDtypeStruct((copies, selector.shape[0], width), jnp.bfloat16),
        scratch_shapes=[pltpu.VMEM((blocks * R * G, width), jnp.float32)],
        compiler_params=pltpu.CompilerParams(vmem_limit_bytes=VMEM),
        name="cross",
    )(wide, selector)


def lags_kernel(stacks_ref, zero_ref, two_ref, odd_ref, out_ref):
    f32, bf16 = jnp.float32, jnp.bfloat16
    copies = stacks_ref.shape[0] // SLICES
    pieces = []
    for piece in range(SLICES):
        total = stacks_ref[piece].astype(f32)
        for copy in range(1, copies):
            total += stacks_ref[copy * SLICES + piece].astype(f32)
        pieces.append(total)

    def product(values, table):
        high = values.astype(bf16)
        low = (values - high.astype(f32)).astype(bf16)
        both = jnp.dot(jnp.concatenate([high, low], axis=0), table, preferred_element_type=f32)
        return both[:BIN_DEV] + both[BIN_DEV:]

    zero = product(jnp.concatenate(pieces[0:2], axis=1), zero_ref[...])
    two = product(jnp.concatenate(pieces[4:6], axis=1), two_ref[...])
    odd = product(jnp.concatenate(pieces[2:4] + pieces[6:8], axis=1), odd_ref[...])
    plus, minus = zero + two, zero - two
    out_ref[:, :LAGQ] = plus + odd[:, :LAGQ]
    out_ref[:, LAGQ:2 * LAGQ] = minus + odd[:, LAGQ:]
    out_ref[:, 2 * LAGQ:3 * LAGQ] = plus - odd[:, :LAGQ]
    out_ref[:, 3 * LAGQ:] = minus - odd[:, LAGQ:]


def lags(stacks):
    tables = [jnp.asarray(table) for table in inverse_tables()]
    return pl.pallas_call(
        lags_kernel,
        out_shape=jax.ShapeDtypeStruct((BIN_DEV, NLAG), jnp.float32),
        compiler_params=pltpu.CompilerParams(vmem_limit_bytes=VMEM),
        name="lags",
    )(stacks, *tables)


def selector_of(channel_mask, owner_ids, local_bins, total_segs, blocks):
    own = jnp.concatenate([channel_mask, owner_ids.reshape(-1) * BIN_DEV + local_bins.reshape(-1)])
    every = lax.all_gather(own, "chan", axis=0, tiled=False)
    chans = channel_mask.shape[0]
    masks = every[:, :chans].astype(jnp.float32).reshape(blocks, G, chans // G)
    labels = every[:, chans:].reshape(-1)
    padded = jnp.concatenate([masks, jnp.zeros((R,) + masks.shape[1:], jnp.float32)], axis=0)
    counts = jnp.stack(
        [jnp.sum(masks * padded[d:d + blocks], axis=2) for d in range(1, R + 1)], axis=1
    ).reshape(-1)
    scale = 1.0 / (total_segs * jnp.maximum(counts, 1.0))
    bins = jnp.arange(blocks * BIN_DEV, dtype=labels.dtype)
    return jnp.where(labels[None, :] == bins[:, None], scale[None, :], 0.0)


def per_device(traces, channel_mask, owner_ids, local_bins):
    seg_count = lax.axis_size("seg")
    chan_count = lax.axis_size("chan")
    segs, chans, length = traces.shape
    total_segs = segs * seg_count
    rows = segs * chans
    block = 2 * chans
    narrow = SLICES * LANES // chan_count
    splits = LANES // narrow
    selector = selector_of(channel_mask, owner_ids, local_bins, total_segs, chan_count)
    mask_column = jnp.tile(channel_mask.astype(jnp.float32), 2)[:, None]
    outgoing = spectra(traces.reshape(rows, length), mask_column, 0, rows, block)
    if splits > 1:
        outgoing = outgoing.reshape(SLICES, rows, 2, splits, narrow).transpose(0, 3, 1, 2, 4)
        outgoing = outgoing.reshape(chan_count, rows, 2 * narrow)
    wide = lax.all_to_all(outgoing, "chan", split_axis=0, concat_axis=0, tiled=True)
    if splits > 1:
        wide = wide.reshape(chan_count, rows, 2, narrow)
        wide = jnp.pad(wide, ((0, 0), (0, 0), (0, 0), (0, LANES - narrow)))
        wide = wide.reshape(chan_count, rows, 2 * LANES)
    stacks = cross_stacks(wide, selector, seg_count)
    stacks = stacks.reshape(seg_count * chan_count, BIN_DEV, 2 * LANES)
    if splits > 1:
        stacks = stacks.reshape(-1, BIN_DEV, 2, LANES)[..., :narrow].reshape(-1, BIN_DEV, 2 * narrow)
    stacks = lax.all_to_all(stacks, ("seg", "chan"), split_axis=0, concat_axis=0, tiled=True)
    if splits > 1:
        stacks = stacks.reshape(seg_count, SLICES, splits, BIN_DEV, 2, narrow).transpose(0, 1, 3, 4, 2, 5)
        stacks = stacks.reshape(seg_count * SLICES, BIN_DEV, 2 * LANES)
    return lags(stacks)


def solution(mesh):
    in_specs = (P("seg", "chan", None), P("chan"), P("chan", None, None), P("chan", None))
    out_specs = P("chan", None)
    return jax.shard_map(
        per_device, mesh=mesh, in_specs=in_specs, out_specs=out_specs, check_vma=False
    )
```

```python
import functools
import math

import jax
import jax.numpy as jnp
import ml_dtypes
import numpy as np
from jax import lax
from jax.experimental import pallas as pl
from jax.experimental.pallas import tpu as pltpu
from jax.sharding import PartitionSpec as P

NT = 4096
DEC = 2
K0 = 8
HW = 64
R = 4
G = 16
BIN_DEV = 8
NB = 1024
NLAG = 2048
EPSILON = 1e-06

LANES = 128
SLICES = NB // LANES
FOLD = 4
CLASS = NB // FOLD
QUARTER = NT // FOLD
LAGQ = NLAG // FOLD
VMEM = 32 * 1024 * 1024
BLOCK = 256
META = 16

SENT = (4, 3, 5, 2, 6, 1, 7)


ORDER = np.arange(NB).reshape(CLASS, FOLD).T.reshape(-1)


def forward_tables():
    samples = np.arange(NT // 2, dtype=np.int64)
    freqs = K0 + ORDER.astype(np.int64)
    phase = samples[:, None] * freqs[None, :] % NT
    angle = (phase.astype(np.float32) * np.float32(2.0 * math.pi / NT)).astype(np.float64)
    cos = np.cos(angle).astype(np.float32).astype(ml_dtypes.bfloat16)
    sin = (-np.sin(angle)).astype(np.float32).astype(ml_dtypes.bfloat16)

    def part(which, rows):
        columns = slice(which * CLASS, (which + 1) * CLASS)
        return [cos[rows, columns], sin[rows, columns]]

    low, high = slice(0, QUARTER), slice(QUARTER, 2 * QUARTER)
    band = (np.abs(ORDER[:, None] - ORDER[None, :]) <= HW).astype(ml_dtypes.bfloat16)
    table = np.concatenate(
        [
            np.concatenate(part(0, low) + part(2, low), axis=1),
            np.concatenate(part(1, low) + part(3, low), axis=1),
            np.concatenate(part(1, high) + part(3, high), axis=1),
            band,
        ],
        axis=0,
    )
    counts = band.astype(np.float32).sum(axis=0)
    return table, (1.0 / counts)[None, :].astype(np.float32)


def inverse_tables():
    freqs = K0 + ORDER.astype(np.int64)
    delays = (np.arange(2 * LAGQ, dtype=np.int64) - NLAG // 2) * DEC
    phase = np.mod(freqs[:, None] * delays[None, :], NT)
    angle = phase.astype(np.float64) * (2.0 * math.pi / NT)
    scale = 1.0 / math.sqrt(NB)
    real = (np.cos(angle) * scale).reshape(SLICES, 1, LANES, 2 * LAGQ)
    imag = (-np.sin(angle) * scale).reshape(SLICES, 1, LANES, 2 * LAGQ)
    rows = np.concatenate([real, imag], axis=1).reshape(FOLD, 2 * CLASS, 2 * LAGQ)
    zero = rows[0][:, :LAGQ]
    two = rows[2][:, :LAGQ]
    odd = np.concatenate([rows[1], rows[3]], axis=0)
    return [table.astype(np.float32).astype(ml_dtypes.bfloat16) for table in (zero, two, odd)]


def two_terms(values):
    high = values.astype(jnp.bfloat16)
    low = (values - high.astype(jnp.float32)).astype(jnp.bfloat16)
    return high, low


def two_term_dot(values_ref, table):
    rows = values_ref.shape[0] // 2
    both = jnp.dot(values_ref[...], table, preferred_element_type=jnp.float32)
    return both[:rows] + both[rows:]


def spectra_kernel(relative, with_meta, *refs):
    f32, bf16 = jnp.float32, jnp.bfloat16
    refs = list(refs)
    order_ref = refs.pop(0) if relative else None
    x_ref, mask_ref, owner_ref, bins_ref, table_ref, inverse_ref = refs[:6]
    out_refs = refs[6:-7]
    u, v, a, b, early, others, hold = refs[-7:]
    part = pl.program_id(1)
    rows = x_ref.shape[0]

    @pl.when(part == 0)
    def fold():
        x = [x_ref[:, m * QUARTER:(m + 1) * QUARTER].astype(f32) for m in range(FOLD)]
        even, odd = x[0] + x[2], x[1] + x[3]
        u[:rows], u[rows:] = two_terms(even + odd)
        v[:rows], v[rows:] = two_terms(even - odd)
        a[:rows], a[rows:] = two_terms(x[0] - x[2])
        b[:rows], b[rows:] = two_terms(x[1] - x[3])
        early[:, :2 * CLASS] = two_term_dot(u, table_ref[:, :2 * CLASS])
        early[:, 2 * CLASS:] = two_term_dot(v, table_ref[:, 2 * CLASS:])

    @pl.when(part == 1)
    def first_half():
        others[...] = two_term_dot(a, table_ref[...])

    @pl.when(part == 2)
    def second_half():
        others[...] += two_term_dot(b, table_ref[...])

    @pl.when(part == 3)
    def whiten():
        holders = [(early, 0), (others, 0), (early, 2 * CLASS), (others, 2 * CLASS)]
        power = []
        for ref, start in holders:
            real, imag = ref[:, start:start + CLASS], ref[:, start + CLASS:start + 2 * CLASS]
            power.append((real * real + imag * imag).astype(bf16))
        power = jnp.concatenate(power, axis=1)
        mean = jnp.dot(power, table_ref[...], preferred_element_type=f32) * inverse_ref[...]
        shape = (LANES, LANES)
        diagonal = lax.broadcasted_iota(jnp.int32, shape, 0) == lax.broadcasted_iota(jnp.int32, shape, 1)
        mask = jnp.where(diagonal, jnp.broadcast_to(mask_ref[...], shape), 0).astype(f32)
        mask = jnp.sum(mask, axis=1, keepdims=True)
        weight = jnp.concatenate([mask] * (rows // LANES), axis=0) * lax.rsqrt(mean + EPSILON)
        per_group = LANES // G
        target = refs[-8] if relative else out_refs[0]
        for piece in range(SLICES):
            ref, start = holders[piece // 2]
            start += (piece % 2) * LANES
            scale = weight[:, piece * LANES:(piece + 1) * LANES]
            hold[0] = ref[:, start:start + LANES] * scale
            hold[1] = ref[:, CLASS + start:CLASS + start + LANES] * scale
            for seg in range(rows // LANES):
                for j in range(per_group):
                    at = seg * LANES + j * G
                    for half in range(2):
                        taken = hold[half, pl.ds(seg * LANES + j, G, stride=per_group), :]
                        target[piece, at:at + G, half * LANES:(half + 1) * LANES] = taken.astype(bf16)
        if with_meta:
            tiles = owner_ref.shape[1]
            labels = (owner_ref[...] * BIN_DEV + bins_ref[...]).astype(f32)
            for piece in range(SLICES):
                at = pl.ds(rows, META)
                target[piece, at, :] = jnp.zeros((META, 2 * LANES), bf16)
                target[piece, at, :LANES] = jnp.broadcast_to(mask_ref[...].astype(f32), (META, LANES)).astype(bf16)
                target[piece, at, LANES:LANES + tiles] = jnp.broadcast_to(labels, (META, tiles)).astype(bf16)
        if relative:
            for slot in range(SLICES):
                out_refs[slot][...] = target[order_ref[slot]]


def spectra(traces, mask, owners, bins, first_row, rows, order=None, with_meta=False):
    table, inverse = forward_tables()
    block, relative = BLOCK, order is not None
    skip = first_row // block
    whole = lambda shape: pl.BlockSpec(shape, lambda i, p, *_: (0, 0))
    in_specs = [
        pl.BlockSpec((block, NT), lambda i, p, *_: (i + skip, 0)),
        whole(mask.shape),
        whole(owners.shape),
        whole(bins.shape),
        pl.BlockSpec((QUARTER, NB), lambda i, p, *_: (p, 0)),
        whole(inverse.shape),
    ]
    f32, bf16 = jnp.float32, jnp.bfloat16
    scratch = [pltpu.VMEM((2 * block, QUARTER), bf16)] * 4
    scratch += [pltpu.VMEM((block, 4 * CLASS), f32)] * 2 + [pltpu.VMEM((2, block, LANES), f32)]
    if relative:
        scratch = [pltpu.VMEM((SLICES, block, 2 * LANES), bf16)] + scratch
        out_specs = [pl.BlockSpec((block, 2 * LANES), lambda i, p, *_: (i, 0))] * SLICES
        out_shape = [jax.ShapeDtypeStruct((rows, 2 * LANES), bf16)] * SLICES
    else:
        extra = META if with_meta else 0
        out_specs = [pl.BlockSpec((SLICES, block + extra, 2 * LANES), lambda i, p, *_: (0, i, 0))]
        out_shape = [jax.ShapeDtypeStruct((SLICES, rows + extra, 2 * LANES), bf16)]
    result = pl.pallas_call(
        functools.partial(spectra_kernel, relative, with_meta),
        grid_spec=pltpu.PrefetchScalarGridSpec(
            num_scalar_prefetch=1 if relative else 0,
            grid=(rows // block, 4),
            in_specs=in_specs,
            out_specs=out_specs,
            scratch_shapes=scratch,
        ),
        out_shape=out_shape,
        compiler_params=pltpu.CompilerParams(vmem_limit_bytes=VMEM),
        cost_estimate=pl.CostEstimate(
            flops=14 * rows * NB * NB, bytes_accessed=rows * NT * 3 + 8 * NB * NB, transcendentals=rows * NB
        ),
        name="spectra",
    )(*([order] if relative else []), traces, mask, owners, bins, jnp.asarray(table), inverse)
    return result if relative else result[0]


def pair_sums(block_refs, pairs, steps, tiles):
    f32 = jnp.float32
    done = 0
    groups, current = [], []
    for pair in pairs:
        members = {m for p in current + [pair] for m in p}
        if current and 4 * (len(current) + 1) + 4 * len(members) > 60:
            groups.append(current)
            current = []
        current = current + [pair]
    groups.append(current)
    for group in groups:
        needed = sorted({m for pair in group for m in pair})

        def body(step, sums):
            at = pl.ds(pl.multiple_of(step * G, G), G)
            real = {m: block_refs[m][at, :LANES].astype(f32) for m in needed}
            imag = {m: block_refs[m][at, LANES:].astype(f32) for m in needed}
            new = []
            for (p, q), (re, im) in zip(group, sums):
                re = re + (real[p] * real[q] + imag[p] * imag[q])
                im = im + (imag[p] * real[q] - real[p] * imag[q])
                new.append((re, im))
            return tuple(new)

        zero = jnp.zeros((G, LANES), f32)
        sums = lax.fori_loop(0, steps, body, tuple((zero, zero) for _ in group), unroll=2)
        for re, im in sums:
            tiles[done:done + G, :LANES] = re
            tiles[done:done + G, LANES:] = im
            done += G


def cross_kernel(split, pairs, steps, has_before, *refs):
    f32 = jnp.float32
    refs = list(refs)
    before_ref = refs.pop(-3) if has_before else None
    *block_refs, scale_ref, onehot_ref, out_ref, tiles = refs
    if split:
        block_refs = [block_refs[0].at[m] for m in range(block_refs[0].shape[0])]
    pair_sums(block_refs, pairs, steps, tiles)
    high, low = two_terms(tiles[...] * scale_ref[...])
    stacked = jnp.dot(onehot_ref[...], high, preferred_element_type=f32)
    stacked += jnp.dot(onehot_ref[...], low, preferred_element_type=f32)
    if has_before:
        stacked += before_ref[...]
    if len(out_ref.shape) == 2:
        out_ref[...] = stacked
    else:
        for copy in range(out_ref.shape[0]):
            out_ref[copy] = stacked.astype(out_ref.dtype)


def cross(blocks, pairs, rows, scale, onehot, before=None, copies=None):
    bins = onehot.shape[0]
    shape = (bins, 2 * LANES)
    split = not isinstance(blocks, (list, tuple))
    inputs = ([blocks] if split else list(blocks)) + [scale, onehot]
    if before is not None:
        inputs.append(before)
    if copies is None:
        out_shape = jax.ShapeDtypeStruct(shape, jnp.float32)
    else:
        out_shape = jax.ShapeDtypeStruct((copies,) + shape, jnp.bfloat16)
    moved = sum(4 * rows * LANES for _ in range(len(pairs)))
    return pl.pallas_call(
        functools.partial(cross_kernel, split, pairs, rows // G, before is not None),
        out_shape=out_shape,
        scratch_shapes=[pltpu.VMEM((len(pairs) * G, 2 * LANES), jnp.float32)],
        compiler_params=pltpu.CompilerParams(vmem_limit_bytes=VMEM),
        cost_estimate=pl.CostEstimate(
            flops=8 * rows * LANES * len(pairs), bytes_accessed=moved, transcendentals=0
        ),
        name="cross",
    )(*inputs)

def lags_kernel(stacks_ref, zero_ref, two_ref, odd_ref, out_ref):
    f32 = jnp.float32
    copies = stacks_ref.shape[0] // SLICES
    pieces = []
    for piece in range(SLICES):
        total = stacks_ref[piece].astype(f32)
        for copy in range(1, copies):
            total += stacks_ref[copy * SLICES + piece].astype(f32)
        pieces.append(total)

    def product(values, table):
        both = jnp.dot(jnp.concatenate(two_terms(values), axis=0), table, preferred_element_type=f32)
        return both[:BIN_DEV] + both[BIN_DEV:]

    zero = product(jnp.concatenate(pieces[0:2], axis=1), zero_ref[...])
    two = product(jnp.concatenate(pieces[4:6], axis=1), two_ref[...])
    odd = product(jnp.concatenate(pieces[2:4] + pieces[6:8], axis=1), odd_ref[...])
    plus, minus = zero + two, zero - two
    out_ref[:, :LAGQ] = plus + odd[:, :LAGQ]
    out_ref[:, LAGQ:2 * LAGQ] = minus + odd[:, LAGQ:]
    out_ref[:, 2 * LAGQ:3 * LAGQ] = plus - odd[:, :LAGQ]
    out_ref[:, 3 * LAGQ:] = minus - odd[:, LAGQ:]


def lags(stacks):
    tables = [jnp.asarray(table) for table in inverse_tables()]
    return pl.pallas_call(
        lags_kernel,
        out_shape=jax.ShapeDtypeStruct((BIN_DEV, NLAG), jnp.float32),
        compiler_params=pltpu.CompilerParams(vmem_limit_bytes=VMEM // 2),
        name="lags",
    )(stacks, *tables)


def weights_of(masks, labels, low, far, sign, total_segs):
    blocks = masks.shape[0]
    valid = (far >= 1) & (far <= R) & (low + far < blocks)
    far = jnp.where(valid, far, 1)
    other = jnp.minimum(low + far, blocks - 1)
    groups = masks.reshape(blocks, G, -1)
    counts = jnp.sum(groups[low] * groups[other], axis=2)
    scale = jnp.where(valid[:, None], 1.0 / (total_segs * jnp.maximum(counts, 1.0)), 0.0)
    chosen = labels.reshape(blocks, R, G)[low, far - 1].reshape(-1)
    half = jnp.repeat(jnp.stack([jnp.ones_like(sign), sign], axis=1), LANES, axis=1)
    wide = (scale[:, :, None] * half[:, None, :]).reshape(-1, 2 * LANES)
    bins = jnp.arange(blocks * BIN_DEV, dtype=jnp.float32)
    return wide, (chosen[None, :] == bins[:, None]).astype(jnp.bfloat16)


def fixed_pairs(blocks):
    return [(b, b + d) for b in range(blocks) for d in range(1, R + 1) if b + d < blocks]


def fixed_weights(masks, labels, total_segs):
    pairs = np.array(fixed_pairs(masks.shape[0]))
    low, far = jnp.asarray(pairs[:, 0]), jnp.asarray(pairs[:, 1] - pairs[:, 0])
    return weights_of(masks, labels, low, far, jnp.ones((len(pairs),), jnp.float32), total_segs)


def slot_weights(masks, labels, pairs, total_segs):
    blocks = masks.shape[0]
    here = lax.axis_index("chan")
    slots = jnp.asarray(np.array(pairs))
    held = (here - slots) % blocks
    low, high = jnp.min(held, axis=1), jnp.max(held, axis=1)
    sign = jnp.where(held[:, 0] < held[:, 1], 1.0, -1.0)
    return weights_of(masks, labels, low, high - low, sign, total_segs)


def sent_along(x, mask, owners, bins, total_segs):
    seg_count = lax.axis_size("seg")
    count = lax.axis_size("chan")
    rows, chans = x.shape[0], mask.shape[1]
    early = BLOCK
    late = rows - early
    first = spectra(x, mask, owners, bins, 0, early, with_meta=True)
    first = lax.all_to_all(first, "chan", split_axis=0, concat_axis=0, tiled=True)
    order = (lax.axis_index("chan") + jnp.arange(count, dtype=jnp.int32)) % count
    second = spectra(x, mask, owners, bins, early, late, order=order)
    slots = {0: second[0]}
    for shift in SENT:
        slots[shift] = lax.ppermute(second[shift], "chan", [(i, (i + shift) % count) for i in range(count)])

    meta = first[:, early, :].astype(jnp.float32)
    masks, labels = meta[:, :chans], meta[:, LANES:LANES + owners.shape[1]]
    stacks = cross(first, fixed_pairs(count), early, *fixed_weights(masks, labels, total_segs))
    known = (0,) + SENT[:-1]
    pairs = [(known[i], known[j]) for i in range(len(known)) for j in range(i + 1, len(known))]
    at = {slot: i for i, slot in enumerate(known)}
    stacks = cross(
        [slots[slot] for slot in known],
        [(at[p], at[q]) for p, q in pairs],
        late,
        *slot_weights(masks, labels, pairs, total_segs),
        before=stacks,
    )
    known = (0,) + SENT
    pairs = [(slot, SENT[-1]) for slot in known[:-1]]
    return cross(
        [slots[slot] for slot in known],
        [(i, len(known) - 1) for i in range(len(known) - 1)],
        late,
        *slot_weights(masks, labels, pairs, total_segs),
        before=stacks,
        copies=seg_count,
    )


def sent_at_once(x, mask, owners, bins, total_segs):
    seg_count = lax.axis_size("seg")
    count = lax.axis_size("chan")
    rows, chans = x.shape[0], mask.shape[1]
    narrow = NB // count
    splits = LANES // narrow
    own = jnp.concatenate([mask, owners * BIN_DEV + bins], axis=1)
    every = lax.all_gather(own, "chan", axis=0, tiled=True).astype(jnp.float32)
    masks, labels = every[:, :chans], every[:, chans:]
    outgoing = spectra(x, mask, owners, bins, 0, rows)
    outgoing = outgoing.reshape(SLICES, rows, 2, splits, narrow).transpose(0, 3, 1, 2, 4)
    outgoing = outgoing.reshape(count, rows, 2 * narrow)
    wide = lax.all_to_all(outgoing, "chan", split_axis=0, concat_axis=0, tiled=True)
    wide = jnp.pad(wide.reshape(count, rows, 2, narrow), ((0, 0), (0, 0), (0, 0), (0, LANES - narrow)))
    wide = wide.reshape(count, rows, 2 * LANES)
    stacks = cross(wide, fixed_pairs(count), rows, *fixed_weights(masks, labels, total_segs), copies=seg_count)
    return stacks.reshape(-1, 2, LANES)[..., :narrow]


def per_device(traces, channel_mask, owner_ids, local_bins):
    seg_count = lax.axis_size("seg")
    count = lax.axis_size("chan")
    segs, chans, length = traces.shape
    x = traces.reshape(segs * chans, length)
    mask = channel_mask.reshape(1, chans)
    owners = owner_ids.reshape(1, -1)
    if count == SLICES:
        stacks = sent_along(x, mask, owners, local_bins, segs * seg_count)
        stacks = stacks.reshape(seg_count * count, BIN_DEV, 2 * LANES)
        stacks = lax.all_to_all(stacks, ("seg", "chan"), split_axis=0, concat_axis=0, tiled=True)
    else:
        narrow = NB // count
        stacks = sent_at_once(x, mask, owners, local_bins, segs * seg_count)
        stacks = stacks.reshape(seg_count * count, BIN_DEV, 2 * narrow)
        stacks = lax.all_to_all(stacks, ("seg", "chan"), split_axis=0, concat_axis=0, tiled=True)
        stacks = stacks.reshape(seg_count, SLICES, count // SLICES, BIN_DEV, 2, narrow)
        stacks = stacks.transpose(0, 1, 3, 4, 2, 5).reshape(seg_count * SLICES, BIN_DEV, 2 * LANES)
    return lags(stacks)


def solution(mesh):
    in_specs = (P("seg", "chan", None), P("chan"), P("chan", None, None), P("chan", None))
    out_specs = P("chan", None)
    return jax.shard_map(
        per_device, mesh=mesh, in_specs=in_specs, out_specs=out_specs, check_vma=False
    )
```

```python
import functools
import math

import jax
import jax.numpy as jnp
import ml_dtypes
import numpy as np
from jax import lax
from jax.experimental import pallas as pl
from jax.experimental.pallas import tpu as pltpu
from jax.sharding import PartitionSpec as P

NT = 4096
DEC = 2
K0 = 8
HW = 64
R = 4
G = 16
BIN_DEV = 8
NB = 1024
NLAG = 2048
EPSILON = 1e-06

LANES = 128
SLICES = NB // LANES
FOLD = 4
CLASS = NB // FOLD
QUARTER = NT // FOLD
LAGQ = NLAG // FOLD
VMEM = 58 * 1024 * 1024
VMEM_SMALL = 20 * 1024 * 1024
BLOCK = 256
META = 16

SENT = (1, 7, 4, 3, 5, 2, 6)
LATEST = 2


ORDER = np.arange(NB).reshape(CLASS, FOLD).T.reshape(-1)


def forward_tables():
    samples = np.arange(NT // 2, dtype=np.int64)
    freqs = K0 + ORDER.astype(np.int64)
    phase = samples[:, None] * freqs[None, :] % NT
    angle = (phase.astype(np.float32) * np.float32(2.0 * math.pi / NT)).astype(np.float64)
    cos = np.cos(angle).astype(np.float32).astype(ml_dtypes.bfloat16)
    sin = (-np.sin(angle)).astype(np.float32).astype(ml_dtypes.bfloat16)

    def part(which, rows):
        columns = slice(which * CLASS, (which + 1) * CLASS)
        return [cos[rows, columns], sin[rows, columns]]

    low, high = slice(0, QUARTER), slice(QUARTER, 2 * QUARTER)
    band = (np.abs(ORDER[:, None] - ORDER[None, :]) <= HW).astype(ml_dtypes.bfloat16)
    table = np.concatenate(
        [
            np.concatenate(part(0, low) + part(2, low), axis=1),
            np.concatenate(part(1, low) + part(3, low), axis=1),
            np.concatenate(part(1, high) + part(3, high), axis=1),
            band,
        ],
        axis=0,
    )
    return table


def inverse_tables():
    freqs = K0 + ORDER.astype(np.int64)
    delays = (np.arange(2 * LAGQ, dtype=np.int64) - NLAG // 2) * DEC
    phase = np.mod(freqs[:, None] * delays[None, :], NT)
    angle = phase.astype(np.float64) * (2.0 * math.pi / NT)
    scale = 1.0 / math.sqrt(NB)
    real = (np.cos(angle) * scale).reshape(SLICES, 1, LANES, 2 * LAGQ)
    imag = (-np.sin(angle) * scale).reshape(SLICES, 1, LANES, 2 * LAGQ)
    rows = np.concatenate([real, imag], axis=1).reshape(FOLD, 2 * CLASS, 2 * LAGQ)
    zero = rows[0][:, :LAGQ]
    two = rows[2][:, :LAGQ]
    odd = np.concatenate([rows[1], rows[3]], axis=0)
    return [table.astype(np.float32).astype(ml_dtypes.bfloat16) for table in (zero, two, odd)]


def two_terms(values):
    high = values.astype(jnp.bfloat16)
    low = (values - high.astype(jnp.float32)).astype(jnp.bfloat16)
    return high, low


def two_term_dot(values_ref, table):
    rows = values_ref.shape[0] // 2
    both = jnp.dot(values_ref[...], table, preferred_element_type=jnp.float32)
    return both[:rows] + both[rows:]


def spectra_kernel(relative, with_meta, *refs):
    f32, bf16 = jnp.float32, jnp.bfloat16
    refs = list(refs)
    here_ref = refs.pop(0) if relative else None
    x_ref, mask_ref, owner_ref, bins_ref, table_ref = refs[:5]
    out_refs = refs[5:-7]
    u, v, a, b, early, others, hold = refs[-7:]
    part = pl.program_id(1)
    rows = x_ref.shape[0]

    @pl.when(part == 0)
    def fold():
        x = [x_ref[:, m * QUARTER:(m + 1) * QUARTER].astype(f32) for m in range(FOLD)]
        even, odd = x[0] + x[2], x[1] + x[3]
        u[:rows], u[rows:] = two_terms(even + odd)
        v[:rows], v[rows:] = two_terms(even - odd)
        a[:rows], a[rows:] = two_terms(x[0] - x[2])
        b[:rows], b[rows:] = two_terms(x[1] - x[3])
        early[:, :2 * CLASS] = two_term_dot(u, table_ref[:, :2 * CLASS])
        early[:, 2 * CLASS:] = two_term_dot(v, table_ref[:, 2 * CLASS:])

    @pl.when(part == 1)
    def first_half():
        others[...] = two_term_dot(a, table_ref[...])

    @pl.when(part == 2)
    def second_half():
        others[...] += two_term_dot(b, table_ref[...])

    @pl.when(part == 3)
    def whiten():
        holders = [(early, 0), (others, 0), (early, 2 * CLASS), (others, 2 * CLASS)]
        power = []
        for ref, start in holders:
            real, imag = ref[:, start:start + CLASS], ref[:, start + CLASS:start + 2 * CLASS]
            power.append((real * real + imag * imag).astype(bf16))
        power = jnp.concatenate(power, axis=1)
        lane = lax.broadcasted_iota(jnp.int32, (1, NB), 1)
        bin_ = (lane % CLASS) * FOLD + lane // CLASS
        within = jnp.minimum(bin_ + HW, NB - 1) - jnp.maximum(bin_ - HW, 0) + 1
        mean = jnp.dot(power, table_ref[...], preferred_element_type=f32) * (1.0 / within.astype(f32))
        shape = (LANES, LANES)
        diagonal = lax.broadcasted_iota(jnp.int32, shape, 0) == lax.broadcasted_iota(jnp.int32, shape, 1)
        mask = jnp.where(diagonal, jnp.broadcast_to(mask_ref[...], shape), 0).astype(f32)
        mask = jnp.sum(mask, axis=1, keepdims=True)
        weight = jnp.concatenate([mask] * (rows // LANES), axis=0) * lax.rsqrt(mean + EPSILON)
        per_group = LANES // G
        target = refs[-8] if relative else out_refs[0]
        for piece in range(SLICES):
            ref, start = holders[piece // 2]
            start += (piece % 2) * LANES
            scale = weight[:, piece * LANES:(piece + 1) * LANES]
            hold[0] = ref[:, start:start + LANES] * scale
            hold[1] = ref[:, CLASS + start:CLASS + start + LANES] * scale
            for seg in range(rows // LANES):
                for j in range(per_group):
                    at = seg * LANES + j * G
                    for half in range(2):
                        taken = hold[half, pl.ds(seg * LANES + j, G, stride=per_group), :]
                        target[piece, at:at + G, half * LANES:(half + 1) * LANES] = taken.astype(bf16)
        if with_meta:
            tiles = owner_ref.shape[1]
            labels = (owner_ref[...] * BIN_DEV + bins_ref[...]).astype(f32)
            for piece in range(SLICES):
                at = pl.ds(rows, META)
                target[piece, at, :] = jnp.zeros((META, 2 * LANES), bf16)
                target[piece, at, :LANES] = jnp.broadcast_to(mask_ref[...].astype(f32), (META, LANES)).astype(bf16)
                target[piece, at, LANES:LANES + tiles] = jnp.broadcast_to(labels, (META, tiles)).astype(bf16)
        if relative:
            for slot in range(SLICES):
                out_refs[slot][...] = target[lax.rem(here_ref[0] + slot, SLICES)]


def spectra(traces, mask, owners, bins, first_row, rows, here=None, with_meta=False):
    block, relative = BLOCK, here is not None
    skip = first_row // block
    whole = lambda shape: pl.BlockSpec(shape, lambda i, p, *_: (0, 0))
    in_specs = [
        pl.BlockSpec((block, NT), lambda i, p, *_: (i + skip, 0)),
        whole(mask.shape),
        whole(owners.shape),
        whole(bins.shape),
        pl.BlockSpec((QUARTER, NB), lambda i, p, *_: (p, 0)),
    ]
    f32, bf16 = jnp.float32, jnp.bfloat16
    scratch = [pltpu.VMEM((2 * block, QUARTER), bf16)] * 4
    scratch += [pltpu.VMEM((block, 4 * CLASS), f32)] * 2 + [pltpu.VMEM((2, block, LANES), f32)]
    if relative:
        scratch = [pltpu.VMEM((SLICES, block, 2 * LANES), bf16)] + scratch
        out_specs = [pl.BlockSpec((block, 2 * LANES), lambda i, p, *_: (i, 0))] * SLICES
        out_shape = [jax.ShapeDtypeStruct((rows, 2 * LANES), bf16)] * SLICES
    else:
        extra = META if with_meta else 0
        out_specs = [pl.BlockSpec((SLICES, block + extra, 2 * LANES), lambda i, p, *_: (0, i, 0))]
        out_shape = [jax.ShapeDtypeStruct((SLICES, rows + extra, 2 * LANES), bf16)]
    result = pl.pallas_call(
        functools.partial(spectra_kernel, relative, with_meta),
        grid_spec=pltpu.PrefetchScalarGridSpec(
            num_scalar_prefetch=1 if relative else 0,
            grid=(rows // block, 4),
            in_specs=in_specs,
            out_specs=out_specs,
            scratch_shapes=scratch,
        ),
        out_shape=out_shape,
        compiler_params=pltpu.CompilerParams(vmem_limit_bytes=VMEM),
        cost_estimate=pl.CostEstimate(
            flops=14 * rows * NB * NB, bytes_accessed=rows * NT * 3 + 8 * NB * NB, transcendentals=rows * NB
        ),
        name="spectra",
    )(*([here] if relative else []), traces, mask, owners, bins, jnp.asarray(forward_tables()))
    return result if relative else result[0]


def pair_sums(block_refs, pairs, steps, tiles):
    f32 = jnp.float32
    done = 0
    groups, current = [], []
    for pair in pairs:
        members = {m for p in current + [pair] for m in p}
        if current and 4 * (len(current) + 1) + 4 * len(members) > 60:
            groups.append(current)
            current = []
        current = current + [pair]
    groups.append(current)
    for group in groups:
        needed = sorted({m for pair in group for m in pair})

        def body(step, sums):
            at = pl.ds(pl.multiple_of(step * G, G), G)
            real = {m: block_refs[m][at, :LANES].astype(f32) for m in needed}
            imag = {m: block_refs[m][at, LANES:].astype(f32) for m in needed}
            new = []
            for (p, q), (re, im) in zip(group, sums):
                re = re + (real[p] * real[q] + imag[p] * imag[q])
                im = im + (imag[p] * real[q] - real[p] * imag[q])
                new.append((re, im))
            return tuple(new)

        zero = jnp.zeros((G, LANES), f32)
        sums = lax.fori_loop(0, steps, body, tuple((zero, zero) for _ in group), unroll=2)
        for re, im in sums:
            tiles[done:done + G, :LANES] = re
            tiles[done:done + G, LANES:] = im
            done += G


def cross_kernel(split, pairs, steps, has_before, *refs):
    f32 = jnp.float32
    refs = list(refs)
    before_ref = refs.pop(-3) if has_before else None
    *block_refs, rows_ref, out_ref, tiles = refs
    if split:
        block_refs = [block_refs[0].at[m] for m in range(block_refs[0].shape[0])]
    pair_sums(block_refs, pairs, steps, tiles)
    bins, count = out_ref.shape[-2], tiles.shape[0]
    wanted = rows_ref[0:1, :] == lax.broadcasted_iota(jnp.int32, (bins, count), 0).astype(f32)
    high, low = two_terms(tiles[...])
    stacked = []
    for half in range(2):
        weights = jnp.where(wanted, jnp.broadcast_to(rows_ref[half + 1:half + 2, :], (bins, count)), 0.0)
        weights = jnp.concatenate(two_terms(weights), axis=0)
        at = slice(half * LANES, (half + 1) * LANES)
        both = jnp.dot(weights, high[:, at], preferred_element_type=f32)
        both = both[:bins] + both[bins:]
        stacked.append(both + jnp.dot(weights[:bins], low[:, at], preferred_element_type=f32))
    stacked = jnp.concatenate(stacked, axis=1)
    if has_before:
        stacked += before_ref[...]
    if len(out_ref.shape) == 2:
        out_ref[...] = stacked
    else:
        for copy in range(out_ref.shape[0]):
            out_ref[copy] = stacked.astype(out_ref.dtype)


def cross(blocks, pairs, steps, bins, weights, before=None, copies=None):
    shape = (bins, 2 * LANES)
    split = not isinstance(blocks, (list, tuple))
    inputs = ([blocks] if split else list(blocks)) + [weights]
    if before is not None:
        inputs.append(before)
    if copies is None:
        out_shape = jax.ShapeDtypeStruct(shape, jnp.float32)
    else:
        out_shape = jax.ShapeDtypeStruct((copies,) + shape, jnp.bfloat16)
    return pl.pallas_call(
        functools.partial(cross_kernel, split, pairs, steps, before is not None),
        out_shape=out_shape,
        scratch_shapes=[pltpu.VMEM((len(pairs) * G, 2 * LANES), jnp.float32)],
        compiler_params=pltpu.CompilerParams(vmem_limit_bytes=VMEM_SMALL if copies is None or not split else VMEM),
        cost_estimate=pl.CostEstimate(
            flops=8 * G * steps * LANES * len(pairs), bytes_accessed=4 * G * steps * LANES * len(pairs), transcendentals=0
        ),
        name="cross",
    )(*inputs)


def weights_kernel(blocks, total_segs, here_ref, meta_ref, *refs):
    f32, bf16 = jnp.float32, jnp.bfloat16
    meta = jnp.concatenate([meta_ref[b, 0:1, :] for b in range(blocks)], axis=0)
    masks, labels = meta[:, :LANES], meta[:, LANES:]
    empty = jnp.zeros((R, LANES), bf16)
    padded = jnp.concatenate([masks.astype(f32), empty.astype(f32)], axis=0)
    half = len(refs) // 2
    for ends_ref, out_ref in zip(refs[:half], refs[half:]):
        lanes = out_ref.shape[1]
        first, second = ends_ref[0:1, :], ends_ref[1:2, :]
        slots = first < 0
        held = [jnp.where(slots, lax.rem(here_ref[0] + end + 2 * blocks, blocks), end) for end in (first, second)]
        low, far = jnp.minimum(held[0], held[1]), jnp.abs(held[0] - held[1])
        sign = jnp.where(held[0] < held[1], 1.0, -1.0)
        block = lax.broadcasted_iota(jnp.int32, (blocks, lanes), 0)
        group = lax.broadcasted_iota(jnp.int32, (LANES, lanes), 1) % G
        place = lax.broadcasted_iota(jnp.int32, (LANES, lanes), 0)
        chosen = (place == (far - 1) * G + group).astype(f32).astype(bf16)
        label = jnp.dot(labels, chosen, preferred_element_type=f32)
        label = jnp.sum(jnp.where(block == low, label, 0.0), axis=0, keepdims=True)
        member = (place // (LANES // G) == group).astype(f32).astype(bf16)
        count = jnp.zeros((1, lanes), f32)
        for d in range(1, R + 1):
            both = (padded[:blocks] * padded[d:d + blocks]).astype(bf16)
            of_block = jnp.dot(both, member, preferred_element_type=f32)
            count += jnp.sum(jnp.where((block == low) & (far == d), of_block, 0.0), axis=0, keepdims=True)
        scale = jnp.where(far <= R, 1.0 / (total_segs * jnp.maximum(count, 1.0)), 0.0)
        out_ref[...] = jnp.concatenate([label, scale, scale * sign, jnp.zeros((5, lanes), f32)], axis=0)


def pair_weights(here, meta, at, total_segs, pair_lists):
    blocks = meta.shape[0]
    ends = [jnp.asarray(np.repeat(np.array(pairs, np.int32).T, G, axis=1)) for pairs in pair_lists]
    whole = lambda shape: pl.BlockSpec(shape, lambda i, *_: (0, 0))
    shapes = [(8, G * len(pairs)) for pairs in pair_lists]
    return pl.pallas_call(
        functools.partial(weights_kernel, blocks, total_segs),
        grid_spec=pltpu.PrefetchScalarGridSpec(
            num_scalar_prefetch=1,
            grid=(1,),
            in_specs=[pl.BlockSpec((blocks, META, 2 * LANES), lambda i, *_: (0, at // META, 0))]
            + [whole(end.shape) for end in ends],
            out_specs=[whole(shape) for shape in shapes],
        ),
        out_shape=[jax.ShapeDtypeStruct(shape, jnp.float32) for shape in shapes],
        compiler_params=pltpu.CompilerParams(vmem_limit_bytes=VMEM_SMALL),
        name="weights",
    )(here, meta, *ends)


def lags_kernel(stacks_ref, zero_ref, two_ref, odd_ref, out_ref):
    f32 = jnp.float32
    copies = stacks_ref.shape[0] // SLICES
    pieces = []
    for piece in range(SLICES):
        total = stacks_ref[piece].astype(f32)
        for copy in range(1, copies):
            total += stacks_ref[copy * SLICES + piece].astype(f32)
        pieces.append(total)

    def product(values, table):
        both = jnp.dot(jnp.concatenate(two_terms(values), axis=0), table, preferred_element_type=f32)
        return both[:BIN_DEV] + both[BIN_DEV:]

    zero = product(jnp.concatenate(pieces[0:2], axis=1), zero_ref[...])
    two = product(jnp.concatenate(pieces[4:6], axis=1), two_ref[...])
    odd = product(jnp.concatenate(pieces[2:4] + pieces[6:8], axis=1), odd_ref[...])
    plus, minus = zero + two, zero - two
    out_ref[:, :LAGQ] = plus + odd[:, :LAGQ]
    out_ref[:, LAGQ:2 * LAGQ] = minus + odd[:, LAGQ:]
    out_ref[:, 2 * LAGQ:3 * LAGQ] = plus - odd[:, :LAGQ]
    out_ref[:, 3 * LAGQ:] = minus - odd[:, LAGQ:]


def lags(stacks):
    tables = [jnp.asarray(table) for table in inverse_tables()]
    return pl.pallas_call(
        lags_kernel,
        out_shape=jax.ShapeDtypeStruct((BIN_DEV, NLAG), jnp.float32),
        compiler_params=pltpu.CompilerParams(vmem_limit_bytes=VMEM_SMALL),
        name="lags",
    )(stacks, *tables)


def fixed_pairs(blocks):
    return [(b, b + d) for b in range(blocks) for d in range(1, R + 1) if b + d < blocks]


def sent_along(x, mask, owners, bins, total_segs):
    seg_count = lax.axis_size("seg")
    count = lax.axis_size("chan")
    early = BLOCK
    late = x.shape[0] - early
    here = lax.axis_index("chan").astype(jnp.int32).reshape(1)
    first = spectra(x, mask, owners, bins, 0, early, with_meta=True)
    first = lax.all_to_all(first, "chan", split_axis=0, concat_axis=0, tiled=True)
    second = spectra(x, mask, owners, bins, early, late, here=here)
    slots = {0: second[0]}
    for shift in SENT:
        slots[shift] = lax.ppermute(second[shift], "chan", [(i, (i + shift) % count) for i in range(count)])

    fixed = fixed_pairs(count)
    known = (0,) + SENT
    before = len(known) - LATEST
    soon = [(i, j) for j in range(1, before) for i in range(j)]
    last = [(i, j) for j in range(before, len(known)) for i in range(j)]
    as_slots = lambda pairs: [(-known[i] - count, -known[j] - count) for i, j in pairs]
    weights = pair_weights(here, first, early, total_segs, [fixed, as_slots(soon), as_slots(last)])
    rows = count * BIN_DEV
    stacks = cross(first, fixed, early // G, rows, weights[0])
    held = [slots[slot] for slot in known]
    stacks = cross(held[:before], soon, late // G, rows, weights[1], before=stacks)
    return cross(held, last, late // G, rows, weights[2], before=stacks, copies=seg_count)


def sent_at_once(x, mask, owners, bins, total_segs):
    seg_count = lax.axis_size("seg")
    count = lax.axis_size("chan")
    rows, chans = x.shape[0], mask.shape[1]
    narrow = NB // count
    splits = LANES // narrow
    here = lax.axis_index("chan").astype(jnp.int32).reshape(1)
    own = jnp.concatenate([mask, owners * BIN_DEV + bins], axis=1)
    every = lax.all_gather(own, "chan", axis=0, tiled=True).astype(jnp.bfloat16)
    every = jnp.pad(every, ((0, 0), (0, 2 * LANES - every.shape[1])))
    every = jnp.broadcast_to(every[:, None, :], (count, META, 2 * LANES))
    fixed = fixed_pairs(count)
    weights = pair_weights(here, every, 0, total_segs, [fixed])
    outgoing = spectra(x, mask, owners, bins, 0, rows)
    outgoing = outgoing.reshape(SLICES, rows, 2, splits, narrow).transpose(0, 3, 1, 2, 4)
    outgoing = outgoing.reshape(count, rows, 2 * narrow)
    wide = lax.all_to_all(outgoing, "chan", split_axis=0, concat_axis=0, tiled=True)
    wide = jnp.pad(wide.reshape(count, rows, 2, narrow), ((0, 0), (0, 0), (0, 0), (0, LANES - narrow)))
    wide = wide.reshape(count, rows, 2 * LANES)
    stacks = cross(wide, fixed, rows // G, count * BIN_DEV, weights[0], copies=seg_count)
    return stacks.reshape(-1, 2, LANES)[..., :narrow]


def per_device(traces, channel_mask, owner_ids, local_bins):
    seg_count = lax.axis_size("seg")
    count = lax.axis_size("chan")
    segs, chans, length = traces.shape
    x = traces.reshape(segs * chans, length)
    mask = channel_mask.reshape(1, chans)
    owners = owner_ids.reshape(1, -1)
    if count == SLICES:
        stacks = sent_along(x, mask, owners, local_bins, segs * seg_count)
        stacks = stacks.reshape(seg_count * count, BIN_DEV, 2 * LANES)
        stacks = lax.all_to_all(stacks, ("seg", "chan"), split_axis=0, concat_axis=0, tiled=True)
    else:
        narrow = NB // count
        stacks = sent_at_once(x, mask, owners, local_bins, segs * seg_count)
        stacks = stacks.reshape(seg_count * count, BIN_DEV, 2 * narrow)
        stacks = lax.all_to_all(stacks, ("seg", "chan"), split_axis=0, concat_axis=0, tiled=True)
        stacks = stacks.reshape(seg_count, SLICES, count // SLICES, BIN_DEV, 2, narrow)
        stacks = stacks.transpose(0, 1, 3, 4, 2, 5).reshape(seg_count * SLICES, BIN_DEV, 2 * LANES)
    return lags(stacks)


def solution(mesh):
    in_specs = (P("seg", "chan", None), P("chan"), P("chan", None, None), P("chan", None))
    out_specs = P("chan", None)
    return jax.shard_map(
        per_device, mesh=mesh, in_specs=in_specs, out_specs=out_specs, check_vma=False
    )
```

```python
import functools
import math

import jax
import jax.numpy as jnp
import ml_dtypes
import numpy as np
from jax import lax
from jax.experimental import pallas as pl
from jax.experimental.pallas import tpu as pltpu
from jax.sharding import PartitionSpec as P

NT = 4096
DEC = 2
K0 = 8
HW = 64
R = 4
G = 16
BIN_DEV = 8
NB = 1024
NLAG = 2048
EPSILON = 1e-06

LANES = 128
SLICES = NB // LANES
FOLD = 4
CLASS = NB // FOLD
QUARTER = NT // FOLD
LAGQ = NLAG // FOLD
VMEM = 58 * 1024 * 1024
VMEM_SMALL = 20 * 1024 * 1024
BLOCK = 256
META = 16

SENT = (1, 7, 4, 3, 5, 2, 6)
STAGES = (6, 7, 8)


ORDER = np.arange(NB).reshape(CLASS, FOLD).T.reshape(-1)


def forward_tables():
    samples = np.arange(NT // 2, dtype=np.int64)
    freqs = K0 + ORDER.astype(np.int64)
    phase = samples[:, None] * freqs[None, :] % NT
    angle = (phase.astype(np.float32) * np.float32(2.0 * math.pi / NT)).astype(np.float64)
    cos = np.cos(angle).astype(np.float32).astype(ml_dtypes.bfloat16)
    sin = (-np.sin(angle)).astype(np.float32).astype(ml_dtypes.bfloat16)

    def part(which, rows):
        columns = slice(which * CLASS, (which + 1) * CLASS)
        return [cos[rows, columns], sin[rows, columns]]

    low, high = slice(0, QUARTER), slice(QUARTER, 2 * QUARTER)
    band = (np.abs(ORDER[:, None] - ORDER[None, :]) <= HW).astype(ml_dtypes.bfloat16)
    table = np.concatenate(
        [
            np.concatenate(part(0, low) + part(2, low), axis=1),
            np.concatenate(part(1, low) + part(3, low), axis=1),
            np.concatenate(part(1, high) + part(3, high), axis=1),
            band,
        ],
        axis=0,
    )
    return table


def inverse_tables():
    freqs = K0 + ORDER.astype(np.int64)
    delays = (np.arange(2 * LAGQ, dtype=np.int64) - NLAG // 2) * DEC
    phase = np.mod(freqs[:, None] * delays[None, :], NT)
    angle = phase.astype(np.float64) * (2.0 * math.pi / NT)
    scale = 1.0 / math.sqrt(NB)
    real = (np.cos(angle) * scale).reshape(SLICES, 1, LANES, 2 * LAGQ)
    imag = (-np.sin(angle) * scale).reshape(SLICES, 1, LANES, 2 * LAGQ)
    rows = np.concatenate([real, imag], axis=1).reshape(FOLD, 2 * CLASS, 2 * LAGQ)
    zero = rows[0][:, :LAGQ]
    two = rows[2][:, :LAGQ]
    odd = np.concatenate([rows[1], rows[3]], axis=0)
    return [table.astype(np.float32).astype(ml_dtypes.bfloat16) for table in (zero, two, odd)]


def two_terms(values):
    high = values.astype(jnp.bfloat16)
    low = (values - high.astype(jnp.float32)).astype(jnp.bfloat16)
    return high, low


def two_term_dot(values_ref, table):
    rows = values_ref.shape[0] // 2
    both = jnp.dot(values_ref[...], table, preferred_element_type=jnp.float32)
    return both[:rows] + both[rows:]


def spectra_kernel(relative, with_meta, *refs):
    f32, bf16 = jnp.float32, jnp.bfloat16
    refs = list(refs)
    here_ref = refs.pop(0) if relative else None
    x_ref, mask_ref, owner_ref, bins_ref, source_ref = refs[:5]
    out_refs = refs[5:-9]
    table_ref, arrived, u, v, a, b, early, others, hold = refs[-9:]
    target = refs[-10] if relative else out_refs[0]
    first = pl.program_id(0) == 0
    rows = x_ref.shape[0]
    copies = [
        pltpu.make_async_copy(source_ref.at[part], table_ref.at[part], arrived.at[part]) for part in range(FOLD)
    ]

    @pl.when(first)
    def start():
        for copy in copies:
            copy.start()

    x = [x_ref[:, m * QUARTER:(m + 1) * QUARTER].astype(f32) for m in range(FOLD)]
    even, odd = x[0] + x[2], x[1] + x[3]
    u[:rows], u[rows:] = two_terms(even + odd)
    v[:rows], v[rows:] = two_terms(even - odd)
    a[:rows], a[rows:] = two_terms(x[0] - x[2])
    b[:rows], b[rows:] = two_terms(x[1] - x[3])

    pl.when(first)(copies[0].wait)
    early[:, :2 * CLASS] = two_term_dot(u, table_ref[0, :, :2 * CLASS])
    early[:, 2 * CLASS:] = two_term_dot(v, table_ref[0, :, 2 * CLASS:])
    pl.when(first)(copies[1].wait)
    others[...] = two_term_dot(a, table_ref[1])
    pl.when(first)(copies[2].wait)
    others[...] += two_term_dot(b, table_ref[2])
    pl.when(first)(copies[3].wait)

    holders = [(early, 0), (others, 0), (early, 2 * CLASS), (others, 2 * CLASS)]
    power = []
    for ref, start in holders:
        real, imag = ref[:, start:start + CLASS], ref[:, start + CLASS:start + 2 * CLASS]
        power.append((real * real + imag * imag).astype(bf16))
    power = jnp.concatenate(power, axis=1)
    lane = lax.broadcasted_iota(jnp.int32, (1, NB), 1)
    bin_ = (lane % CLASS) * FOLD + lane // CLASS
    within = jnp.minimum(bin_ + HW, NB - 1) - jnp.maximum(bin_ - HW, 0) + 1
    mean = jnp.dot(power, table_ref[3], preferred_element_type=f32) * (1.0 / within.astype(f32))
    shape = (LANES, LANES)
    diagonal = lax.broadcasted_iota(jnp.int32, shape, 0) == lax.broadcasted_iota(jnp.int32, shape, 1)
    mask = jnp.where(diagonal, jnp.broadcast_to(mask_ref[...], shape), 0).astype(f32)
    mask = jnp.sum(mask, axis=1, keepdims=True)
    weight = jnp.concatenate([mask] * (rows // LANES), axis=0) * lax.rsqrt(mean + EPSILON)
    per_group = LANES // G
    for piece in range(SLICES):
        ref, start = holders[piece // 2]
        start += (piece % 2) * LANES
        scale = weight[:, piece * LANES:(piece + 1) * LANES]
        hold[0] = ref[:, start:start + LANES] * scale
        hold[1] = ref[:, CLASS + start:CLASS + start + LANES] * scale
        for seg in range(rows // LANES):
            for j in range(per_group):
                at = seg * LANES + j * G
                for half in range(2):
                    taken = hold[half, pl.ds(seg * LANES + j, G, stride=per_group), :]
                    target[piece, at:at + G, half * LANES:(half + 1) * LANES] = taken.astype(bf16)
    if with_meta:
        tiles = owner_ref.shape[1]
        labels = (owner_ref[...] * BIN_DEV + bins_ref[...]).astype(f32)
        for piece in range(SLICES):
            at = pl.ds(rows, META)
            target[piece, at, :] = jnp.zeros((META, 2 * LANES), bf16)
            target[piece, at, :LANES] = jnp.broadcast_to(mask_ref[...].astype(f32), (META, LANES)).astype(bf16)
            target[piece, at, LANES:LANES + tiles] = jnp.broadcast_to(labels, (META, tiles)).astype(bf16)
    if relative:
        for slot in range(SLICES):
            out_refs[slot][...] = target[lax.rem(here_ref[0] + slot, SLICES)]


def spectra(traces, mask, owners, bins, first_row, rows, here=None, with_meta=False):
    block, relative = BLOCK, here is not None
    skip = first_row // block
    whole = lambda shape: pl.BlockSpec(shape, lambda i, *_: (0, 0))
    in_specs = [
        pl.BlockSpec((block, NT), lambda i, *_: (i + skip, 0)),
        whole(mask.shape),
        whole(owners.shape),
        whole(bins.shape),
        pl.BlockSpec(memory_space=pl.ANY),
    ]
    f32, bf16 = jnp.float32, jnp.bfloat16
    scratch = [pltpu.VMEM((FOLD, QUARTER, NB), bf16), pltpu.SemaphoreType.DMA((FOLD,))]
    scratch += [pltpu.VMEM((2 * block, QUARTER), bf16)] * 4
    scratch += [pltpu.VMEM((block, 4 * CLASS), f32)] * 2 + [pltpu.VMEM((2, block, LANES), f32)]
    if relative:
        scratch = [pltpu.VMEM((SLICES, block, 2 * LANES), bf16)] + scratch
        out_specs = [pl.BlockSpec((block, 2 * LANES), lambda i, *_: (i, 0))] * SLICES
        out_shape = [jax.ShapeDtypeStruct((rows, 2 * LANES), bf16)] * SLICES
    else:
        extra = META if with_meta else 0
        out_specs = [pl.BlockSpec((SLICES, block + extra, 2 * LANES), lambda i, *_: (0, i, 0))]
        out_shape = [jax.ShapeDtypeStruct((SLICES, rows + extra, 2 * LANES), bf16)]
    result = pl.pallas_call(
        functools.partial(spectra_kernel, relative, with_meta),
        grid_spec=pltpu.PrefetchScalarGridSpec(
            num_scalar_prefetch=1 if relative else 0,
            grid=(rows // block,),
            in_specs=in_specs,
            out_specs=out_specs,
            scratch_shapes=scratch,
        ),
        out_shape=out_shape,
        compiler_params=pltpu.CompilerParams(vmem_limit_bytes=VMEM),
        cost_estimate=pl.CostEstimate(
            flops=14 * rows * NB * NB, bytes_accessed=rows * NT * 3 + 8 * NB * NB, transcendentals=rows * NB
        ),
        name="spectra",
    )(*([here] if relative else []), traces, mask, owners, bins, jnp.asarray(forward_tables()).reshape(FOLD, QUARTER, NB))
    return result if relative else result[0]


def pair_sums(block_refs, pairs, steps, tiles):
    f32 = jnp.float32
    done = 0
    groups, current = [], []
    for pair in pairs:
        members = {m for p in current + [pair] for m in p}
        if current and 4 * (len(current) + 1) + 4 * len(members) > 60:
            groups.append(current)
            current = []
        current = current + [pair]
    groups.append(current)
    for group in groups:
        needed = sorted({m for pair in group for m in pair})

        def body(step, sums):
            at = pl.ds(pl.multiple_of(step * G, G), G)
            real = {m: block_refs[m][at, :LANES].astype(f32) for m in needed}
            imag = {m: block_refs[m][at, LANES:].astype(f32) for m in needed}
            new = []
            for (p, q), (re, im) in zip(group, sums):
                re = re + (real[p] * real[q] + imag[p] * imag[q])
                im = im + (imag[p] * real[q] - real[p] * imag[q])
                new.append((re, im))
            return tuple(new)

        zero = jnp.zeros((G, LANES), f32)
        sums = lax.fori_loop(0, steps, body, tuple((zero, zero) for _ in group), unroll=2)
        for re, im in sums:
            tiles[done:done + G, :LANES] = re
            tiles[done:done + G, LANES:] = im
            done += G


def cross_kernel(split, pairs, steps, has_before, *refs):
    f32 = jnp.float32
    refs = list(refs)
    before_ref = refs.pop(-3) if has_before else None
    *block_refs, rows_ref, out_ref, tiles = refs
    if split:
        block_refs = [block_refs[0].at[m] for m in range(block_refs[0].shape[0])]
    pair_sums(block_refs, pairs, steps, tiles)
    bins, count = out_ref.shape[-2], tiles.shape[0]
    wanted = rows_ref[0:1, :] == lax.broadcasted_iota(jnp.int32, (bins, count), 0).astype(f32)
    high, low = two_terms(tiles[...])
    stacked = []
    for half in range(2):
        weights = jnp.where(wanted, jnp.broadcast_to(rows_ref[half + 1:half + 2, :], (bins, count)), 0.0)
        weights = jnp.concatenate(two_terms(weights), axis=0)
        at = slice(half * LANES, (half + 1) * LANES)
        both = jnp.dot(weights, high[:, at], preferred_element_type=f32)
        both = both[:bins] + both[bins:]
        stacked.append(both + jnp.dot(weights[:bins], low[:, at], preferred_element_type=f32))
    stacked = jnp.concatenate(stacked, axis=1)
    if has_before:
        stacked += before_ref[...]
    if len(out_ref.shape) == 2:
        out_ref[...] = stacked
    else:
        for copy in range(out_ref.shape[0]):
            out_ref[copy] = stacked.astype(out_ref.dtype)


def cross(blocks, pairs, steps, bins, weights, before=None, copies=None):
    shape = (bins, 2 * LANES)
    split = not isinstance(blocks, (list, tuple))
    inputs = ([blocks] if split else list(blocks)) + [weights]
    if before is not None:
        inputs.append(before)
    if copies is None:
        out_shape = jax.ShapeDtypeStruct(shape, jnp.float32)
    else:
        out_shape = jax.ShapeDtypeStruct((copies,) + shape, jnp.bfloat16)
    return pl.pallas_call(
        functools.partial(cross_kernel, split, pairs, steps, before is not None),
        out_shape=out_shape,
        scratch_shapes=[pltpu.VMEM((len(pairs) * G, 2 * LANES), jnp.float32)],
        compiler_params=pltpu.CompilerParams(vmem_limit_bytes=VMEM_SMALL if copies is None or not split else VMEM),
        cost_estimate=pl.CostEstimate(
            flops=8 * G * steps * LANES * len(pairs), bytes_accessed=4 * G * steps * LANES * len(pairs), transcendentals=0
        ),
        name="cross",
    )(*inputs)


def weights_kernel(blocks, total_segs, here_ref, meta_ref, *refs):
    f32, bf16 = jnp.float32, jnp.bfloat16
    meta = jnp.concatenate([meta_ref[b, 0:1, :] for b in range(blocks)], axis=0)
    masks, labels = meta[:, :LANES], meta[:, LANES:]
    empty = jnp.zeros((R, LANES), bf16)
    padded = jnp.concatenate([masks.astype(f32), empty.astype(f32)], axis=0)
    half = len(refs) // 2
    for ends_ref, out_ref in zip(refs[:half], refs[half:]):
        lanes = out_ref.shape[1]
        first, second = ends_ref[0:1, :], ends_ref[1:2, :]
        slots = first < 0
        held = [jnp.where(slots, lax.rem(here_ref[0] + end + 2 * blocks, blocks), end) for end in (first, second)]
        low, far = jnp.minimum(held[0], held[1]), jnp.abs(held[0] - held[1])
        sign = jnp.where(held[0] < held[1], 1.0, -1.0)
        block = lax.broadcasted_iota(jnp.int32, (blocks, lanes), 0)
        group = lax.broadcasted_iota(jnp.int32, (LANES, lanes), 1) % G
        place = lax.broadcasted_iota(jnp.int32, (LANES, lanes), 0)
        chosen = (place == (far - 1) * G + group).astype(f32).astype(bf16)
        label = jnp.dot(labels, chosen, preferred_element_type=f32)
        label = jnp.sum(jnp.where(block == low, label, 0.0), axis=0, keepdims=True)
        member = (place // (LANES // G) == group).astype(f32).astype(bf16)
        count = jnp.zeros((1, lanes), f32)
        for d in range(1, R + 1):
            both = (padded[:blocks] * padded[d:d + blocks]).astype(bf16)
            of_block = jnp.dot(both, member, preferred_element_type=f32)
            count += jnp.sum(jnp.where((block == low) & (far == d), of_block, 0.0), axis=0, keepdims=True)
        scale = jnp.where(far <= R, 1.0 / (total_segs * jnp.maximum(count, 1.0)), 0.0)
        out_ref[...] = jnp.concatenate([label, scale, scale * sign, jnp.zeros((5, lanes), f32)], axis=0)


def pair_weights(here, meta, at, total_segs, pair_lists):
    blocks = meta.shape[0]
    ends = [jnp.asarray(np.repeat(np.array(pairs, np.int32).T, G, axis=1)) for pairs in pair_lists]
    whole = lambda shape: pl.BlockSpec(shape, lambda i, *_: (0, 0))
    shapes = [(8, G * len(pairs)) for pairs in pair_lists]
    return pl.pallas_call(
        functools.partial(weights_kernel, blocks, total_segs),
        grid_spec=pltpu.PrefetchScalarGridSpec(
            num_scalar_prefetch=1,
            grid=(1,),
            in_specs=[pl.BlockSpec((blocks, META, 2 * LANES), lambda i, *_: (0, at // META, 0))]
            + [whole(end.shape) for end in ends],
            out_specs=[whole(shape) for shape in shapes],
        ),
        out_shape=[jax.ShapeDtypeStruct(shape, jnp.float32) for shape in shapes],
        compiler_params=pltpu.CompilerParams(vmem_limit_bytes=VMEM_SMALL),
        name="weights",
    )(here, meta, *ends)


def lags_kernel(stacks_ref, zero_ref, two_ref, odd_ref, out_ref):
    f32 = jnp.float32
    copies = stacks_ref.shape[0] // SLICES
    pieces = []
    for piece in range(SLICES):
        total = stacks_ref[piece].astype(f32)
        for copy in range(1, copies):
            total += stacks_ref[copy * SLICES + piece].astype(f32)
        pieces.append(total)

    def product(values, table):
        both = jnp.dot(jnp.concatenate(two_terms(values), axis=0), table, preferred_element_type=f32)
        return both[:BIN_DEV] + both[BIN_DEV:]

    zero = product(jnp.concatenate(pieces[0:2], axis=1), zero_ref[...])
    two = product(jnp.concatenate(pieces[4:6], axis=1), two_ref[...])
    odd = product(jnp.concatenate(pieces[2:4] + pieces[6:8], axis=1), odd_ref[...])
    plus, minus = zero + two, zero - two
    out_ref[:, :LAGQ] = plus + odd[:, :LAGQ]
    out_ref[:, LAGQ:2 * LAGQ] = minus + odd[:, LAGQ:]
    out_ref[:, 2 * LAGQ:3 * LAGQ] = plus - odd[:, :LAGQ]
    out_ref[:, 3 * LAGQ:] = minus - odd[:, LAGQ:]


def lags(stacks):
    tables = [jnp.asarray(table) for table in inverse_tables()]
    return pl.pallas_call(
        lags_kernel,
        out_shape=jax.ShapeDtypeStruct((BIN_DEV, NLAG), jnp.float32),
        compiler_params=pltpu.CompilerParams(vmem_limit_bytes=VMEM_SMALL),
        name="lags",
    )(stacks, *tables)


def fixed_pairs(blocks):
    return [(b, b + d) for b in range(blocks) for d in range(1, R + 1) if b + d < blocks]


def sent_along(x, mask, owners, bins, total_segs):
    seg_count = lax.axis_size("seg")
    count = lax.axis_size("chan")
    early = BLOCK
    late = x.shape[0] - early
    here = lax.axis_index("chan").astype(jnp.int32).reshape(1)
    first = spectra(x, mask, owners, bins, 0, early, with_meta=True)
    first = lax.all_to_all(first, "chan", split_axis=0, concat_axis=0, tiled=True)
    second = spectra(x, mask, owners, bins, early, late, here=here)
    slots = {0: second[0]}
    for shift in SENT:
        slots[shift] = lax.ppermute(second[shift], "chan", [(i, (i + shift) % count) for i in range(count)])

    fixed = fixed_pairs(count)
    known = (0,) + SENT
    stages = [
        [(i, j) for j in range(start, end) for i in range(j)] for start, end in zip((1,) + STAGES, STAGES)
    ]
    as_slots = lambda pairs: [(-known[i] - count, -known[j] - count) for i, j in pairs]
    weights = pair_weights(here, first, early, total_segs, [fixed] + [as_slots(pairs) for pairs in stages])
    rows = count * BIN_DEV
    stacks = cross(first, fixed, early // G, rows, weights[0])
    held = [slots[slot] for slot in known]
    for end, pairs, weight in zip(STAGES, stages, weights[1:]):
        copies = seg_count if end == len(known) else None
        stacks = cross(held[:end], pairs, late // G, rows, weight, before=stacks, copies=copies)
    return stacks


def sent_at_once(x, mask, owners, bins, total_segs):
    seg_count = lax.axis_size("seg")
    count = lax.axis_size("chan")
    rows, chans = x.shape[0], mask.shape[1]
    narrow = NB // count
    splits = LANES // narrow
    here = lax.axis_index("chan").astype(jnp.int32).reshape(1)
    own = jnp.concatenate([mask, owners * BIN_DEV + bins], axis=1)
    every = lax.all_gather(own, "chan", axis=0, tiled=True).astype(jnp.bfloat16)
    every = jnp.pad(every, ((0, 0), (0, 2 * LANES - every.shape[1])))
    every = jnp.broadcast_to(every[:, None, :], (count, META, 2 * LANES))
    fixed = fixed_pairs(count)
    weights = pair_weights(here, every, 0, total_segs, [fixed])
    outgoing = spectra(x, mask, owners, bins, 0, rows)
    outgoing = outgoing.reshape(SLICES, rows, 2, splits, narrow).transpose(0, 3, 1, 2, 4)
    outgoing = outgoing.reshape(count, rows, 2 * narrow)
    wide = lax.all_to_all(outgoing, "chan", split_axis=0, concat_axis=0, tiled=True)
    wide = jnp.pad(wide.reshape(count, rows, 2, narrow), ((0, 0), (0, 0), (0, 0), (0, LANES - narrow)))
    wide = wide.reshape(count, rows, 2 * LANES)
    stacks = cross(wide, fixed, rows // G, count * BIN_DEV, weights[0], copies=seg_count)
    return stacks.reshape(-1, 2, LANES)[..., :narrow]


def per_device(traces, channel_mask, owner_ids, local_bins):
    seg_count = lax.axis_size("seg")
    count = lax.axis_size("chan")
    segs, chans, length = traces.shape
    x = traces.reshape(segs * chans, length)
    mask = channel_mask.reshape(1, chans)
    owners = owner_ids.reshape(1, -1)
    if count == SLICES:
        stacks = sent_along(x, mask, owners, local_bins, segs * seg_count)
        stacks = stacks.reshape(seg_count * count, BIN_DEV, 2 * LANES)
        stacks = lax.all_to_all(stacks, ("seg", "chan"), split_axis=0, concat_axis=0, tiled=True)
    else:
        narrow = NB // count
        stacks = sent_at_once(x, mask, owners, local_bins, segs * seg_count)
        stacks = stacks.reshape(seg_count * count, BIN_DEV, 2 * narrow)
        stacks = lax.all_to_all(stacks, ("seg", "chan"), split_axis=0, concat_axis=0, tiled=True)
        stacks = stacks.reshape(seg_count, SLICES, count // SLICES, BIN_DEV, 2, narrow)
        stacks = stacks.transpose(0, 1, 3, 4, 2, 5).reshape(seg_count * SLICES, BIN_DEV, 2 * LANES)
    return lags(stacks)


def solution(mesh):
    in_specs = (P("seg", "chan", None), P("chan"), P("chan", None, None), P("chan", None))
    out_specs = P("chan", None)
    return jax.shard_map(
        per_device, mesh=mesh, in_specs=in_specs, out_specs=out_specs, check_vma=False
    )
```

```python
import functools
import math

import jax
import jax.numpy as jnp
import ml_dtypes
import numpy as np
from jax import lax
from jax.experimental import pallas as pl
from jax.experimental.pallas import tpu as pltpu
from jax.sharding import PartitionSpec as P

NT = 4096
DEC = 2
K0 = 8
HW = 64
R = 4
G = 16
BIN_DEV = 8
NB = 1024
NLAG = 2048
EPSILON = 1e-06

LANES = 128
SLICES = NB // LANES
FOLD = 4
PART = LANES // FOLD
LAGQ = NLAG // FOLD
VMEM = 58 * 1024 * 1024
VMEM_SMALL = 20 * 1024 * 1024
BLOCK = 256
META = 16

SENT = (1, 7, 4, 3, 5, 2, 6)
STAGES = (6, 8)

WITHIN = np.arange(LANES).reshape(PART, FOLD).T.reshape(-1)
ORDER = (np.arange(SLICES)[:, None] * LANES + WITHIN[None, :]).reshape(-1)


def forward_table():
    samples = np.arange(NT, dtype=np.int64)
    freqs = K0 + ORDER.astype(np.int64)
    phase = samples[:, None] * freqs[None, :] % NT
    angle = np.arange(NT).astype(np.float32) * np.float32(2.0 * math.pi / NT)
    cos = np.cos(angle.astype(np.float64)).astype(np.float32).astype(ml_dtypes.bfloat16)
    sin = (-np.sin(angle.astype(np.float64))).astype(np.float32).astype(ml_dtypes.bfloat16)
    both = [table[phase].reshape(NT, SLICES, 1, LANES) for table in (cos, sin)]
    return np.concatenate(both, axis=2).reshape(NT, SLICES, 2 * LANES).transpose(1, 0, 2)


def band_table():
    around = (np.arange(3)[:, None] * LANES + WITHIN[None, :]).reshape(-1)
    return (np.abs(around[:, None] - (LANES + WITHIN)[None, :]) <= HW).astype(ml_dtypes.bfloat16)


def inverse_tables():
    freqs = K0 + ORDER.astype(np.int64)
    delays = (np.arange(2 * LAGQ, dtype=np.int64) - NLAG // 2) * DEC
    phase = np.mod(freqs[:, None] * delays[None, :], NT)
    angle = np.arange(NT).astype(np.float64) * (2.0 * math.pi / NT)
    scale = 1.0 / math.sqrt(NB)
    real = (np.cos(angle) * scale).astype(np.float32).astype(ml_dtypes.bfloat16)[phase]
    imag = (-np.sin(angle) * scale).astype(np.float32).astype(ml_dtypes.bfloat16)[phase]
    parts = [table.reshape(SLICES, FOLD, PART, 2 * LAGQ).transpose(1, 0, 2, 3) for table in (real, imag)]
    rows = np.stack(parts, axis=1).reshape(FOLD, 2 * SLICES * PART, 2 * LAGQ)
    return rows[0][:, :LAGQ], rows[2][:, :LAGQ], np.concatenate([rows[1], rows[3]], axis=0)


def two_terms(values):
    high = values.astype(jnp.bfloat16)
    low = (values - high.astype(jnp.float32)).astype(jnp.bfloat16)
    return high, low


def spectra_kernel(relative, with_meta, skip, *refs):
    f32, bf16 = jnp.float32, jnp.bfloat16
    refs = list(refs)
    here_ref = refs.pop(0) if relative else None
    x_any, mask_ref, owner_ref, bins_ref, table_any, band_ref = refs[:6]
    x_ref, table_ref, x_came, table_came, spectrum, power, hold = refs[-7:]
    out_refs = refs[6:-8] if relative else refs[6:-7]
    target = refs[-8] if relative else out_refs[0]
    step, steps = pl.program_id(0), pl.num_programs(0)
    first = step == 0
    rows = x_ref.shape[1]
    slot = lax.rem(step, 2)

    def trace_copy(block, slot):
        at = pl.ds(pl.multiple_of((block + skip) * rows, rows), rows)
        return pltpu.make_async_copy(x_any.at[at], x_ref.at[slot], x_came.at[slot])

    table_copies = [
        pltpu.make_async_copy(table_any.at[piece], table_ref.at[piece], table_came.at[piece])
        for piece in range(SLICES)
    ]

    @pl.when(first)
    def start():
        trace_copy(0, 0).start()
        for copy in table_copies:
            copy.start()

    shape = (LANES, LANES)
    diagonal = lax.broadcasted_iota(jnp.int32, shape, 0) == lax.broadcasted_iota(jnp.int32, shape, 1)
    mask = jnp.where(diagonal, jnp.broadcast_to(mask_ref[...], shape), 0).astype(f32)
    mask = jnp.concatenate([jnp.sum(mask, axis=1, keepdims=True)] * (rows // LANES), axis=0)
    lane = lax.broadcasted_iota(jnp.int32, (1, LANES), 1)
    place = (lane % PART) * FOLD + lane // PART
    per_group = LANES // G

    trace_copy(step, slot).wait()

    @pl.when(step + 1 < steps)
    def ahead():
        trace_copy(step + 1, 1 - slot).start()

    def whiten(piece):
        low, high = max(piece - 1, 0), min(piece + 2, SLICES)
        start = (low - piece + 1) * LANES
        sums = jnp.dot(
            power[:, low * LANES:high * LANES],
            band_ref[start:start + (high - low) * LANES],
            preferred_element_type=f32,
        )
        bin_ = place + piece * LANES
        within = jnp.minimum(bin_ + HW, NB - 1) - jnp.maximum(bin_ - HW, 0) + 1
        weight = mask * lax.rsqrt(sums * (1.0 / within.astype(f32)) + EPSILON)
        hold[piece % 2, 0] = spectrum[piece, :, :LANES] * weight
        hold[piece % 2, 1] = spectrum[piece, :, LANES:] * weight
        for seg in range(rows // LANES):
            for j in range(per_group):
                at = seg * LANES + j * G
                for half in range(2):
                    taken = hold[piece % 2, half, pl.ds(seg * LANES + j, G, stride=per_group), :]
                    target[piece, at:at + G, half * LANES:(half + 1) * LANES] = taken.astype(bf16)

    for piece in range(SLICES):
        pl.when(first)(table_copies[piece].wait)
        both = jnp.dot(x_ref[slot], table_ref[piece], preferred_element_type=f32)
        real, imag = both[:, :LANES], both[:, LANES:]
        spectrum[piece] = both
        power[:, piece * LANES:(piece + 1) * LANES] = (real * real + imag * imag).astype(bf16)
        if piece:
            whiten(piece - 1)
    whiten(SLICES - 1)

    if with_meta:
        tiles = owner_ref.shape[1]
        labels = (owner_ref[...] * BIN_DEV + bins_ref[...]).astype(f32)
        for piece in range(SLICES):
            at = pl.ds(rows, META)
            target[piece, at, :] = jnp.zeros((META, 2 * LANES), bf16)
            target[piece, at, :LANES] = jnp.broadcast_to(mask_ref[...].astype(f32), (META, LANES)).astype(bf16)
            target[piece, at, LANES:LANES + tiles] = jnp.broadcast_to(labels, (META, tiles)).astype(bf16)
    if relative:
        for other in range(SLICES):
            out_refs[other][...] = target[lax.rem(here_ref[0] + other, SLICES)]


def spectra(traces, mask, owners, bins, first_row, rows, block, here=None, with_meta=False):
    relative = here is not None
    table, band = jnp.asarray(forward_table()), jnp.asarray(band_table())
    whole = lambda array: pl.BlockSpec(array.shape, lambda i, *_: (0, 0))
    in_place = pl.BlockSpec(memory_space=pl.ANY)
    f32, bf16 = jnp.float32, jnp.bfloat16
    scratch = [
        pltpu.VMEM((2, block, NT), bf16),
        pltpu.VMEM(table.shape, bf16),
        pltpu.SemaphoreType.DMA((2,)),
        pltpu.SemaphoreType.DMA((SLICES,)),
        pltpu.VMEM((SLICES, block, 2 * LANES), f32),
        pltpu.VMEM((block, NB), bf16),
        pltpu.VMEM((2, 2, block, LANES), f32),
    ]
    if relative:
        scratch = [pltpu.VMEM((SLICES, block, 2 * LANES), bf16)] + scratch
        out_specs = [pl.BlockSpec((block, 2 * LANES), lambda i, *_: (i, 0))] * SLICES
        out_shape = [jax.ShapeDtypeStruct((rows, 2 * LANES), bf16)] * SLICES
    else:
        extra = META if with_meta else 0
        out_specs = [pl.BlockSpec((SLICES, block + extra, 2 * LANES), lambda i, *_: (0, i, 0))]
        out_shape = [jax.ShapeDtypeStruct((SLICES, rows + extra, 2 * LANES), bf16)]
    result = pl.pallas_call(
        functools.partial(spectra_kernel, relative, with_meta, first_row // block),
        grid_spec=pltpu.PrefetchScalarGridSpec(
            num_scalar_prefetch=1 if relative else 0,
            grid=(rows // block,),
            in_specs=[in_place, whole(mask), whole(owners), whole(bins), in_place, whole(band)],
            out_specs=out_specs,
            scratch_shapes=scratch,
        ),
        out_shape=out_shape,
        compiler_params=pltpu.CompilerParams(vmem_limit_bytes=VMEM),
        cost_estimate=pl.CostEstimate(
            flops=4 * rows * NT * NB, bytes_accessed=rows * NT * 3 + 4 * NT * NB, transcendentals=rows * NB
        ),
        name="spectra",
    )(*([here] if relative else []), traces, mask, owners, bins, table, band)
    return result if relative else result[0]


def pair_sums(block_refs, pairs, steps, tiles):
    f32 = jnp.float32
    done = 0
    groups, current = [], []
    for pair in pairs:
        members = {m for p in current + [pair] for m in p}
        if current and 4 * (len(current) + 1) + 4 * len(members) > 60:
            groups.append(current)
            current = []
        current = current + [pair]
    groups.append(current)
    for group in groups:
        needed = sorted({m for pair in group for m in pair})

        def body(step, sums):
            at = pl.ds(pl.multiple_of(step * G, G), G)
            real = {m: block_refs[m][at, :LANES].astype(f32) for m in needed}
            imag = {m: block_refs[m][at, LANES:].astype(f32) for m in needed}
            new = []
            for (p, q), (re, im) in zip(group, sums):
                re = re + (real[p] * real[q] + imag[p] * imag[q])
                im = im + (imag[p] * real[q] - real[p] * imag[q])
                new.append((re, im))
            return tuple(new)

        zero = jnp.zeros((G, LANES), f32)
        sums = lax.fori_loop(0, steps, body, tuple((zero, zero) for _ in group), unroll=2)
        for re, im in sums:
            tiles[done:done + G, :LANES] = re
            tiles[done:done + G, LANES:] = im
            done += G


def cross_kernel(split, pairs, steps, has_before, *refs):
    f32 = jnp.float32
    refs = list(refs)
    before_ref = refs.pop(-3) if has_before else None
    *block_refs, rows_ref, out_ref, tiles = refs
    if split:
        block_refs = [block_refs[0].at[m] for m in range(block_refs[0].shape[0])]
    pair_sums(block_refs, pairs, steps, tiles)
    bins, count = out_ref.shape[-2], tiles.shape[0]
    wanted = rows_ref[0:1, :] == lax.broadcasted_iota(jnp.int32, (bins, count), 0).astype(f32)
    high, low = two_terms(tiles[...])
    stacked = []
    for half in range(2):
        weights = jnp.where(wanted, jnp.broadcast_to(rows_ref[half + 1:half + 2, :], (bins, count)), 0.0)
        weights = jnp.concatenate(two_terms(weights), axis=0)
        at = slice(half * LANES, (half + 1) * LANES)
        both = jnp.dot(weights, high[:, at], preferred_element_type=f32)
        both = both[:bins] + both[bins:]
        stacked.append(both + jnp.dot(weights[:bins], low[:, at], preferred_element_type=f32))
    stacked = jnp.concatenate(stacked, axis=1)
    if has_before:
        stacked += before_ref[...]
    if len(out_ref.shape) == 2:
        out_ref[...] = stacked
    else:
        for copy in range(out_ref.shape[0]):
            out_ref[copy] = stacked.astype(out_ref.dtype)


def cross(blocks, pairs, steps, bins, weights, before=None, copies=None):
    shape = (bins, 2 * LANES)
    split = not isinstance(blocks, (list, tuple))
    inputs = ([blocks] if split else list(blocks)) + [weights]
    if before is not None:
        inputs.append(before)
    if copies is None:
        out_shape = jax.ShapeDtypeStruct(shape, jnp.float32)
    else:
        out_shape = jax.ShapeDtypeStruct((copies,) + shape, jnp.bfloat16)
    return pl.pallas_call(
        functools.partial(cross_kernel, split, pairs, steps, before is not None),
        out_shape=out_shape,
        scratch_shapes=[pltpu.VMEM((len(pairs) * G, 2 * LANES), jnp.float32)],
        compiler_params=pltpu.CompilerParams(vmem_limit_bytes=VMEM_SMALL if copies is None or not split else VMEM),
        cost_estimate=pl.CostEstimate(
            flops=8 * G * steps * LANES * len(pairs), bytes_accessed=4 * G * steps * LANES * len(pairs), transcendentals=0
        ),
        name="cross",
    )(*inputs)


def weights_kernel(blocks, total_segs, here_ref, meta_ref, *refs):
    f32, bf16 = jnp.float32, jnp.bfloat16
    meta = jnp.concatenate([meta_ref[b, 0:1, :] for b in range(blocks)], axis=0)
    masks, labels = meta[:, :LANES], meta[:, LANES:]
    empty = jnp.zeros((R, LANES), bf16)
    padded = jnp.concatenate([masks.astype(f32), empty.astype(f32)], axis=0)
    half = len(refs) // 2
    for ends_ref, out_ref in zip(refs[:half], refs[half:]):
        lanes = out_ref.shape[1]
        first, second = ends_ref[0:1, :], ends_ref[1:2, :]
        slots = first < 0
        held = [jnp.where(slots, lax.rem(here_ref[0] + end + 2 * blocks, blocks), end) for end in (first, second)]
        low, far = jnp.minimum(held[0], held[1]), jnp.abs(held[0] - held[1])
        sign = jnp.where(held[0] < held[1], 1.0, -1.0)
        block = lax.broadcasted_iota(jnp.int32, (blocks, lanes), 0)
        group = lax.broadcasted_iota(jnp.int32, (LANES, lanes), 1) % G
        place = lax.broadcasted_iota(jnp.int32, (LANES, lanes), 0)
        chosen = (place == (far - 1) * G + group).astype(f32).astype(bf16)
        label = jnp.dot(labels, chosen, preferred_element_type=f32)
        label = jnp.sum(jnp.where(block == low, label, 0.0), axis=0, keepdims=True)
        member = (place // (LANES // G) == group).astype(f32).astype(bf16)
        count = jnp.zeros((1, lanes), f32)
        for d in range(1, R + 1):
            both = (padded[:blocks] * padded[d:d + blocks]).astype(bf16)
            of_block = jnp.dot(both, member, preferred_element_type=f32)
            count += jnp.sum(jnp.where((block == low) & (far == d), of_block, 0.0), axis=0, keepdims=True)
        scale = jnp.where(far <= R, 1.0 / (total_segs * jnp.maximum(count, 1.0)), 0.0)
        out_ref[...] = jnp.concatenate([label, scale, scale * sign, jnp.zeros((5, lanes), f32)], axis=0)


def pair_weights(here, meta, at, total_segs, pair_lists):
    blocks = meta.shape[0]
    ends = [jnp.asarray(np.repeat(np.array(pairs, np.int32).T, G, axis=1)) for pairs in pair_lists]
    whole = lambda shape: pl.BlockSpec(shape, lambda i, *_: (0, 0))
    shapes = [(8, G * len(pairs)) for pairs in pair_lists]
    return pl.pallas_call(
        functools.partial(weights_kernel, blocks, total_segs),
        grid_spec=pltpu.PrefetchScalarGridSpec(
            num_scalar_prefetch=1,
            grid=(1,),
            in_specs=[pl.BlockSpec((blocks, META, 2 * LANES), lambda i, *_: (0, at // META, 0))]
            + [whole(end.shape) for end in ends],
            out_specs=[whole(shape) for shape in shapes],
        ),
        out_shape=[jax.ShapeDtypeStruct(shape, jnp.float32) for shape in shapes],
        compiler_params=pltpu.CompilerParams(vmem_limit_bytes=VMEM_SMALL),
        name="weights",
    )(here, meta, *ends)


def lags_kernel(stacks_ref, zero_ref, two_ref, odd_ref, out_ref):
    f32 = jnp.float32
    copies = stacks_ref.shape[0] // SLICES
    pieces = []
    for piece in range(SLICES):
        total = stacks_ref[piece].astype(f32)
        for copy in range(1, copies):
            total += stacks_ref[copy * SLICES + piece].astype(f32)
        pieces.append(total)

    def product(values, table):
        both = jnp.dot(jnp.concatenate(two_terms(values), axis=0), table, preferred_element_type=f32)
        return both[:BIN_DEV] + both[BIN_DEV:]

    def of_class(which):
        at = which * PART
        parts = [piece[:, at + half:at + half + PART] for half in (0, LANES) for piece in pieces]
        return jnp.concatenate(parts, axis=1)

    zero = product(of_class(0), zero_ref[...])
    two = product(of_class(2), two_ref[...])
    odd = product(jnp.concatenate([of_class(1), of_class(3)], axis=1), odd_ref[...])
    plus, minus = zero + two, zero - two
    out_ref[:, :LAGQ] = plus + odd[:, :LAGQ]
    out_ref[:, LAGQ:2 * LAGQ] = minus + odd[:, LAGQ:]
    out_ref[:, 2 * LAGQ:3 * LAGQ] = plus - odd[:, :LAGQ]
    out_ref[:, 3 * LAGQ:] = minus - odd[:, LAGQ:]


def lags(stacks):
    tables = [jnp.asarray(table) for table in inverse_tables()]
    return pl.pallas_call(
        lags_kernel,
        out_shape=jax.ShapeDtypeStruct((BIN_DEV, NLAG), jnp.float32),
        compiler_params=pltpu.CompilerParams(vmem_limit_bytes=VMEM_SMALL),
        name="lags",
    )(stacks, *tables)


def fixed_pairs(blocks):
    return [(b, b + d) for b in range(blocks) for d in range(1, R + 1) if b + d < blocks]


def sent_along(x, mask, owners, bins, total_segs):
    seg_count = lax.axis_size("seg")
    count = lax.axis_size("chan")
    early = BLOCK
    late = x.shape[0] - early
    here = lax.axis_index("chan").astype(jnp.int32).reshape(1)
    first = spectra(x, mask, owners, bins, 0, early, BLOCK, with_meta=True)
    first = lax.all_to_all(first, "chan", split_axis=0, concat_axis=0, tiled=True)
    second = spectra(x, mask, owners, bins, early, late, BLOCK, here=here)
    slots = {0: second[0]}
    for shift in SENT:
        slots[shift] = lax.ppermute(second[shift], "chan", [(i, (i + shift) % count) for i in range(count)])

    fixed = fixed_pairs(count)
    known = (0,) + SENT
    stages = [
        [(i, j) for j in range(start, end) for i in range(j)] for start, end in zip((1,) + STAGES, STAGES)
    ]
    as_slots = lambda pairs: [(-known[i] - count, -known[j] - count) for i, j in pairs]
    weights = pair_weights(here, first, early, total_segs, [fixed] + [as_slots(pairs) for pairs in stages])
    rows = count * BIN_DEV
    stacks = cross(first, fixed, early // G, rows, weights[0])
    held = [slots[slot] for slot in known]
    for end, pairs, weight in zip(STAGES, stages, weights[1:]):
        copies = seg_count if end == len(known) else None
        stacks = cross(held[:end], pairs, late // G, rows, weight, before=stacks, copies=copies)
    return stacks


def sent_at_once(x, mask, owners, bins, total_segs):
    seg_count = lax.axis_size("seg")
    count = lax.axis_size("chan")
    rows, chans = x.shape[0], mask.shape[1]
    narrow = NB // count
    splits = LANES // narrow
    here = lax.axis_index("chan").astype(jnp.int32).reshape(1)
    own = jnp.concatenate([mask, owners * BIN_DEV + bins], axis=1)
    every = lax.all_gather(own, "chan", axis=0, tiled=True).astype(jnp.bfloat16)
    every = jnp.pad(every, ((0, 0), (0, 2 * LANES - every.shape[1])))
    every = jnp.broadcast_to(every[:, None, :], (count, META, 2 * LANES))
    fixed = fixed_pairs(count)
    weights = pair_weights(here, every, 0, total_segs, [fixed])
    outgoing = spectra(x, mask, owners, bins, 0, rows, BLOCK)
    outgoing = outgoing.reshape(SLICES, rows, 2, splits, narrow).transpose(0, 3, 1, 2, 4)
    outgoing = outgoing.reshape(count, rows, 2 * narrow)
    wide = lax.all_to_all(outgoing, "chan", split_axis=0, concat_axis=0, tiled=True)
    wide = jnp.pad(wide.reshape(count, rows, 2, narrow), ((0, 0), (0, 0), (0, 0), (0, LANES - narrow)))
    wide = wide.reshape(count, rows, 2 * LANES)
    stacks = cross(wide, fixed, rows // G, count * BIN_DEV, weights[0], copies=seg_count)
    return stacks.reshape(-1, 2, LANES)[..., :narrow]


def per_device(traces, channel_mask, owner_ids, local_bins):
    seg_count = lax.axis_size("seg")
    count = lax.axis_size("chan")
    segs, chans, length = traces.shape
    x = traces.reshape(segs * chans, length)
    mask = channel_mask.reshape(1, chans)
    owners = owner_ids.reshape(1, -1)
    if count == SLICES:
        stacks = sent_along(x, mask, owners, local_bins, segs * seg_count)
        stacks = stacks.reshape(seg_count * count, BIN_DEV, 2 * LANES)
        stacks = lax.all_to_all(stacks, ("seg", "chan"), split_axis=0, concat_axis=0, tiled=True)
    else:
        narrow = NB // count
        stacks = sent_at_once(x, mask, owners, local_bins, segs * seg_count)
        stacks = stacks.reshape(seg_count * count, BIN_DEV, 2 * narrow)
        stacks = lax.all_to_all(stacks, ("seg", "chan"), split_axis=0, concat_axis=0, tiled=True)
        stacks = stacks.reshape(seg_count, SLICES, count // SLICES, BIN_DEV, 2, narrow)
        stacks = stacks.transpose(0, 1, 3, 4, 2, 5).reshape(seg_count * SLICES, BIN_DEV, 2 * LANES)
    return lags(stacks)


def solution(mesh):
    in_specs = (P("seg", "chan", None), P("chan"), P("chan", None, None), P("chan", None))
    out_specs = P("chan", None)
    return jax.shard_map(
        per_device, mesh=mesh, in_specs=in_specs, out_specs=out_specs, check_vma=False
    )
```

```python
import functools
import math

import jax
import jax.numpy as jnp
import ml_dtypes
import numpy as np
from jax import lax
from jax.experimental import pallas as pl
from jax.experimental.pallas import tpu as pltpu
from jax.sharding import PartitionSpec as P

NT = 4096
DEC = 2
K0 = 8
HW = 64
R = 4
G = 16
BIN_DEV = 8
NB = 1024
NLAG = 2048
EPSILON = 1e-06

LANES = 128
SLICES = NB // LANES
FOLD = 4
CLASS = NB // FOLD
QUARTER = NT // FOLD
LAGQ = NLAG // FOLD
VMEM = 58 * 1024 * 1024
VMEM_SMALL = 20 * 1024 * 1024
META = 16
KEPT = 112
EARLY_SEGS = 2
LATE_SEGS_A_BLOCK = 2

SENT = (1, 7, 4, 3, 5, 2, 6)
STAGES = (6, 8)


ORDER = np.arange(NB).reshape(CLASS, FOLD).T.reshape(-1)


def forward_tables():
    samples = np.arange(NT // 2, dtype=np.int64)
    freqs = K0 + ORDER.astype(np.int64)
    phase = samples[:, None] * freqs[None, :] % NT
    angle = (phase.astype(np.float32) * np.float32(2.0 * math.pi / NT)).astype(np.float64)
    cos = np.cos(angle).astype(np.float32).astype(ml_dtypes.bfloat16)
    sin = (-np.sin(angle)).astype(np.float32).astype(ml_dtypes.bfloat16)

    def part(which, rows):
        columns = slice(which * CLASS, (which + 1) * CLASS)
        return [cos[rows, columns], sin[rows, columns]]

    low, high = slice(0, QUARTER), slice(QUARTER, 2 * QUARTER)
    band = (np.abs(ORDER[:, None] - ORDER[None, :]) <= HW).astype(ml_dtypes.bfloat16)
    table = np.concatenate(
        [
            np.concatenate(part(0, low) + part(2, low), axis=1),
            np.concatenate(part(1, low) + part(3, low), axis=1),
            np.concatenate(part(1, high) + part(3, high), axis=1),
            band,
        ],
        axis=0,
    )
    return table


def inverse_tables():
    freqs = K0 + ORDER.astype(np.int64)
    delays = (np.arange(2 * LAGQ, dtype=np.int64) - NLAG // 2) * DEC
    phase = np.mod(freqs[:, None] * delays[None, :], NT)
    angle = phase.astype(np.float64) * (2.0 * math.pi / NT)
    scale = 1.0 / math.sqrt(NB)
    real = (np.cos(angle) * scale).reshape(SLICES, 1, LANES, 2 * LAGQ)
    imag = (-np.sin(angle) * scale).reshape(SLICES, 1, LANES, 2 * LAGQ)
    rows = np.concatenate([real, imag], axis=1).reshape(FOLD, 2 * CLASS, 2 * LAGQ)
    zero = rows[0][:, :LAGQ]
    two = rows[2][:, :LAGQ]
    odd = np.concatenate([rows[1], rows[3]], axis=0)
    return [table.astype(np.float32).astype(ml_dtypes.bfloat16) for table in (zero, two, odd)]


def two_terms(values):
    high = values.astype(jnp.bfloat16)
    low = (values - high.astype(jnp.float32)).astype(jnp.bfloat16)
    return high, low


def two_term_dot(values_ref, table):
    rows = values_ref.shape[0] // 2
    both = jnp.dot(values_ref[...], table, preferred_element_type=jnp.float32)
    return both[:rows] + both[rows:]


def ranks(mask_row):
    shape = (LANES, LANES)
    upto = lax.broadcasted_iota(jnp.int32, shape, 0) <= lax.broadcasted_iota(jnp.int32, shape, 1)
    row = jnp.broadcast_to(mask_row, (META, LANES)).astype(jnp.bfloat16)
    count = jnp.dot(row, upto.astype(jnp.float32).astype(jnp.bfloat16), preferred_element_type=jnp.float32)
    return jnp.where(mask_row > 0, count[0:1] - 1.0, -1.0)


def channel_of_place(shape, axis):
    place = lax.broadcasted_iota(jnp.int32, shape, axis)
    return (place % G) * (LANES // G) + place // G


def spectra_kernel(relative, with_meta, kept, skip, *refs):
    f32, bf16 = jnp.float32, jnp.bfloat16
    refs = list(refs)
    here_ref = refs.pop(0) if relative else None
    x_any, mask_ref, owner_ref, bins_ref, source_ref = refs[:5]
    x_refs, table_ref, x_came, arrived, u, v, a, b, early, others = refs[-10:]
    out_refs = refs[5:-11] if relative else refs[5:-10]
    head = refs[-11] if relative else out_refs[0]
    rest = out_refs[-1] if kept < LANES else None
    step, steps = pl.program_id(0), pl.num_programs(0)
    first = step == 0
    rows = x_refs.shape[1]
    slot = lax.rem(step, 2)
    copies = [
        pltpu.make_async_copy(source_ref.at[part], table_ref.at[part], arrived.at[part]) for part in range(FOLD)
    ]

    def trace_copy(block, slot):
        at = pl.ds(pl.multiple_of(block * rows + skip, LANES), rows)
        return pltpu.make_async_copy(x_any.at[at], x_refs.at[slot], x_came.at[slot])

    @pl.when(first)
    def start():
        trace_copy(0, 0).start()
        for copy in copies:
            copy.start()

    mask = mask_ref[...].astype(f32)
    shape = (LANES, LANES)
    if kept < LANES:
        chosen = ranks(mask) == lax.broadcasted_iota(jnp.int32, shape, 0).astype(f32)
    else:
        chosen = channel_of_place(shape, 0) == lax.broadcasted_iota(jnp.int32, shape, 1)
        chosen = chosen & (jnp.broadcast_to(mask, shape) > 0)
    chosen = chosen.astype(f32).astype(bf16)

    trace_copy(step, slot).wait()

    @pl.when(step + 1 < steps)
    def ahead():
        trace_copy(step + 1, 1 - slot).start()

    x_ref = x_refs.at[slot]
    x = [x_ref[:, m * QUARTER:(m + 1) * QUARTER].astype(f32) for m in range(FOLD)]
    even, odd = x[0] + x[2], x[1] + x[3]
    u[:rows], u[rows:] = two_terms(even + odd)
    v[:rows], v[rows:] = two_terms(even - odd)
    a[:rows], a[rows:] = two_terms(x[0] - x[2])
    b[:rows], b[rows:] = two_terms(x[1] - x[3])

    pl.when(first)(copies[0].wait)
    early[:, :2 * CLASS] = two_term_dot(u, table_ref[0, :, :2 * CLASS])
    early[:, 2 * CLASS:] = two_term_dot(v, table_ref[0, :, 2 * CLASS:])
    pl.when(first)(copies[1].wait)
    others[...] = two_term_dot(a, table_ref[1])
    pl.when(first)(copies[2].wait)
    others[...] += two_term_dot(b, table_ref[2])
    pl.when(first)(copies[3].wait)

    holders = [(early, 0), (others, 0), (early, 2 * CLASS), (others, 2 * CLASS)]
    power = []
    for ref, start in holders:
        real, imag = ref[:, start:start + CLASS], ref[:, start + CLASS:start + 2 * CLASS]
        power.append((real * real + imag * imag).astype(bf16))
    power = jnp.concatenate(power, axis=1)
    lane = lax.broadcasted_iota(jnp.int32, (1, NB), 1)
    bin_ = (lane % CLASS) * FOLD + lane // CLASS
    within = jnp.minimum(bin_ + HW, NB - 1) - jnp.maximum(bin_ - HW, 0) + 1
    mean = jnp.dot(power, table_ref[3], preferred_element_type=f32) * (1.0 / within.astype(f32))
    weight = lax.rsqrt(mean + EPSILON)
    spare = LANES - kept
    for piece in range(SLICES):
        ref, start = holders[piece // 2]
        start += (piece % 2) * LANES
        scale = weight[:, piece * LANES:(piece + 1) * LANES]
        real = (ref[:, start:start + LANES] * scale).astype(bf16)
        imag = (ref[:, CLASS + start:CLASS + start + LANES] * scale).astype(bf16)
        both = jnp.concatenate([real, imag], axis=1)
        for seg in range(rows // LANES):
            sorted_ = jnp.dot(chosen, both[seg * LANES:(seg + 1) * LANES], preferred_element_type=f32).astype(bf16)
            head[piece, seg * kept:(seg + 1) * kept, :] = sorted_[:kept]
            if spare:
                rest[piece, seg * spare:(seg + 1) * spare, :] = sorted_[kept:]
    if with_meta:
        tiles = owner_ref.shape[1]
        labels = (owner_ref[...] * BIN_DEV + bins_ref[...]).astype(f32)
        for piece in range(SLICES):
            at = pl.ds(rows // LANES * kept, META)
            head[piece, at, :] = jnp.zeros((META, 2 * LANES), bf16)
            head[piece, at, :LANES] = jnp.broadcast_to(mask, (META, LANES)).astype(bf16)
            head[piece, at, LANES:LANES + tiles] = jnp.broadcast_to(labels, (META, tiles)).astype(bf16)
    if relative:
        for other in range(SLICES):
            out_refs[other][...] = head[lax.rem(here_ref[0] + other, SLICES)]


def spectra(traces, mask, owners, bins, first_row, rows, block, kept, here=None, with_meta=False):
    relative = here is not None
    table = jnp.asarray(forward_tables()).reshape(FOLD, QUARTER, NB)
    whole = lambda array: pl.BlockSpec(array.shape, lambda i, *_: (0, 0))
    in_place = pl.BlockSpec(memory_space=pl.ANY)
    f32, bf16 = jnp.float32, jnp.bfloat16
    segs = block // LANES
    scratch = [
        pltpu.VMEM((2, block, NT), bf16),
        pltpu.VMEM(table.shape, bf16),
        pltpu.SemaphoreType.DMA((2,)),
        pltpu.SemaphoreType.DMA((FOLD,)),
    ]
    scratch += [pltpu.VMEM((2 * block, QUARTER), bf16)] * 4 + [pltpu.VMEM((block, 4 * CLASS), f32)] * 2
    if relative:
        scratch = [pltpu.VMEM((SLICES, segs * kept, 2 * LANES), bf16)] + scratch
        out_specs = [pl.BlockSpec((segs * kept, 2 * LANES), lambda i, *_: (i, 0))] * SLICES
        out_shape = [jax.ShapeDtypeStruct((rows // LANES * kept, 2 * LANES), bf16)] * SLICES
    else:
        extra = META if with_meta else 0
        out_specs = [pl.BlockSpec((SLICES, segs * kept + extra, 2 * LANES), lambda i, *_: (0, i, 0))]
        out_shape = [jax.ShapeDtypeStruct((SLICES, rows // LANES * kept + extra, 2 * LANES), bf16)]
    if kept < LANES:
        spare = LANES - kept
        out_specs += [pl.BlockSpec((SLICES, segs * spare, 2 * LANES), lambda i, *_: (0, i, 0))]
        out_shape += [jax.ShapeDtypeStruct((SLICES, rows // LANES * spare, 2 * LANES), bf16)]
    return pl.pallas_call(
        functools.partial(spectra_kernel, relative, with_meta, kept, first_row),
        grid_spec=pltpu.PrefetchScalarGridSpec(
            num_scalar_prefetch=1 if relative else 0,
            grid=(rows // block,),
            in_specs=[in_place, whole(mask), whole(owners), whole(bins), in_place],
            out_specs=out_specs,
            scratch_shapes=scratch,
        ),
        out_shape=out_shape,
        compiler_params=pltpu.CompilerParams(vmem_limit_bytes=VMEM),
        cost_estimate=pl.CostEstimate(
            flops=14 * rows * NB * NB, bytes_accessed=rows * NT * 3 + 8 * NB * NB, transcendentals=rows * NB
        ),
        name="spectra",
    )(*([here] if relative else []), traces, mask, owners, bins, table)


def pair_sums(block_refs, pairs, steps, tiles):
    f32 = jnp.float32
    done = 0
    groups, current = [], []
    for pair in pairs:
        members = {m for p in current + [pair] for m in p}
        if current and 4 * (len(current) + 1) + 4 * len(members) > 60:
            groups.append(current)
            current = []
        current = current + [pair]
    groups.append(current)
    for group in groups:
        needed = sorted({m for pair in group for m in pair})

        def body(step, sums):
            at = pl.ds(pl.multiple_of(step * G, G), G)
            real = {m: block_refs[m][at, :LANES].astype(f32) for m in needed}
            imag = {m: block_refs[m][at, LANES:].astype(f32) for m in needed}
            new = []
            for (p, q), (re, im) in zip(group, sums):
                re = re + (real[p] * real[q] + imag[p] * imag[q])
                im = im + (imag[p] * real[q] - real[p] * imag[q])
                new.append((re, im))
            return tuple(new)

        zero = jnp.zeros((G, LANES), f32)
        sums = lax.fori_loop(0, steps, body, tuple((zero, zero) for _ in group), unroll=2)
        for re, im in sums:
            tiles[done:done + G, :LANES] = re
            tiles[done:done + G, LANES:] = im
            done += G


def place_rows(head_ref, rest_ref, rest_row, places, out_ref):
    spare = LANES - KEPT
    for seg in range(out_ref.shape[0] // LANES):
        at = rest_row + seg * spare
        rows = jnp.concatenate([head_ref[seg * KEPT:(seg + 1) * KEPT], rest_ref[at:at + spare]], axis=0)
        placed = jnp.dot(places, rows, preferred_element_type=jnp.float32)
        out_ref[seg * LANES:(seg + 1) * LANES, :] = placed.astype(out_ref.dtype)


def cross_kernel(plan, here_ref, *refs):
    f32 = jnp.float32
    refs = list(refs)
    take = lambda count: [refs.pop(0) for _ in range(count)]
    ready, heads = take(plan["ready"]), take(plan["heads"])
    rest_ref, places_ref = take(2) if heads else (None, None)
    (rows_ref,) = take(1)
    before_ref = refs.pop(0) if plan["before"] else None
    out_ref = refs.pop(0)
    placed = take(len(plan["slots"])) if plan["hand_on"] else None
    tiles = refs.pop(0)
    if plan["stacked"]:
        source = heads[0] if heads else ready[0]
        count = source.shape[0]
        heads = [source.at[m] for m in range(count)] if heads else []
        ready = [] if heads else [source.at[m] for m in range(count)]
    if heads:
        if placed is None:
            (room,) = refs
            placed = [room.at[i] for i in range(len(heads))]
        for i, head in enumerate(heads):
            block = i if plan["stacked"] else lax.rem(here_ref[0] - plan["slots"][i] + SLICES, SLICES)
            place_rows(head, rest_ref.at[block], plan["rest_row"], places_ref[block], placed[i])
        ready = ready + placed
    pair_sums(ready, plan["pairs"], plan["steps"], tiles)
    bins, count = out_ref.shape[-2], tiles.shape[0]
    wanted = rows_ref[0:1, :] == lax.broadcasted_iota(jnp.int32, (bins, count), 0).astype(f32)
    high, low = two_terms(tiles[...])
    stacked = []
    for half in range(2):
        weights = jnp.where(wanted, jnp.broadcast_to(rows_ref[half + 1:half + 2, :], (bins, count)), 0.0)
        weights = jnp.concatenate(two_terms(weights), axis=0)
        at = slice(half * LANES, (half + 1) * LANES)
        both = jnp.dot(weights, high[:, at], preferred_element_type=f32)
        both = both[:bins] + both[bins:]
        stacked.append(both + jnp.dot(weights[:bins], low[:, at], preferred_element_type=f32))
    stacked = jnp.concatenate(stacked, axis=1)
    if before_ref is not None:
        stacked += before_ref[...]
    if len(out_ref.shape) == 2:
        out_ref[...] = stacked
    else:
        for copy in range(out_ref.shape[0]):
            out_ref[copy] = stacked.astype(out_ref.dtype)


def cross(here, pairs, steps, bins, weights, ready=(), heads=(), slots=(), rest=None, rest_row=0, places=None,
          before=None, copies=None, hand_on=False, stacked=False):
    shape = (bins, 2 * LANES)
    inputs = list(ready) + list(heads) + ([rest, places] if heads else []) + [weights]
    if before is not None:
        inputs.append(before)
    if copies is None:
        out_shape = [jax.ShapeDtypeStruct(shape, jnp.float32)]
    else:
        out_shape = [jax.ShapeDtypeStruct((copies,) + shape, jnp.bfloat16)]
    scratch = [pltpu.VMEM((len(pairs) * G, 2 * LANES), jnp.float32)]
    if hand_on:
        out_shape += [jax.ShapeDtypeStruct((G * steps, 2 * LANES), jnp.bfloat16)] * len(heads)
    elif heads:
        count = heads[0].shape[0] if stacked else len(heads)
        scratch.append(pltpu.VMEM((count, G * steps, 2 * LANES), jnp.bfloat16))
    plan = dict(
        ready=len(ready), heads=len(heads), slots=slots, before=before is not None, hand_on=hand_on,
        stacked=stacked, rest_row=rest_row, pairs=pairs, steps=steps,
    )
    whole = lambda array: pl.BlockSpec(array.shape, lambda i, *_: (0,) * len(array.shape))
    result = pl.pallas_call(
        functools.partial(cross_kernel, plan),
        grid_spec=pltpu.PrefetchScalarGridSpec(
            num_scalar_prefetch=1,
            grid=(1,),
            in_specs=[whole(array) for array in inputs],
            out_specs=[whole(array) for array in out_shape],
            scratch_shapes=scratch,
        ),
        out_shape=out_shape,
        compiler_params=pltpu.CompilerParams(vmem_limit_bytes=VMEM if stacked and copies else VMEM_SMALL),
        cost_estimate=pl.CostEstimate(
            flops=8 * G * steps * LANES * len(pairs), bytes_accessed=4 * G * steps * LANES * len(pairs), transcendentals=0
        ),
        name="cross",
    )(here, *inputs)
    return result if hand_on else result[0]


def weights_kernel(blocks, total_segs, here_ref, meta_ref, *refs):
    f32, bf16 = jnp.float32, jnp.bfloat16
    meta = jnp.concatenate([meta_ref[b, 0:1, :] for b in range(blocks)], axis=0)
    masks, labels = meta[:, :LANES], meta[:, LANES:]
    empty = jnp.zeros((R, LANES), bf16)
    padded = jnp.concatenate([masks.astype(f32), empty.astype(f32)], axis=0)
    half = len(refs) // 2
    places_ref = refs[-1]
    shape = (LANES, LANES)
    channel = lax.broadcasted_iota(jnp.int32, shape, 1)
    of_place = (channel_of_place(shape, 0) == channel).astype(f32).astype(bf16)
    for b in range(blocks):
        rank = ranks(masks[b:b + 1].astype(f32))
        sorted_ = (rank == lax.broadcasted_iota(jnp.int32, shape, 0).astype(f32)).astype(f32).astype(bf16)
        places = lax.dot_general(of_place, sorted_, (((1,), (1,)), ((), ())), preferred_element_type=f32)
        places_ref[b] = places.astype(bf16)
    for ends_ref, out_ref in zip(refs[:half], refs[half:-1]):
        lanes = out_ref.shape[1]
        first, second = ends_ref[0:1, :], ends_ref[1:2, :]
        slots = first < 0
        held = [jnp.where(slots, lax.rem(here_ref[0] + end + 2 * blocks, blocks), end) for end in (first, second)]
        low, far = jnp.minimum(held[0], held[1]), jnp.abs(held[0] - held[1])
        sign = jnp.where(held[0] < held[1], 1.0, -1.0)
        block = lax.broadcasted_iota(jnp.int32, (blocks, lanes), 0)
        group = lax.broadcasted_iota(jnp.int32, (LANES, lanes), 1) % G
        place = lax.broadcasted_iota(jnp.int32, (LANES, lanes), 0)
        chosen = (place == (far - 1) * G + group).astype(f32).astype(bf16)
        label = jnp.dot(labels, chosen, preferred_element_type=f32)
        label = jnp.sum(jnp.where(block == low, label, 0.0), axis=0, keepdims=True)
        member = (place // (LANES // G) == group).astype(f32).astype(bf16)
        count = jnp.zeros((1, lanes), f32)
        for d in range(1, R + 1):
            both = (padded[:blocks] * padded[d:d + blocks]).astype(bf16)
            of_block = jnp.dot(both, member, preferred_element_type=f32)
            count += jnp.sum(jnp.where((block == low) & (far == d), of_block, 0.0), axis=0, keepdims=True)
        scale = jnp.where(far <= R, 1.0 / (total_segs * jnp.maximum(count, 1.0)), 0.0)
        out_ref[...] = jnp.concatenate([label, scale, scale * sign, jnp.zeros((5, lanes), f32)], axis=0)


def pair_weights(here, meta, at, total_segs, pair_lists):
    blocks = meta.shape[0]
    ends = [jnp.asarray(np.repeat(np.array(pairs, np.int32).T, G, axis=1)) for pairs in pair_lists]
    whole = lambda shape: pl.BlockSpec(shape, lambda i, *_: (0, 0))
    shapes = [(8, G * len(pairs)) for pairs in pair_lists]
    return pl.pallas_call(
        functools.partial(weights_kernel, blocks, total_segs),
        grid_spec=pltpu.PrefetchScalarGridSpec(
            num_scalar_prefetch=1,
            grid=(1,),
            in_specs=[pl.BlockSpec((blocks, META, 2 * LANES), lambda i, *_: (0, at // META, 0))]
            + [whole(end.shape) for end in ends],
            out_specs=[whole(shape) for shape in shapes]
            + [pl.BlockSpec((blocks, LANES, LANES), lambda i, *_: (0, 0, 0))],
        ),
        out_shape=[jax.ShapeDtypeStruct(shape, jnp.float32) for shape in shapes]
        + [jax.ShapeDtypeStruct((blocks, LANES, LANES), jnp.bfloat16)],
        compiler_params=pltpu.CompilerParams(vmem_limit_bytes=VMEM_SMALL),
        name="weights",
    )(here, meta, *ends)


def lags_kernel(stacks_ref, zero_ref, two_ref, odd_ref, out_ref):
    f32 = jnp.float32
    copies = stacks_ref.shape[0] // SLICES
    pieces = []
    for piece in range(SLICES):
        total = stacks_ref[piece].astype(f32)
        for copy in range(1, copies):
            total += stacks_ref[copy * SLICES + piece].astype(f32)
        pieces.append(total)

    def product(values, table):
        both = jnp.dot(jnp.concatenate(two_terms(values), axis=0), table, preferred_element_type=f32)
        return both[:BIN_DEV] + both[BIN_DEV:]

    zero = product(jnp.concatenate(pieces[0:2], axis=1), zero_ref[...])
    two = product(jnp.concatenate(pieces[4:6], axis=1), two_ref[...])
    odd = product(jnp.concatenate(pieces[2:4] + pieces[6:8], axis=1), odd_ref[...])
    plus, minus = zero + two, zero - two
    out_ref[:, :LAGQ] = plus + odd[:, :LAGQ]
    out_ref[:, LAGQ:2 * LAGQ] = minus + odd[:, LAGQ:]
    out_ref[:, 2 * LAGQ:3 * LAGQ] = plus - odd[:, :LAGQ]
    out_ref[:, 3 * LAGQ:] = minus - odd[:, LAGQ:]


def lags(stacks):
    tables = [jnp.asarray(table) for table in inverse_tables()]
    return pl.pallas_call(
        lags_kernel,
        out_shape=jax.ShapeDtypeStruct((BIN_DEV, NLAG), jnp.float32),
        compiler_params=pltpu.CompilerParams(vmem_limit_bytes=VMEM_SMALL),
        name="lags",
    )(stacks, *tables)


def fixed_pairs(blocks):
    return [(b, b + d) for b in range(blocks) for d in range(1, R + 1) if b + d < blocks]


def sent_along(x, mask, owners, bins, total_segs):
    seg_count = lax.axis_size("seg")
    count = lax.axis_size("chan")
    early = EARLY_SEGS * LANES
    late = x.shape[0] - early
    spare = LANES - KEPT
    here = lax.axis_index("chan").astype(jnp.int32).reshape(1)
    first, spare_early = spectra(x, mask, owners, bins, 0, early, early, KEPT, with_meta=True)
    first = lax.all_to_all(first, "chan", split_axis=0, concat_axis=0, tiled=True)
    *second, spare_late = spectra(
        x, mask, owners, bins, early, late, LATE_SEGS_A_BLOCK * LANES, KEPT, here=here
    )
    slots = {0: second[0]}
    for shift in SENT:
        slots[shift] = lax.ppermute(second[shift], "chan", [(i, (i + shift) % count) for i in range(count)])

    at = EARLY_SEGS * KEPT
    most = jnp.max(jnp.sum(first[:, at, :LANES].astype(jnp.float32), axis=1))
    rest = lax.cond(
        most > KEPT,
        lambda rows: lax.all_to_all(jnp.concatenate(rows, axis=1), "chan", split_axis=0, concat_axis=0, tiled=True),
        lambda rows: jnp.zeros((count, (early + late) // LANES * spare, 2 * LANES), jnp.bfloat16),
        (spare_early, spare_late),
    )

    fixed = fixed_pairs(count)
    known = (0,) + SENT
    stages = [
        [(i, j) for j in range(start, end) for i in range(j)] for start, end in zip((1,) + STAGES, STAGES)
    ]
    as_slots = lambda pairs: [(-known[i] - count, -known[j] - count) for i, j in pairs]
    weights = pair_weights(here, first, at, total_segs, [fixed] + [as_slots(pairs) for pairs in stages])
    places = weights[-1]
    bins = count * BIN_DEV
    stacks = cross(
        here, fixed, early // G, bins, weights[0], heads=[first], rest=rest, places=places, stacked=True
    )
    ready, start = [], 0
    for end, pairs, weight in zip(STAGES, stages, weights[1:]):
        final = end == len(known)
        result = cross(
            here, pairs, late // G, bins, weight,
            ready=ready, heads=[slots[slot] for slot in known[start:end]], slots=known[start:end],
            rest=rest, rest_row=EARLY_SEGS * spare, places=places, before=stacks,
            copies=seg_count if final else None, hand_on=not final,
        )
        if final:
            return result
        stacks, ready, start = result[0], ready + list(result[1:]), end


def sent_at_once(x, mask, owners, bins, total_segs):
    seg_count = lax.axis_size("seg")
    count = lax.axis_size("chan")
    rows, chans = x.shape[0], mask.shape[1]
    narrow = NB // count
    splits = LANES // narrow
    here = lax.axis_index("chan").astype(jnp.int32).reshape(1)
    own = jnp.concatenate([mask, owners * BIN_DEV + bins], axis=1)
    every = lax.all_gather(own, "chan", axis=0, tiled=True).astype(jnp.bfloat16)
    every = jnp.pad(every, ((0, 0), (0, 2 * LANES - every.shape[1])))
    every = jnp.broadcast_to(every[:, None, :], (count, META, 2 * LANES))
    fixed = fixed_pairs(count)
    weights = pair_weights(here, every, 0, total_segs, [fixed])[:1]
    (outgoing,) = spectra(x, mask, owners, bins, 0, rows, 2 * LANES, LANES)
    outgoing = outgoing.reshape(SLICES, rows, 2, splits, narrow).transpose(0, 3, 1, 2, 4)
    outgoing = outgoing.reshape(count, rows, 2 * narrow)
    wide = lax.all_to_all(outgoing, "chan", split_axis=0, concat_axis=0, tiled=True)
    wide = jnp.pad(wide.reshape(count, rows, 2, narrow), ((0, 0), (0, 0), (0, 0), (0, LANES - narrow)))
    wide = wide.reshape(count, rows, 2 * LANES)
    stacks = cross(
        here, fixed, rows // G, count * BIN_DEV, weights[0], ready=[wide], copies=seg_count, stacked=True
    )
    return stacks.reshape(-1, 2, LANES)[..., :narrow]


def per_device(traces, channel_mask, owner_ids, local_bins):
    seg_count = lax.axis_size("seg")
    count = lax.axis_size("chan")
    segs, chans, length = traces.shape
    x = traces.reshape(segs * chans, length)
    mask = channel_mask.reshape(1, chans)
    owners = owner_ids.reshape(1, -1)
    if count == SLICES:
        stacks = sent_along(x, mask, owners, local_bins, segs * seg_count)
        stacks = stacks.reshape(seg_count * count, BIN_DEV, 2 * LANES)
        stacks = lax.all_to_all(stacks, ("seg", "chan"), split_axis=0, concat_axis=0, tiled=True)
    else:
        narrow = NB // count
        stacks = sent_at_once(x, mask, owners, local_bins, segs * seg_count)
        stacks = stacks.reshape(seg_count * count, BIN_DEV, 2 * narrow)
        stacks = lax.all_to_all(stacks, ("seg", "chan"), split_axis=0, concat_axis=0, tiled=True)
        stacks = stacks.reshape(seg_count, SLICES, count // SLICES, BIN_DEV, 2, narrow)
        stacks = stacks.transpose(0, 1, 3, 4, 2, 5).reshape(seg_count * SLICES, BIN_DEV, 2 * LANES)
    return lags(stacks)


def solution(mesh):
    in_specs = (P("seg", "chan", None), P("chan"), P("chan", None, None), P("chan", None))
    out_specs = P("chan", None)
    return jax.shard_map(
        per_device, mesh=mesh, in_specs=in_specs, out_specs=out_specs, check_vma=False
    )
```

```python
import functools
import math

import jax
import jax.numpy as jnp
import ml_dtypes
import numpy as np
from jax import lax
from jax.experimental import pallas as pl
from jax.experimental.pallas import tpu as pltpu
from jax.sharding import PartitionSpec as P

NT = 4096
DEC = 2
K0 = 8
HW = 64
R = 4
G = 16
BIN_DEV = 8
NB = 1024
NLAG = 2048
EPSILON = 1e-06

LANES = 128
SLICES = NB // LANES
FOLD = 4
CLASS = NB // FOLD
QUARTER = NT // FOLD
LAGQ = NLAG // FOLD
VMEM = 58 * 1024 * 1024
VMEM_SMALL = 20 * 1024 * 1024
META = 16
KEPT = 112
EARLY_SEGS = 2
LATE_SEGS_A_BLOCK = 2

SENT = (1, 7, 4, 3, 5, 2, 6)
STAGES = (6, 8)


ORDER = np.arange(NB).reshape(CLASS, FOLD).T.reshape(-1)


def forward_tables():
    samples = np.arange(QUARTER, dtype=np.int64)
    freqs = K0 + ORDER.astype(np.int64)
    phase = samples[:, None] * freqs[None, :] % NT
    angle = (phase.astype(np.float32) * np.float32(2.0 * math.pi / NT)).astype(np.float64)
    cos = np.cos(angle).astype(np.float32).astype(ml_dtypes.bfloat16)
    sin = (-np.sin(angle)).astype(np.float32).astype(ml_dtypes.bfloat16)

    def part(which):
        columns = slice(which * CLASS, (which + 1) * CLASS)
        return [cos[:, columns], sin[:, columns]]

    return np.stack([np.concatenate(part(i) + part(i + 2), axis=1) for i in range(2)])


def band_table():
    near = np.arange(CLASS)
    apart = FOLD * (near[:, None] - near[None, :])
    blocks = [np.abs(apart + shift) <= HW for shift in (0, -1, 1)]
    return np.concatenate(blocks, axis=0).astype(ml_dtypes.bfloat16)


def inverse_tables():
    freqs = K0 + ORDER.astype(np.int64)
    delays = (np.arange(2 * LAGQ, dtype=np.int64) - NLAG // 2) * DEC
    phase = np.mod(freqs[:, None] * delays[None, :], NT)
    angle = phase.astype(np.float64) * (2.0 * math.pi / NT)
    scale = 1.0 / math.sqrt(NB)
    real = (np.cos(angle) * scale).reshape(SLICES, 1, LANES, 2 * LAGQ)
    imag = (-np.sin(angle) * scale).reshape(SLICES, 1, LANES, 2 * LAGQ)
    rows = np.concatenate([real, imag], axis=1).reshape(FOLD, 2 * CLASS, 2 * LAGQ)
    zero = rows[0][:, :LAGQ]
    two = rows[2][:, :LAGQ]
    odd = np.concatenate([rows[1], rows[3]], axis=0)
    return [table.astype(np.float32).astype(ml_dtypes.bfloat16) for table in (zero, two, odd)]


def two_terms(values):
    high = values.astype(jnp.bfloat16)
    low = (values - high.astype(jnp.float32)).astype(jnp.bfloat16)
    return high, low


def two_term_dot(values_ref, table):
    rows = values_ref.shape[0] // 2
    both = jnp.dot(values_ref[...], table, preferred_element_type=jnp.float32)
    return both[:rows] + both[rows:]


def ranks(mask_row):
    shape = (LANES, LANES)
    upto = lax.broadcasted_iota(jnp.int32, shape, 0) <= lax.broadcasted_iota(jnp.int32, shape, 1)
    row = jnp.broadcast_to(mask_row, (META, LANES)).astype(jnp.bfloat16)
    count = jnp.dot(row, upto.astype(jnp.float32).astype(jnp.bfloat16), preferred_element_type=jnp.float32)
    return jnp.where(mask_row > 0, count[0:1] - 1.0, -1.0)


def channel_of_place(shape, axis):
    place = lax.broadcasted_iota(jnp.int32, shape, axis)
    return (place % G) * (LANES // G) + place // G


def spectra_kernel(relative, with_meta, kept, skip, alone, *refs):
    f32, bf16 = jnp.float32, jnp.bfloat16
    refs = list(refs)
    here_ref = refs.pop(0) if relative else None
    x_any, mask_ref, owner_ref, bins_ref, source_ref, band_any = refs[:6]
    x_refs, table_ref, band_ref, x_came, arrived, u, v, ab, early, others, windows = refs[-11:]
    out_refs = refs[6:-12] if relative else refs[6:-11]
    head = refs[-12] if relative else out_refs[0]
    rest = out_refs[-1] if kept < LANES else None
    step, steps = pl.program_id(0), pl.num_programs(0)
    first = step == 0
    rows = x_refs.shape[1]
    slot = 0 if alone else lax.rem(step, 2)
    at_first = (lambda act: act()) if alone else pl.when(first)
    copies = [
        pltpu.make_async_copy(source_ref.at[part], table_ref.at[part], arrived.at[part]) for part in range(2)
    ] + [pltpu.make_async_copy(band_any, band_ref, arrived.at[2])]

    def trace_copy(block, slot):
        at = pl.ds(pl.multiple_of(block * rows + skip, LANES), rows)
        return pltpu.make_async_copy(x_any.at[at], x_refs.at[slot], x_came.at[slot])

    @at_first
    def start():
        trace_copy(0, 0).start()
        for copy in copies:
            copy.start()

    mask = mask_ref[...].astype(f32)
    shape = (LANES, LANES)
    if kept < LANES:
        chosen = ranks(mask) == lax.broadcasted_iota(jnp.int32, shape, 0).astype(f32)
    else:
        chosen = channel_of_place(shape, 0) == lax.broadcasted_iota(jnp.int32, shape, 1)
        chosen = chosen & (jnp.broadcast_to(mask, shape) > 0)
    chosen = chosen.astype(f32).astype(bf16)

    trace_copy(step, slot).wait()

    if not alone:

        @pl.when(step + 1 < steps)
        def ahead():
            trace_copy(step + 1, 1 - slot).start()

    @at_first
    def table_waits():
        for copy in copies:
            copy.wait()

    x_ref = x_refs.at[slot]
    x = [x_ref[:, m * QUARTER:(m + 1) * QUARTER].astype(f32) for m in range(FOLD)]
    even, odd = x[0] + x[2], x[1] + x[3]
    u[:rows], u[rows:] = two_terms(even + odd)
    v[:rows], v[rows:] = two_terms(even - odd)
    ab[:rows], ab[rows:2 * rows] = two_terms(x[0] - x[2])
    ab[2 * rows:3 * rows], ab[3 * rows:] = two_terms(x[1] - x[3])

    early[:, :2 * CLASS] = two_term_dot(u, table_ref[0, :, :2 * CLASS])
    early[:, 2 * CLASS:] = two_term_dot(v, table_ref[0, :, 2 * CLASS:])
    turned = jnp.dot(ab[...], table_ref[1], preferred_element_type=f32)
    straight = turned[:rows] + turned[rows:2 * rows]
    turned = turned[2 * rows:3 * rows] + turned[3 * rows:]
    columns = [slice(i * CLASS, (i + 1) * CLASS) for i in range(4)]
    others[:, columns[0]] = straight[:, columns[0]] + turned[:, columns[1]]
    others[:, columns[1]] = straight[:, columns[1]] - turned[:, columns[0]]
    others[:, columns[2]] = straight[:, columns[2]] - turned[:, columns[3]]
    others[:, columns[3]] = straight[:, columns[3]] + turned[:, columns[2]]

    holders = [(early, 0), (others, 0), (early, 2 * CLASS), (others, 2 * CLASS)]
    power = []
    for ref, start in holders:
        real, imag = ref[:, start:start + CLASS], ref[:, start + CLASS:start + 2 * CLASS]
        power.append(real * real + imag * imag)
    before = [jnp.zeros_like(power[0]), power[0], power[0] + power[1], power[0] + power[1] + power[2]]
    after = [power[1] + power[2] + power[3], power[2] + power[3], power[3], jnp.zeros_like(power[0])]
    for which in range(FOLD):
        at = slice(which * rows, (which + 1) * rows)
        windows[at, :CLASS] = power[which].astype(bf16)
        windows[at, CLASS:2 * CLASS] = before[which].astype(bf16)
        windows[at, 2 * CLASS:] = after[which].astype(bf16)
    sums = jnp.dot(windows[...], band_ref[...], preferred_element_type=f32)
    weight = []
    for which in range(FOLD):
        bin_ = lax.broadcasted_iota(jnp.int32, (1, CLASS), 1) * FOLD + which
        within = jnp.minimum(bin_ + HW, NB - 1) - jnp.maximum(bin_ - HW, 0) + 1
        mean = sums[which * rows:(which + 1) * rows] * (1.0 / within.astype(f32))
        weight.append(lax.rsqrt(mean + EPSILON))
    spare = LANES - kept
    for piece in range(SLICES):
        ref, start = holders[piece // 2]
        start += (piece % 2) * LANES
        scale = weight[piece // 2][:, (piece % 2) * LANES:(piece % 2 + 1) * LANES]
        real = (ref[:, start:start + LANES] * scale).astype(bf16)
        imag = (ref[:, CLASS + start:CLASS + start + LANES] * scale).astype(bf16)
        both = jnp.concatenate([real, imag], axis=1)
        for seg in range(rows // LANES):
            sorted_ = jnp.dot(chosen, both[seg * LANES:(seg + 1) * LANES], preferred_element_type=f32).astype(bf16)
            head[piece, seg * kept:(seg + 1) * kept, :] = sorted_[:kept]
            if spare:
                rest[piece, seg * spare:(seg + 1) * spare, :] = sorted_[kept:]
    if with_meta:
        tiles = owner_ref.shape[1]
        labels = (owner_ref[...] * BIN_DEV + bins_ref[...]).astype(f32)
        for piece in range(SLICES):
            at = pl.ds(rows // LANES * kept, META)
            head[piece, at, :] = jnp.zeros((META, 2 * LANES), bf16)
            head[piece, at, :LANES] = jnp.broadcast_to(mask, (META, LANES)).astype(bf16)
            head[piece, at, LANES:LANES + tiles] = jnp.broadcast_to(labels, (META, tiles)).astype(bf16)
    if relative:
        for other in range(SLICES):
            out_refs[other][...] = head[lax.rem(here_ref[0] + other, SLICES)]


def spectra(traces, mask, owners, bins, first_row, rows, block, kept, here=None, with_meta=False):
    relative = here is not None
    table, band = jnp.asarray(forward_tables()), jnp.asarray(band_table())
    whole = lambda array: pl.BlockSpec(array.shape, lambda i, *_: (0, 0))
    in_place = pl.BlockSpec(memory_space=pl.ANY)
    f32, bf16 = jnp.float32, jnp.bfloat16
    segs = block // LANES
    scratch = [
        pltpu.VMEM((2, block, NT), bf16),
        pltpu.VMEM(table.shape, bf16),
        pltpu.VMEM(band.shape, bf16),
        pltpu.SemaphoreType.DMA((2,)),
        pltpu.SemaphoreType.DMA((3,)),
    ]
    scratch += [pltpu.VMEM((terms * block, QUARTER), bf16) for terms in (2, 2, 4)]
    scratch += [pltpu.VMEM((block, 4 * CLASS), f32)] * 2
    scratch += [pltpu.VMEM((FOLD * block, 3 * CLASS), bf16)]
    if relative:
        scratch = [pltpu.VMEM((SLICES, segs * kept, 2 * LANES), bf16)] + scratch
        out_specs = [pl.BlockSpec((segs * kept, 2 * LANES), lambda i, *_: (i, 0))] * SLICES
        out_shape = [jax.ShapeDtypeStruct((rows // LANES * kept, 2 * LANES), bf16)] * SLICES
    else:
        extra = META if with_meta else 0
        out_specs = [pl.BlockSpec((SLICES, segs * kept + extra, 2 * LANES), lambda i, *_: (0, i, 0))]
        out_shape = [jax.ShapeDtypeStruct((SLICES, rows // LANES * kept + extra, 2 * LANES), bf16)]
    if kept < LANES:
        spare = LANES - kept
        out_specs += [pl.BlockSpec((SLICES, segs * spare, 2 * LANES), lambda i, *_: (0, i, 0))]
        out_shape += [jax.ShapeDtypeStruct((SLICES, rows // LANES * spare, 2 * LANES), bf16)]
    return pl.pallas_call(
        functools.partial(spectra_kernel, relative, with_meta, kept, first_row, rows == block),
        grid_spec=pltpu.PrefetchScalarGridSpec(
            num_scalar_prefetch=1 if relative else 0,
            grid=(rows // block,),
            in_specs=[in_place, whole(mask), whole(owners), whole(bins), in_place, in_place],
            out_specs=out_specs,
            scratch_shapes=scratch,
        ),
        out_shape=out_shape,
        compiler_params=pltpu.CompilerParams(vmem_limit_bytes=VMEM),
        cost_estimate=pl.CostEstimate(
            flops=14 * rows * NB * NB, bytes_accessed=rows * NT * 3 + 8 * NB * NB, transcendentals=rows * NB
        ),
        name="spectra",
    )(*([here] if relative else []), traces, mask, owners, bins, table, band)


def pair_sums(block_refs, pairs, steps, tiles):
    f32 = jnp.float32
    done = 0
    groups, current = [], []
    for pair in pairs:
        members = {m for p in current + [pair] for m in p}
        if current and 4 * (len(current) + 1) + 4 * len(members) > 60:
            groups.append(current)
            current = []
        current = current + [pair]
    groups.append(current)
    for group in groups:
        needed = sorted({m for pair in group for m in pair})

        def body(step, sums):
            at = pl.ds(pl.multiple_of(step * G, G), G)
            real = {m: block_refs[m][at, :LANES].astype(f32) for m in needed}
            imag = {m: block_refs[m][at, LANES:].astype(f32) for m in needed}
            new = []
            for (p, q), (re, im) in zip(group, sums):
                re = re + (real[p] * real[q] + imag[p] * imag[q])
                im = im + (imag[p] * real[q] - real[p] * imag[q])
                new.append((re, im))
            return tuple(new)

        zero = jnp.zeros((G, LANES), f32)
        sums = lax.fori_loop(0, steps, body, tuple((zero, zero) for _ in group), unroll=2)
        for re, im in sums:
            tiles[done:done + G, :LANES] = re
            tiles[done:done + G, LANES:] = im
            done += G


def place_rows(head_ref, rest_ref, rest_row, places, out_ref):
    spare = LANES - KEPT
    for seg in range(out_ref.shape[0] // LANES):
        at = rest_row + seg * spare
        rows = jnp.concatenate([head_ref[seg * KEPT:(seg + 1) * KEPT], rest_ref[at:at + spare]], axis=0)
        placed = jnp.dot(places, rows, preferred_element_type=jnp.float32)
        out_ref[seg * LANES:(seg + 1) * LANES, :] = placed.astype(out_ref.dtype)


def cross_kernel(plan, here_ref, *refs):
    f32 = jnp.float32
    refs = list(refs)
    take = lambda count: [refs.pop(0) for _ in range(count)]
    ready, heads = take(plan["ready"]), take(plan["heads"])
    rest_ref, places_ref = take(2) if heads else (None, None)
    (rows_ref,) = take(1)
    before_ref = refs.pop(0) if plan["before"] else None
    out_ref = refs.pop(0)
    placed = take(len(plan["slots"])) if plan["hand_on"] else None
    tiles = refs.pop(0)
    if plan["stacked"]:
        source = heads[0] if heads else ready[0]
        count = source.shape[0]
        heads = [source.at[m] for m in range(count)] if heads else []
        ready = [] if heads else [source.at[m] for m in range(count)]
    if heads:
        if placed is None:
            (room,) = refs
            placed = [room.at[i] for i in range(len(heads))]
        for i, head in enumerate(heads):
            block = i if plan["stacked"] else lax.rem(here_ref[0] - plan["slots"][i] + SLICES, SLICES)
            place_rows(head, rest_ref.at[block], plan["rest_row"], places_ref[block], placed[i])
        ready = ready + placed
    pair_sums(ready, plan["pairs"], plan["steps"], tiles)
    bins, count = out_ref.shape[-2], tiles.shape[0]
    wanted = rows_ref[0:1, :] == lax.broadcasted_iota(jnp.int32, (bins, count), 0).astype(f32)
    high, low = two_terms(tiles[...])
    stacked = []
    for half in range(2):
        weights = jnp.where(wanted, jnp.broadcast_to(rows_ref[half + 1:half + 2, :], (bins, count)), 0.0)
        weights = jnp.concatenate(two_terms(weights), axis=0)
        at = slice(half * LANES, (half + 1) * LANES)
        both = jnp.dot(weights, high[:, at], preferred_element_type=f32)
        both = both[:bins] + both[bins:]
        stacked.append(both + jnp.dot(weights[:bins], low[:, at], preferred_element_type=f32))
    stacked = jnp.concatenate(stacked, axis=1)
    if before_ref is not None:
        stacked += before_ref[...]
    if len(out_ref.shape) == 2:
        out_ref[...] = stacked
    else:
        for copy in range(out_ref.shape[0]):
            out_ref[copy] = stacked.astype(out_ref.dtype)


def cross(here, pairs, steps, bins, weights, ready=(), heads=(), slots=(), rest=None, rest_row=0, places=None,
          before=None, copies=None, hand_on=False, stacked=False):
    shape = (bins, 2 * LANES)
    inputs = list(ready) + list(heads) + ([rest, places] if heads else []) + [weights]
    if before is not None:
        inputs.append(before)
    if copies is None:
        out_shape = [jax.ShapeDtypeStruct(shape, jnp.float32)]
    else:
        out_shape = [jax.ShapeDtypeStruct((copies,) + shape, jnp.bfloat16)]
    scratch = [pltpu.VMEM((len(pairs) * G, 2 * LANES), jnp.float32)]
    if hand_on:
        out_shape += [jax.ShapeDtypeStruct((G * steps, 2 * LANES), jnp.bfloat16)] * len(heads)
    elif heads:
        count = heads[0].shape[0] if stacked else len(heads)
        scratch.append(pltpu.VMEM((count, G * steps, 2 * LANES), jnp.bfloat16))
    plan = dict(
        ready=len(ready), heads=len(heads), slots=slots, before=before is not None, hand_on=hand_on,
        stacked=stacked, rest_row=rest_row, pairs=pairs, steps=steps,
    )
    result = pl.pallas_call(
        functools.partial(cross_kernel, plan),
        in_specs=[pl.BlockSpec(memory_space=pltpu.SMEM)] + [pl.BlockSpec(memory_space=pltpu.VMEM)] * len(inputs),
        out_shape=out_shape,
        scratch_shapes=scratch,
        compiler_params=pltpu.CompilerParams(vmem_limit_bytes=VMEM if stacked and copies else VMEM_SMALL),
        cost_estimate=pl.CostEstimate(
            flops=8 * G * steps * LANES * len(pairs), bytes_accessed=4 * G * steps * LANES * len(pairs), transcendentals=0
        ),
        name="cross",
    )(here, *inputs)
    return result if hand_on else result[0]


def weights_kernel(blocks, total_segs, here_ref, meta_ref, *refs):
    f32, bf16 = jnp.float32, jnp.bfloat16
    meta = jnp.concatenate([meta_ref[b, 0:1, :] for b in range(blocks)], axis=0)
    masks, labels = meta[:, :LANES], meta[:, LANES:]
    empty = jnp.zeros((R, LANES), bf16)
    padded = jnp.concatenate([masks.astype(f32), empty.astype(f32)], axis=0)
    half = len(refs) // 2
    places_ref = refs[-1]
    shape = (LANES, LANES)
    channel = lax.broadcasted_iota(jnp.int32, shape, 1)
    of_place = (channel_of_place(shape, 0) == channel).astype(f32).astype(bf16)
    for b in range(blocks):
        rank = ranks(masks[b:b + 1].astype(f32))
        sorted_ = (rank == lax.broadcasted_iota(jnp.int32, shape, 0).astype(f32)).astype(f32).astype(bf16)
        places = lax.dot_general(of_place, sorted_, (((1,), (1,)), ((), ())), preferred_element_type=f32)
        places_ref[b] = places.astype(bf16)
    for ends_ref, out_ref in zip(refs[:half], refs[half:-1]):
        lanes = out_ref.shape[1]
        first, second = ends_ref[0:1, :], ends_ref[1:2, :]
        slots = first < 0
        held = [jnp.where(slots, lax.rem(here_ref[0] + end + 2 * blocks, blocks), end) for end in (first, second)]
        low, far = jnp.minimum(held[0], held[1]), jnp.abs(held[0] - held[1])
        sign = jnp.where(held[0] < held[1], 1.0, -1.0)
        block = lax.broadcasted_iota(jnp.int32, (blocks, lanes), 0)
        group = lax.broadcasted_iota(jnp.int32, (LANES, lanes), 1) % G
        place = lax.broadcasted_iota(jnp.int32, (LANES, lanes), 0)
        chosen = (place == (far - 1) * G + group).astype(f32).astype(bf16)
        label = jnp.dot(labels, chosen, preferred_element_type=f32)
        label = jnp.sum(jnp.where(block == low, label, 0.0), axis=0, keepdims=True)
        member = (place // (LANES // G) == group).astype(f32).astype(bf16)
        count = jnp.zeros((1, lanes), f32)
        for d in range(1, R + 1):
            both = (padded[:blocks] * padded[d:d + blocks]).astype(bf16)
            of_block = jnp.dot(both, member, preferred_element_type=f32)
            count += jnp.sum(jnp.where((block == low) & (far == d), of_block, 0.0), axis=0, keepdims=True)
        scale = jnp.where(far <= R, 1.0 / (total_segs * jnp.maximum(count, 1.0)), 0.0)
        out_ref[...] = jnp.concatenate([label, scale, scale * sign, jnp.zeros((5, lanes), f32)], axis=0)


def pair_weights(here, meta, at, total_segs, pair_lists):
    blocks = meta.shape[0]
    ends = [jnp.asarray(np.repeat(np.array(pairs, np.int32).T, G, axis=1)) for pairs in pair_lists]
    whole = lambda shape: pl.BlockSpec(shape, lambda i, *_: (0, 0))
    shapes = [(8, G * len(pairs)) for pairs in pair_lists]
    return pl.pallas_call(
        functools.partial(weights_kernel, blocks, total_segs),
        grid_spec=pltpu.PrefetchScalarGridSpec(
            num_scalar_prefetch=1,
            grid=(1,),
            in_specs=[pl.BlockSpec((blocks, META, 2 * LANES), lambda i, *_: (0, at // META, 0))]
            + [whole(end.shape) for end in ends],
            out_specs=[whole(shape) for shape in shapes]
            + [pl.BlockSpec((blocks, LANES, LANES), lambda i, *_: (0, 0, 0))],
        ),
        out_shape=[jax.ShapeDtypeStruct(shape, jnp.float32) for shape in shapes]
        + [jax.ShapeDtypeStruct((blocks, LANES, LANES), jnp.bfloat16)],
        compiler_params=pltpu.CompilerParams(vmem_limit_bytes=VMEM_SMALL),
        name="weights",
    )(here, meta, *ends)


def lags_kernel(stacks_ref, zero_ref, two_ref, odd_ref, out_ref):
    f32 = jnp.float32
    copies = stacks_ref.shape[0] // SLICES
    pieces = []
    for piece in range(SLICES):
        total = stacks_ref[piece].astype(f32)
        for copy in range(1, copies):
            total += stacks_ref[copy * SLICES + piece].astype(f32)
        pieces.append(total)

    def product(values, table):
        both = jnp.dot(jnp.concatenate(two_terms(values), axis=0), table, preferred_element_type=f32)
        return both[:BIN_DEV] + both[BIN_DEV:]

    zero = product(jnp.concatenate(pieces[0:2], axis=1), zero_ref[...])
    two = product(jnp.concatenate(pieces[4:6], axis=1), two_ref[...])
    odd = product(jnp.concatenate(pieces[2:4] + pieces[6:8], axis=1), odd_ref[...])
    plus, minus = zero + two, zero - two
    out_ref[:, :LAGQ] = plus + odd[:, :LAGQ]
    out_ref[:, LAGQ:2 * LAGQ] = minus + odd[:, LAGQ:]
    out_ref[:, 2 * LAGQ:3 * LAGQ] = plus - odd[:, :LAGQ]
    out_ref[:, 3 * LAGQ:] = minus - odd[:, LAGQ:]


def lags(stacks):
    tables = [jnp.asarray(table) for table in inverse_tables()]
    return pl.pallas_call(
        lags_kernel,
        out_shape=jax.ShapeDtypeStruct((BIN_DEV, NLAG), jnp.float32),
        compiler_params=pltpu.CompilerParams(vmem_limit_bytes=VMEM_SMALL),
        name="lags",
    )(stacks, *tables)


def fixed_pairs(blocks):
    return [(b, b + d) for b in range(blocks) for d in range(1, R + 1) if b + d < blocks]


def sent_along(x, mask, owners, bins, total_segs):
    seg_count = lax.axis_size("seg")
    count = lax.axis_size("chan")
    early = EARLY_SEGS * LANES
    late = x.shape[0] - early
    spare = LANES - KEPT
    here = lax.axis_index("chan").astype(jnp.int32).reshape(1)
    first, spare_early = spectra(x, mask, owners, bins, 0, early, early, KEPT, with_meta=True)
    first = lax.all_to_all(first, "chan", split_axis=0, concat_axis=0, tiled=True)
    *second, spare_late = spectra(
        x, mask, owners, bins, early, late, LATE_SEGS_A_BLOCK * LANES, KEPT, here=here
    )
    slots = {0: second[0]}
    for shift in SENT:
        slots[shift] = lax.ppermute(second[shift], "chan", [(i, (i + shift) % count) for i in range(count)])

    at = EARLY_SEGS * KEPT
    most = jnp.max(jnp.sum(first[:, at, :LANES].astype(jnp.float32), axis=1))
    rest = lax.cond(
        most > KEPT,
        lambda rows: lax.all_to_all(jnp.concatenate(rows, axis=1), "chan", split_axis=0, concat_axis=0, tiled=True),
        lambda rows: jnp.zeros((count, (early + late) // LANES * spare, 2 * LANES), jnp.bfloat16),
        (spare_early, spare_late),
    )

    fixed = fixed_pairs(count)
    known = (0,) + SENT
    stages = [
        [(i, j) for j in range(start, end) for i in range(j)] for start, end in zip((1,) + STAGES, STAGES)
    ]
    as_slots = lambda pairs: [(-known[i] - count, -known[j] - count) for i, j in pairs]
    weights = pair_weights(here, first, at, total_segs, [fixed] + [as_slots(pairs) for pairs in stages])
    places = weights[-1]
    bins = count * BIN_DEV
    stacks = cross(
        here, fixed, early // G, bins, weights[0], heads=[first], rest=rest, places=places, stacked=True
    )
    ready, start = [], 0
    for end, pairs, weight in zip(STAGES, stages, weights[1:]):
        final = end == len(known)
        result = cross(
            here, pairs, late // G, bins, weight,
            ready=ready, heads=[slots[slot] for slot in known[start:end]], slots=known[start:end],
            rest=rest, rest_row=EARLY_SEGS * spare, places=places, before=stacks,
            copies=seg_count if final else None, hand_on=not final,
        )
        if final:
            return result
        stacks, ready, start = result[0], ready + list(result[1:]), end


def sent_at_once(x, mask, owners, bins, total_segs):
    seg_count = lax.axis_size("seg")
    count = lax.axis_size("chan")
    rows, chans = x.shape[0], mask.shape[1]
    narrow = NB // count
    splits = LANES // narrow
    here = lax.axis_index("chan").astype(jnp.int32).reshape(1)
    own = jnp.concatenate([mask, owners * BIN_DEV + bins], axis=1)
    every = lax.all_gather(own, "chan", axis=0, tiled=True).astype(jnp.bfloat16)
    every = jnp.pad(every, ((0, 0), (0, 2 * LANES - every.shape[1])))
    every = jnp.broadcast_to(every[:, None, :], (count, META, 2 * LANES))
    fixed = fixed_pairs(count)
    weights = pair_weights(here, every, 0, total_segs, [fixed])[:1]
    (outgoing,) = spectra(x, mask, owners, bins, 0, rows, 2 * LANES, LANES)
    outgoing = outgoing.reshape(SLICES, rows, 2, splits, narrow).transpose(0, 3, 1, 2, 4)
    outgoing = outgoing.reshape(count, rows, 2 * narrow)
    wide = lax.all_to_all(outgoing, "chan", split_axis=0, concat_axis=0, tiled=True)
    wide = jnp.pad(wide.reshape(count, rows, 2, narrow), ((0, 0), (0, 0), (0, 0), (0, LANES - narrow)))
    wide = wide.reshape(count, rows, 2 * LANES)
    stacks = cross(
        here, fixed, rows // G, count * BIN_DEV, weights[0], ready=[wide], copies=seg_count, stacked=True
    )
    return stacks.reshape(-1, 2, LANES)[..., :narrow]


def per_device(traces, channel_mask, owner_ids, local_bins):
    seg_count = lax.axis_size("seg")
    count = lax.axis_size("chan")
    segs, chans, length = traces.shape
    x = traces.reshape(segs * chans, length)
    mask = channel_mask.reshape(1, chans)
    owners = owner_ids.reshape(1, -1)
    if count == SLICES:
        stacks = sent_along(x, mask, owners, local_bins, segs * seg_count)
        stacks = stacks.reshape(seg_count * count, BIN_DEV, 2 * LANES)
        stacks = lax.all_to_all(stacks, ("seg", "chan"), split_axis=0, concat_axis=0, tiled=True)
    else:
        narrow = NB // count
        stacks = sent_at_once(x, mask, owners, local_bins, segs * seg_count)
        stacks = stacks.reshape(seg_count * count, BIN_DEV, 2 * narrow)
        stacks = lax.all_to_all(stacks, ("seg", "chan"), split_axis=0, concat_axis=0, tiled=True)
        stacks = stacks.reshape(seg_count, SLICES, count // SLICES, BIN_DEV, 2, narrow)
        stacks = stacks.transpose(0, 1, 3, 4, 2, 5).reshape(seg_count * SLICES, BIN_DEV, 2 * LANES)
    return lags(stacks)


def solution(mesh):
    in_specs = (P("seg", "chan", None), P("chan"), P("chan", None, None), P("chan", None))
    out_specs = P("chan", None)
    return jax.shard_map(
        per_device, mesh=mesh, in_specs=in_specs, out_specs=out_specs, check_vma=False
    )
```

```python
import functools
import math

import jax
import jax.numpy as jnp
import ml_dtypes
import numpy as np
from jax import lax
from jax.experimental import pallas as pl
from jax.experimental.pallas import tpu as pltpu
from jax.sharding import PartitionSpec as P

NT = 4096
DEC = 2
K0 = 8
HW = 64
R = 4
G = 16
BIN_DEV = 8
NB = 1024
NLAG = 2048
EPSILON = 1e-06

LANES = 128
SLICES = NB // LANES
FOLD = 4
CLASS = NB // FOLD
QUARTER = NT // FOLD
LAGQ = NLAG // FOLD
VMEM = 58 * 1024 * 1024
VMEM_SMALL = 20 * 1024 * 1024
META = 16
PAIR = 2 * LANES
TIERS = (104, 8, 16)
KEPT = 2 * TIERS[0]
EARLY_SEGS = 2

SENT = (4, 1, 7, 3, 5, 2, 6)
STAGES = (6, 8)


ORDER = np.arange(NB).reshape(CLASS, FOLD).T.reshape(-1)


def forward_tables():
    samples = np.arange(QUARTER, dtype=np.int64)
    freqs = K0 + ORDER.astype(np.int64)
    phase = samples[:, None] * freqs[None, :] % NT
    angle = (phase.astype(np.float32) * np.float32(2.0 * math.pi / NT)).astype(np.float64)
    cos = np.cos(angle).astype(np.float32).astype(ml_dtypes.bfloat16)
    sin = (-np.sin(angle)).astype(np.float32).astype(ml_dtypes.bfloat16)

    def part(which):
        columns = slice(which * CLASS, (which + 1) * CLASS)
        return [cos[:, columns], sin[:, columns]]

    return np.stack([np.concatenate(part(i) + part(i + 2), axis=1) for i in range(2)])


def band_table():
    near = np.arange(CLASS)
    apart = FOLD * (near[:, None] - near[None, :])
    blocks = [np.abs(apart + shift) <= HW for shift in (0, -1, 1)]
    return np.concatenate(blocks, axis=0).astype(ml_dtypes.bfloat16)


def inverse_tables():
    freqs = K0 + ORDER.astype(np.int64)
    delays = (np.arange(2 * LAGQ, dtype=np.int64) - NLAG // 2) * DEC
    phase = np.mod(freqs[:, None] * delays[None, :], NT)
    angle = phase.astype(np.float64) * (2.0 * math.pi / NT)
    scale = 1.0 / math.sqrt(NB)
    real = (np.cos(angle) * scale).reshape(SLICES, 1, LANES, 2 * LAGQ)
    imag = (-np.sin(angle) * scale).reshape(SLICES, 1, LANES, 2 * LAGQ)
    rows = np.concatenate([real, imag], axis=1).reshape(FOLD, 2 * CLASS, 2 * LAGQ)
    zero = rows[0][:, :LAGQ]
    two = rows[2][:, :LAGQ]
    odd = np.concatenate([rows[1], rows[3]], axis=0)
    return [table.astype(np.float32).astype(ml_dtypes.bfloat16) for table in (zero, two, odd)]


def two_terms(values):
    high = values.astype(jnp.bfloat16)
    low = (values - high.astype(jnp.float32)).astype(jnp.bfloat16)
    return high, low


def two_term_dot(values_ref, table):
    rows = values_ref.shape[0] // 2
    both = jnp.dot(values_ref[...], table, preferred_element_type=jnp.float32)
    return both[:rows] + both[rows:]


def ranks(mask_row):
    shape = (LANES, LANES)
    upto = lax.broadcasted_iota(jnp.int32, shape, 0) <= lax.broadcasted_iota(jnp.int32, shape, 1)
    row = jnp.broadcast_to(mask_row, (META, LANES)).astype(jnp.bfloat16)
    count = jnp.dot(row, upto.astype(jnp.float32).astype(jnp.bfloat16), preferred_element_type=jnp.float32)
    return jnp.where(mask_row > 0, count[0:1] - 1.0, -1.0)


def sorted_rows(mask_row):
    rank = ranks(mask_row)
    rows = []
    for seg in range(2):
        row, below, done = jnp.full_like(rank, -1.0), 0, 0
        for tier in TIERS:
            inside = (rank >= below) & (rank < below + tier)
            row = jnp.where(inside, rank - below + done + seg * tier, row)
            below, done = below + tier, done + 2 * tier
        rows.append(row)
    rows = jnp.concatenate(rows, axis=1)
    return rows == lax.broadcasted_iota(jnp.int32, (PAIR, PAIR), 0).astype(jnp.float32)


def place_order():
    place = lax.broadcasted_iota(jnp.int32, (PAIR, PAIR), 0)
    row = lax.broadcasted_iota(jnp.int32, (PAIR, PAIR), 1)
    inside = place % LANES
    return (place // LANES) * LANES + (inside % G) * (LANES // G) + inside // G == row


def spectra_kernel(relative, with_meta, kept, skip, alone, *refs):
    f32, bf16 = jnp.float32, jnp.bfloat16
    refs = list(refs)
    here_ref = refs.pop(0) if relative else None
    x_any, mask_ref, owner_ref, bins_ref, source_ref, band_any = refs[:6]
    x_refs, table_ref, band_ref, x_came, arrived, u, v, ab, early, others, windows = refs[-11:]
    out_refs = refs[6:-12] if relative else refs[6:-11]
    head = refs[-12] if relative else out_refs[0]
    spares = out_refs[1 - len(TIERS):] if kept < PAIR else []
    step, steps = pl.program_id(0), pl.num_programs(0)
    first = step == 0
    rows = x_refs.shape[1]
    slot = 0 if alone else lax.rem(step, 2)
    at_first = (lambda act: act()) if alone else pl.when(first)
    copies = [
        pltpu.make_async_copy(source_ref.at[part], table_ref.at[part], arrived.at[part]) for part in range(2)
    ] + [pltpu.make_async_copy(band_any, band_ref, arrived.at[2])]

    def trace_copy(block, slot):
        at = pl.ds(pl.multiple_of(block * rows + skip, LANES), rows)
        return pltpu.make_async_copy(x_any.at[at], x_refs.at[slot], x_came.at[slot])

    @at_first
    def start():
        trace_copy(0, 0).start()
        for copy in copies:
            copy.start()

    mask = mask_ref[...].astype(f32)
    if kept < PAIR:
        chosen = sorted_rows(mask)
    else:
        chosen = place_order() & (jnp.concatenate([mask, mask], axis=1) > 0)
    chosen = chosen.astype(f32).astype(bf16)

    trace_copy(step, slot).wait()

    if not alone:

        @pl.when(step + 1 < steps)
        def ahead():
            trace_copy(step + 1, 1 - slot).start()

    @at_first
    def table_waits():
        for copy in copies:
            copy.wait()

    x_ref = x_refs.at[slot]
    x = [x_ref[:, m * QUARTER:(m + 1) * QUARTER].astype(f32) for m in range(FOLD)]
    even, odd = x[0] + x[2], x[1] + x[3]
    u[:rows], u[rows:] = two_terms(even + odd)
    v[:rows], v[rows:] = two_terms(even - odd)
    ab[:rows], ab[rows:2 * rows] = two_terms(x[0] - x[2])
    ab[2 * rows:3 * rows], ab[3 * rows:] = two_terms(x[1] - x[3])

    early[:, :2 * CLASS] = two_term_dot(u, table_ref[0, :, :2 * CLASS])
    early[:, 2 * CLASS:] = two_term_dot(v, table_ref[0, :, 2 * CLASS:])
    turned = jnp.dot(ab[...], table_ref[1], preferred_element_type=f32)
    straight = turned[:rows] + turned[rows:2 * rows]
    turned = turned[2 * rows:3 * rows] + turned[3 * rows:]
    columns = [slice(i * CLASS, (i + 1) * CLASS) for i in range(4)]
    others[:, columns[0]] = straight[:, columns[0]] + turned[:, columns[1]]
    others[:, columns[1]] = straight[:, columns[1]] - turned[:, columns[0]]
    others[:, columns[2]] = straight[:, columns[2]] - turned[:, columns[3]]
    others[:, columns[3]] = straight[:, columns[3]] + turned[:, columns[2]]

    holders = [(early, 0), (others, 0), (early, 2 * CLASS), (others, 2 * CLASS)]
    power = []
    for ref, start in holders:
        real, imag = ref[:, start:start + CLASS], ref[:, start + CLASS:start + 2 * CLASS]
        power.append(real * real + imag * imag)
    before = [jnp.zeros_like(power[0]), power[0], power[0] + power[1], power[0] + power[1] + power[2]]
    after = [power[1] + power[2] + power[3], power[2] + power[3], power[3], jnp.zeros_like(power[0])]
    for which in range(FOLD):
        at = slice(which * rows, (which + 1) * rows)
        windows[at, :CLASS] = power[which].astype(bf16)
        windows[at, CLASS:2 * CLASS] = before[which].astype(bf16)
        windows[at, 2 * CLASS:] = after[which].astype(bf16)
    sums = jnp.dot(windows[...], band_ref[...], preferred_element_type=f32)
    weight = []
    for which in range(FOLD):
        bin_ = lax.broadcasted_iota(jnp.int32, (1, CLASS), 1) * FOLD + which
        within = jnp.minimum(bin_ + HW, NB - 1) - jnp.maximum(bin_ - HW, 0) + 1
        mean = sums[which * rows:(which + 1) * rows] * (1.0 / within.astype(f32))
        weight.append(lax.rsqrt(mean + EPSILON))
    for piece in range(SLICES):
        ref, column = holders[piece // 2]
        column += (piece % 2) * LANES
        scale = weight[piece // 2][:, (piece % 2) * LANES:(piece % 2 + 1) * LANES]
        real = (ref[:, column:column + LANES] * scale).astype(bf16)
        imag = (ref[:, CLASS + column:CLASS + column + LANES] * scale).astype(bf16)
        both = jnp.concatenate([real, imag], axis=1)
        for pair in range(rows // PAIR):
            sorted_ = jnp.dot(chosen, both[pair * PAIR:(pair + 1) * PAIR], preferred_element_type=f32).astype(bf16)
            head[piece, pair * kept:(pair + 1) * kept, :] = sorted_[:kept]
            start = kept
            for spare, tier in zip(spares, TIERS[1:]):
                spare[piece, pair * 2 * tier:(pair + 1) * 2 * tier, :] = sorted_[start:start + 2 * tier]
                start += 2 * tier
    if with_meta:
        tiles = owner_ref.shape[1]
        labels = (owner_ref[...] * BIN_DEV + bins_ref[...]).astype(f32)
        for piece in range(SLICES):
            at = pl.ds(rows // PAIR * kept, META)
            head[piece, at, :] = jnp.zeros((META, 2 * LANES), bf16)
            head[piece, at, :LANES] = jnp.broadcast_to(mask, (META, LANES)).astype(bf16)
            head[piece, at, LANES:LANES + tiles] = jnp.broadcast_to(labels, (META, tiles)).astype(bf16)
    if relative:
        for other in range(SLICES):
            out_refs[other][...] = head[lax.rem(here_ref[0] + other, SLICES)]


def spectra(traces, mask, owners, bins, first_row, rows, block, kept, here=None, with_meta=False):
    relative = here is not None
    table, band = jnp.asarray(forward_tables()), jnp.asarray(band_table())
    whole = lambda array: pl.BlockSpec(array.shape, lambda i, *_: (0, 0))
    in_place = pl.BlockSpec(memory_space=pl.ANY)
    f32, bf16 = jnp.float32, jnp.bfloat16
    pairs = block // PAIR
    scratch = [
        pltpu.VMEM((2, block, NT), bf16),
        pltpu.VMEM(table.shape, bf16),
        pltpu.VMEM(band.shape, bf16),
        pltpu.SemaphoreType.DMA((2,)),
        pltpu.SemaphoreType.DMA((3,)),
    ]
    scratch += [pltpu.VMEM((terms * block, QUARTER), bf16) for terms in (2, 2, 4)]
    scratch += [pltpu.VMEM((block, 4 * CLASS), f32)] * 2
    scratch += [pltpu.VMEM((FOLD * block, 3 * CLASS), bf16)]
    if relative:
        scratch = [pltpu.VMEM((SLICES, pairs * kept, 2 * LANES), bf16)] + scratch
        out_specs = [pl.BlockSpec((pairs * kept, 2 * LANES), lambda i, *_: (i, 0))] * SLICES
        out_shape = [jax.ShapeDtypeStruct((rows // PAIR * kept, 2 * LANES), bf16)] * SLICES
    else:
        extra = META if with_meta else 0
        out_specs = [pl.BlockSpec((SLICES, pairs * kept + extra, 2 * LANES), lambda i, *_: (0, i, 0))]
        out_shape = [jax.ShapeDtypeStruct((SLICES, rows // PAIR * kept + extra, 2 * LANES), bf16)]
    for tier in TIERS[1:] if kept < PAIR else ():
        out_specs.append(pl.BlockSpec((SLICES, pairs * 2 * tier, 2 * LANES), lambda i, *_: (0, i, 0)))
        out_shape.append(jax.ShapeDtypeStruct((SLICES, rows // LANES * tier, 2 * LANES), bf16))
    return pl.pallas_call(
        functools.partial(spectra_kernel, relative, with_meta, kept, first_row, rows == block),
        grid_spec=pltpu.PrefetchScalarGridSpec(
            num_scalar_prefetch=1 if relative else 0,
            grid=(rows // block,),
            in_specs=[in_place, whole(mask), whole(owners), whole(bins), in_place, in_place],
            out_specs=out_specs,
            scratch_shapes=scratch,
        ),
        out_shape=out_shape,
        compiler_params=pltpu.CompilerParams(vmem_limit_bytes=VMEM),
        cost_estimate=pl.CostEstimate(
            flops=14 * rows * NB * NB, bytes_accessed=rows * NT * 3 + 8 * NB * NB, transcendentals=rows * NB
        ),
        name="spectra",
    )(*([here] if relative else []), traces, mask, owners, bins, table, band)


def pair_sums(block_refs, pairs, steps, tiles):
    f32 = jnp.float32
    done = 0
    groups, current = [], []
    for pair in pairs:
        members = {m for p in current + [pair] for m in p}
        if current and 4 * (len(current) + 1) + 4 * len(members) > 60:
            groups.append(current)
            current = []
        current = current + [pair]
    groups.append(current)
    for group in groups:
        needed = sorted({m for pair in group for m in pair})

        def body(step, sums):
            at = pl.ds(pl.multiple_of(step * G, G), G)
            real = {m: block_refs[m][at, :LANES].astype(f32) for m in needed}
            imag = {m: block_refs[m][at, LANES:].astype(f32) for m in needed}
            new = []
            for (p, q), (re, im) in zip(group, sums):
                re = re + (real[p] * real[q] + imag[p] * imag[q])
                im = im + (imag[p] * real[q] - real[p] * imag[q])
                new.append((re, im))
            return tuple(new)

        zero = jnp.zeros((G, LANES), f32)
        sums = lax.fori_loop(0, steps, body, tuple((zero, zero) for _ in group), unroll=2)
        for re, im in sums:
            tiles[done:done + G, :LANES] = re
            tiles[done:done + G, LANES:] = im
            done += G


def place_rows(head_ref, spare_refs, first_pair, places, out_ref):
    for pair in range(out_ref.shape[0] // PAIR):
        rows = [head_ref[pair * KEPT:(pair + 1) * KEPT]]
        for spare_ref, tier in zip(spare_refs, TIERS[1:]):
            at = (first_pair + pair) * 2 * tier
            rows.append(spare_ref[at:at + 2 * tier])
        placed = jnp.dot(places, jnp.concatenate(rows, axis=0), preferred_element_type=jnp.float32)
        out_ref[pair * PAIR:(pair + 1) * PAIR, :] = placed.astype(out_ref.dtype)


def cross_kernel(plan, here_ref, *refs):
    f32 = jnp.float32
    refs = list(refs)
    take = lambda count: [refs.pop(0) for _ in range(count)]
    ready, heads = take(plan["ready"]), take(plan["heads"])
    *spare_refs, places_ref = take(len(TIERS)) if heads else [None]
    (rows_ref,) = take(1)
    before_ref = refs.pop(0) if plan["before"] else None
    out_ref = refs.pop(0)
    placed = take(len(plan["slots"])) if plan["hand_on"] else None
    tiles = refs.pop(0)
    if plan["stacked"]:
        source = heads[0] if heads else ready[0]
        count = source.shape[0]
        heads = [source.at[m] for m in range(count)] if heads else []
        ready = [] if heads else [source.at[m] for m in range(count)]
    if heads:
        if placed is None:
            (room,) = refs
            placed = [room.at[i] for i in range(len(heads))]
        for i, head in enumerate(heads):
            block = i if plan["stacked"] else lax.rem(here_ref[0] - plan["slots"][i] + SLICES, SLICES)
            spares = [spare_ref.at[block] for spare_ref in spare_refs]
            place_rows(head, spares, plan["first_pair"], places_ref[block], placed[i])
        ready = ready + placed
    pair_sums(ready, plan["pairs"], plan["steps"], tiles)
    bins, count = out_ref.shape[-2], tiles.shape[0]
    wanted = rows_ref[0:1, :] == lax.broadcasted_iota(jnp.int32, (bins, count), 0).astype(f32)
    high, low = two_terms(tiles[...])
    stacked = []
    for half in range(2):
        weights = jnp.where(wanted, jnp.broadcast_to(rows_ref[half + 1:half + 2, :], (bins, count)), 0.0)
        weights = jnp.concatenate(two_terms(weights), axis=0)
        at = slice(half * LANES, (half + 1) * LANES)
        both = jnp.dot(weights, high[:, at], preferred_element_type=f32)
        both = both[:bins] + both[bins:]
        stacked.append(both + jnp.dot(weights[:bins], low[:, at], preferred_element_type=f32))
    stacked = jnp.concatenate(stacked, axis=1)
    if before_ref is not None:
        stacked += before_ref[...]
    if len(out_ref.shape) == 2:
        out_ref[...] = stacked
    else:
        for copy in range(out_ref.shape[0]):
            out_ref[copy] = stacked.astype(out_ref.dtype)


def cross(here, pairs, steps, bins, weights, ready=(), heads=(), slots=(), spares=(), first_pair=0, places=None,
          before=None, copies=None, hand_on=False, stacked=False):
    shape = (bins, 2 * LANES)
    inputs = list(ready) + list(heads) + (list(spares) + [places] if heads else []) + [weights]
    if before is not None:
        inputs.append(before)
    if copies is None:
        out_shape = [jax.ShapeDtypeStruct(shape, jnp.float32)]
    else:
        out_shape = [jax.ShapeDtypeStruct((copies,) + shape, jnp.bfloat16)]
    scratch = [pltpu.VMEM((len(pairs) * G, 2 * LANES), jnp.float32)]
    if hand_on:
        out_shape += [jax.ShapeDtypeStruct((G * steps, 2 * LANES), jnp.bfloat16)] * len(heads)
    elif heads:
        count = heads[0].shape[0] if stacked else len(heads)
        scratch.append(pltpu.VMEM((count, G * steps, 2 * LANES), jnp.bfloat16))
    plan = dict(
        ready=len(ready), heads=len(heads), slots=slots, before=before is not None, hand_on=hand_on,
        stacked=stacked, first_pair=first_pair, pairs=pairs, steps=steps,
    )
    result = pl.pallas_call(
        functools.partial(cross_kernel, plan),
        in_specs=[pl.BlockSpec(memory_space=pltpu.SMEM)] + [pl.BlockSpec(memory_space=pltpu.VMEM)] * len(inputs),
        out_shape=out_shape,
        scratch_shapes=scratch,
        compiler_params=pltpu.CompilerParams(vmem_limit_bytes=VMEM if stacked and copies else VMEM_SMALL),
        cost_estimate=pl.CostEstimate(
            flops=8 * G * steps * LANES * len(pairs), bytes_accessed=4 * G * steps * LANES * len(pairs), transcendentals=0
        ),
        name="cross",
    )(here, *inputs)
    return result if hand_on else result[0]


def weights_kernel(blocks, total_segs, here_ref, meta_ref, *refs):
    f32, bf16 = jnp.float32, jnp.bfloat16
    meta = jnp.concatenate([meta_ref[b, 0:1, :] for b in range(blocks)], axis=0)
    masks, labels = meta[:, :LANES], meta[:, LANES:]
    empty = jnp.zeros((R, LANES), bf16)
    padded = jnp.concatenate([masks.astype(f32), empty.astype(f32)], axis=0)
    half = len(refs) // 2
    places_ref = refs[-1]
    in_place = place_order().astype(f32).astype(bf16)
    for b in range(blocks):
        rows = sorted_rows(masks[b:b + 1].astype(f32)).astype(f32).astype(bf16)
        places = lax.dot_general(in_place, rows, (((1,), (1,)), ((), ())), preferred_element_type=f32)
        places_ref[b] = places.astype(bf16)
    for ends_ref, out_ref in zip(refs[:half], refs[half:-1]):
        lanes = out_ref.shape[1]
        first, second = ends_ref[0:1, :], ends_ref[1:2, :]
        slots = first < 0
        held = [jnp.where(slots, lax.rem(here_ref[0] + end + 2 * blocks, blocks), end) for end in (first, second)]
        low, far = jnp.minimum(held[0], held[1]), jnp.abs(held[0] - held[1])
        sign = jnp.where(held[0] < held[1], 1.0, -1.0)
        block = lax.broadcasted_iota(jnp.int32, (blocks, lanes), 0)
        group = lax.broadcasted_iota(jnp.int32, (LANES, lanes), 1) % G
        place = lax.broadcasted_iota(jnp.int32, (LANES, lanes), 0)
        chosen = (place == (far - 1) * G + group).astype(f32).astype(bf16)
        label = jnp.dot(labels, chosen, preferred_element_type=f32)
        label = jnp.sum(jnp.where(block == low, label, 0.0), axis=0, keepdims=True)
        member = (place // (LANES // G) == group).astype(f32).astype(bf16)
        count = jnp.zeros((1, lanes), f32)
        for d in range(1, R + 1):
            both = (padded[:blocks] * padded[d:d + blocks]).astype(bf16)
            of_block = jnp.dot(both, member, preferred_element_type=f32)
            count += jnp.sum(jnp.where((block == low) & (far == d), of_block, 0.0), axis=0, keepdims=True)
        scale = jnp.where(far <= R, 1.0 / (total_segs * jnp.maximum(count, 1.0)), 0.0)
        out_ref[...] = jnp.concatenate([label, scale, scale * sign, jnp.zeros((5, lanes), f32)], axis=0)


def pair_weights(here, meta, at, total_segs, pair_lists):
    blocks = meta.shape[0]
    ends = [jnp.asarray(np.repeat(np.array(pairs, np.int32).T, G, axis=1)) for pairs in pair_lists]
    whole = lambda shape: pl.BlockSpec(shape, lambda i, *_: (0, 0))
    shapes = [(8, G * len(pairs)) for pairs in pair_lists]
    return pl.pallas_call(
        functools.partial(weights_kernel, blocks, total_segs),
        grid_spec=pltpu.PrefetchScalarGridSpec(
            num_scalar_prefetch=1,
            grid=(1,),
            in_specs=[pl.BlockSpec((blocks, META, 2 * LANES), lambda i, *_: (0, at // META, 0))]
            + [whole(end.shape) for end in ends],
            out_specs=[whole(shape) for shape in shapes]
            + [pl.BlockSpec((blocks, PAIR, PAIR), lambda i, *_: (0, 0, 0))],
        ),
        out_shape=[jax.ShapeDtypeStruct(shape, jnp.float32) for shape in shapes]
        + [jax.ShapeDtypeStruct((blocks, PAIR, PAIR), jnp.bfloat16)],
        compiler_params=pltpu.CompilerParams(vmem_limit_bytes=VMEM_SMALL),
        name="weights",
    )(here, meta, *ends)


def lags_kernel(stacks_ref, zero_ref, two_ref, odd_ref, out_ref):
    f32 = jnp.float32
    copies = stacks_ref.shape[0] // SLICES
    pieces = []
    for piece in range(SLICES):
        total = stacks_ref[piece].astype(f32)
        for copy in range(1, copies):
            total += stacks_ref[copy * SLICES + piece].astype(f32)
        pieces.append(total)

    def product(values, table):
        both = jnp.dot(jnp.concatenate(two_terms(values), axis=0), table, preferred_element_type=f32)
        return both[:BIN_DEV] + both[BIN_DEV:]

    zero = product(jnp.concatenate(pieces[0:2], axis=1), zero_ref[...])
    two = product(jnp.concatenate(pieces[4:6], axis=1), two_ref[...])
    odd = product(jnp.concatenate(pieces[2:4] + pieces[6:8], axis=1), odd_ref[...])
    plus, minus = zero + two, zero - two
    out_ref[:, :LAGQ] = plus + odd[:, :LAGQ]
    out_ref[:, LAGQ:2 * LAGQ] = minus + odd[:, LAGQ:]
    out_ref[:, 2 * LAGQ:3 * LAGQ] = plus - odd[:, :LAGQ]
    out_ref[:, 3 * LAGQ:] = minus - odd[:, LAGQ:]


def lags(stacks):
    tables = [jnp.asarray(table) for table in inverse_tables()]
    return pl.pallas_call(
        lags_kernel,
        out_shape=jax.ShapeDtypeStruct((BIN_DEV, NLAG), jnp.float32),
        compiler_params=pltpu.CompilerParams(vmem_limit_bytes=VMEM_SMALL),
        name="lags",
    )(stacks, *tables)


def fixed_pairs(blocks):
    return [(b, b + d) for b in range(blocks) for d in range(1, R + 1) if b + d < blocks]


def sent_along(x, mask, owners, bins, total_segs):
    seg_count = lax.axis_size("seg")
    count = lax.axis_size("chan")
    early = EARLY_SEGS * LANES
    late = x.shape[0] - early
    here = lax.axis_index("chan").astype(jnp.int32).reshape(1)
    first, *spare_early = spectra(x, mask, owners, bins, 0, early, early, KEPT, with_meta=True)
    first = lax.all_to_all(first, "chan", split_axis=0, concat_axis=0, tiled=True)
    second = spectra(x, mask, owners, bins, early, late, PAIR, KEPT, here=here)
    spare_late = second[SLICES:]
    slots = {0: second[0]}
    for shift in SENT:
        slots[shift] = lax.ppermute(second[shift], "chan", [(i, (i + shift) % count) for i in range(count)])

    at = early // PAIR * KEPT
    most = jnp.max(jnp.sum(first[:, at, :LANES].astype(jnp.float32), axis=1))
    spares, below = [], TIERS[0]
    for tier, *parts in zip(TIERS[1:], spare_early, spare_late):
        spares.append(lax.cond(
            most > below,
            lambda parts: lax.all_to_all(jnp.concatenate(parts, axis=1), "chan", split_axis=0, concat_axis=0, tiled=True),
            lambda parts: jnp.zeros((count, sum(part.shape[1] for part in parts), 2 * LANES), jnp.bfloat16),
            parts,
        ))
        below += tier

    fixed = fixed_pairs(count)
    known = (0,) + SENT
    stages = [
        [(i, j) for j in range(start, end) for i in range(j)] for start, end in zip((1,) + STAGES, STAGES)
    ]
    as_slots = lambda pairs: [(-known[i] - count, -known[j] - count) for i, j in pairs]
    weights = pair_weights(here, first, at, total_segs, [fixed] + [as_slots(pairs) for pairs in stages])
    places = weights[-1]
    bins = count * BIN_DEV
    stacks = cross(
        here, fixed, early // G, bins, weights[0], heads=[first], spares=spares, places=places, stacked=True
    )
    ready, start = [], 0
    for end, pairs, weight in zip(STAGES, stages, weights[1:]):
        final = end == len(known)
        result = cross(
            here, pairs, late // G, bins, weight,
            ready=ready, heads=[slots[slot] for slot in known[start:end]], slots=known[start:end],
            spares=spares, first_pair=early // PAIR, places=places, before=stacks,
            copies=seg_count if final else None, hand_on=not final,
        )
        if final:
            return result
        stacks, ready, start = result[0], ready + list(result[1:]), end


def sent_at_once(x, mask, owners, bins, total_segs):
    seg_count = lax.axis_size("seg")
    count = lax.axis_size("chan")
    rows, chans = x.shape[0], mask.shape[1]
    narrow = NB // count
    splits = LANES // narrow
    here = lax.axis_index("chan").astype(jnp.int32).reshape(1)
    own = jnp.concatenate([mask, owners * BIN_DEV + bins], axis=1)
    every = lax.all_gather(own, "chan", axis=0, tiled=True).astype(jnp.bfloat16)
    every = jnp.pad(every, ((0, 0), (0, 2 * LANES - every.shape[1])))
    every = jnp.broadcast_to(every[:, None, :], (count, META, 2 * LANES))
    fixed = fixed_pairs(count)
    weights = pair_weights(here, every, 0, total_segs, [fixed])[:1]
    (outgoing,) = spectra(x, mask, owners, bins, 0, rows, PAIR, PAIR)
    outgoing = outgoing.reshape(SLICES, rows, 2, splits, narrow).transpose(0, 3, 1, 2, 4)
    outgoing = outgoing.reshape(count, rows, 2 * narrow)
    wide = lax.all_to_all(outgoing, "chan", split_axis=0, concat_axis=0, tiled=True)
    wide = jnp.pad(wide.reshape(count, rows, 2, narrow), ((0, 0), (0, 0), (0, 0), (0, LANES - narrow)))
    wide = wide.reshape(count, rows, 2 * LANES)
    stacks = cross(
        here, fixed, rows // G, count * BIN_DEV, weights[0], ready=[wide], copies=seg_count, stacked=True
    )
    return stacks.reshape(-1, 2, LANES)[..., :narrow]


def per_device(traces, channel_mask, owner_ids, local_bins):
    seg_count = lax.axis_size("seg")
    count = lax.axis_size("chan")
    segs, chans, length = traces.shape
    x = traces.reshape(segs * chans, length)
    mask = channel_mask.reshape(1, chans)
    owners = owner_ids.reshape(1, -1)
    if count == SLICES:
        stacks = sent_along(x, mask, owners, local_bins, segs * seg_count)
        stacks = stacks.reshape(seg_count * count, BIN_DEV, 2 * LANES)
        stacks = lax.all_to_all(stacks, ("seg", "chan"), split_axis=0, concat_axis=0, tiled=True)
    else:
        narrow = NB // count
        stacks = sent_at_once(x, mask, owners, local_bins, segs * seg_count)
        stacks = stacks.reshape(seg_count * count, BIN_DEV, 2 * narrow)
        stacks = lax.all_to_all(stacks, ("seg", "chan"), split_axis=0, concat_axis=0, tiled=True)
        stacks = stacks.reshape(seg_count, SLICES, count // SLICES, BIN_DEV, 2, narrow)
        stacks = stacks.transpose(0, 1, 3, 4, 2, 5).reshape(seg_count * SLICES, BIN_DEV, 2 * LANES)
    return lags(stacks)


def solution(mesh):
    in_specs = (P("seg", "chan", None), P("chan"), P("chan", None, None), P("chan", None))
    out_specs = P("chan", None)
    return jax.shard_map(
        per_device, mesh=mesh, in_specs=in_specs, out_specs=out_specs, check_vma=False
    )
```

```python
import functools
import math

import jax
import jax.numpy as jnp
import ml_dtypes
import numpy as np
from jax import lax
from jax.experimental import pallas as pl
from jax.experimental.pallas import tpu as pltpu
from jax.sharding import PartitionSpec as P

NT = 4096
DEC = 2
K0 = 8
HW = 64
R = 4
G = 16
BIN_DEV = 8
NB = 1024
NLAG = 2048
EPSILON = 1e-06

LANES = 128
SLICES = NB // LANES
FOLD = 4
CLASS = NB // FOLD
QUARTER = NT // FOLD
LAGQ = NLAG // FOLD
VMEM = 58 * 1024 * 1024
VMEM_SMALL = 20 * 1024 * 1024
META = 16
PAIR = 2 * LANES
TIERS = (104, 8, 16)
KEPT = 2 * TIERS[0]
EARLY_SEGS = 2

SENT = (4, 1, 7, 3, 5, 2, 6)
STAGES = (6, 8)


ORDER = np.arange(NB).reshape(CLASS, FOLD).T.reshape(-1)


def forward_tables():
    samples = np.arange(QUARTER, dtype=np.int64)
    freqs = K0 + ORDER.astype(np.int64)
    phase = samples[:, None] * freqs[None, :] % NT
    angle = (phase.astype(np.float32) * np.float32(2.0 * math.pi / NT)).astype(np.float64)
    cos = np.cos(angle).astype(np.float32).astype(ml_dtypes.bfloat16)
    sin = (-np.sin(angle)).astype(np.float32).astype(ml_dtypes.bfloat16)

    def part(which):
        columns = slice(which * CLASS, (which + 1) * CLASS)
        return [cos[:, columns], sin[:, columns]]

    return np.stack([np.concatenate(part(i) + part(i + 2), axis=1) for i in range(2)])


def band_table():
    near = np.arange(CLASS)
    apart = FOLD * (near[:, None] - near[None, :])
    blocks = [np.abs(apart + shift) <= HW for shift in (0, -1, 1)]
    return np.concatenate(blocks, axis=0).astype(ml_dtypes.bfloat16)


def inverse_tables():
    freqs = K0 + ORDER.astype(np.int64)
    delays = (np.arange(2 * LAGQ, dtype=np.int64) - NLAG // 2) * DEC
    phase = np.mod(freqs[:, None] * delays[None, :], NT)
    angle = phase.astype(np.float64) * (2.0 * math.pi / NT)
    scale = 1.0 / math.sqrt(NB)
    real = (np.cos(angle) * scale).reshape(SLICES, 1, LANES, 2 * LAGQ)
    imag = (-np.sin(angle) * scale).reshape(SLICES, 1, LANES, 2 * LAGQ)
    rows = np.concatenate([real, imag], axis=1).reshape(FOLD, 2 * CLASS, 2 * LAGQ)
    zero = rows[0][:, :LAGQ]
    two = rows[2][:, :LAGQ]
    odd = np.concatenate([rows[1], rows[3]], axis=0)
    return [table.astype(np.float32).astype(ml_dtypes.bfloat16) for table in (zero, two, odd)]


def two_terms(values):
    high = values.astype(jnp.bfloat16)
    low = (values - high.astype(jnp.float32)).astype(jnp.bfloat16)
    return high, low


def two_term_dot(values_ref, table):
    rows = values_ref.shape[0] // 2
    both = jnp.dot(values_ref[...], table, preferred_element_type=jnp.float32)
    return both[:rows] + both[rows:]


def ranks(mask_row):
    shape = (LANES, LANES)
    upto = lax.broadcasted_iota(jnp.int32, shape, 0) <= lax.broadcasted_iota(jnp.int32, shape, 1)
    row = jnp.broadcast_to(mask_row, (META, LANES)).astype(jnp.bfloat16)
    count = jnp.dot(row, upto.astype(jnp.float32).astype(jnp.bfloat16), preferred_element_type=jnp.float32)
    return jnp.where(mask_row > 0, count[0:1] - 1.0, -1.0)


def sorted_rows(mask_row):
    rank = ranks(mask_row)
    rows = []
    for seg in range(2):
        row, below, done = jnp.full_like(rank, -1.0), 0, 0
        for tier in TIERS:
            inside = (rank >= below) & (rank < below + tier)
            row = jnp.where(inside, rank - below + done + seg * tier, row)
            below, done = below + tier, done + 2 * tier
        rows.append(row)
    rows = jnp.concatenate(rows, axis=1)
    return rows == lax.broadcasted_iota(jnp.int32, (PAIR, PAIR), 0).astype(jnp.float32)


def place_order():
    place = lax.broadcasted_iota(jnp.int32, (PAIR, PAIR), 0)
    row = lax.broadcasted_iota(jnp.int32, (PAIR, PAIR), 1)
    inside = place % LANES
    return (place // LANES) * LANES + (inside % G) * (LANES // G) + inside // G == row


def spectra_kernel(relative, with_meta, kept, skip, alone, *refs):
    f32, bf16 = jnp.float32, jnp.bfloat16
    refs = list(refs)
    here_ref = refs.pop(0) if relative else None
    x_any, mask_ref, owner_ref, bins_ref, source_ref, band_any = refs[:6]
    x_refs, table_ref, band_ref, x_came, arrived, u, v, ab, early, others, windows = refs[-11:]
    out_refs = refs[6:-12] if relative else refs[6:-11]
    head = refs[-12] if relative else out_refs[0]
    spares = out_refs[1 - len(TIERS):] if kept < PAIR else []
    step, steps = pl.program_id(0), pl.num_programs(0)
    first = step == 0
    rows = x_refs.shape[1]
    slot = 0 if alone else lax.rem(step, 2)
    at_first = (lambda act: act()) if alone else pl.when(first)
    copies = [
        pltpu.make_async_copy(source_ref.at[part], table_ref.at[part], arrived.at[part]) for part in range(2)
    ] + [pltpu.make_async_copy(band_any, band_ref, arrived.at[2])]

    def trace_copy(block, slot):
        at = pl.ds(pl.multiple_of(block * rows + skip, LANES), rows)
        return pltpu.make_async_copy(x_any.at[at], x_refs.at[slot], x_came.at[slot])

    @at_first
    def start():
        trace_copy(0, 0).start()
        for copy in copies:
            copy.start()

    mask = mask_ref[...].astype(f32)
    if kept < PAIR:
        chosen = sorted_rows(mask)
    else:
        chosen = place_order() & (jnp.concatenate([mask, mask], axis=1) > 0)
    chosen = chosen.astype(f32).astype(bf16)

    trace_copy(step, slot).wait()

    if not alone:

        @pl.when(step + 1 < steps)
        def ahead():
            trace_copy(step + 1, 1 - slot).start()

    @at_first
    def table_waits():
        for copy in copies:
            copy.wait()

    x_ref = x_refs.at[slot]
    x = [x_ref[:, m * QUARTER:(m + 1) * QUARTER].astype(f32) for m in range(FOLD)]
    even, odd = x[0] + x[2], x[1] + x[3]
    u[:rows], u[rows:] = two_terms(even + odd)
    v[:rows], v[rows:] = two_terms(even - odd)
    ab[:rows], ab[rows:2 * rows] = two_terms(x[0] - x[2])
    ab[2 * rows:3 * rows], ab[3 * rows:] = two_terms(x[1] - x[3])

    early[:, :2 * CLASS] = two_term_dot(u, table_ref[0, :, :2 * CLASS])
    early[:, 2 * CLASS:] = two_term_dot(v, table_ref[0, :, 2 * CLASS:])
    turned = jnp.dot(ab[...], table_ref[1], preferred_element_type=f32)
    straight = turned[:rows] + turned[rows:2 * rows]
    turned = turned[2 * rows:3 * rows] + turned[3 * rows:]
    columns = [slice(i * CLASS, (i + 1) * CLASS) for i in range(4)]
    others[:, columns[0]] = straight[:, columns[0]] + turned[:, columns[1]]
    others[:, columns[1]] = straight[:, columns[1]] - turned[:, columns[0]]
    others[:, columns[2]] = straight[:, columns[2]] - turned[:, columns[3]]
    others[:, columns[3]] = straight[:, columns[3]] + turned[:, columns[2]]

    holders = [(early, 0), (others, 0), (early, 2 * CLASS), (others, 2 * CLASS)]
    power = []
    for ref, start in holders:
        real, imag = ref[:, start:start + CLASS], ref[:, start + CLASS:start + 2 * CLASS]
        power.append(real * real + imag * imag)
    before = [jnp.zeros_like(power[0]), power[0], power[0] + power[1], power[0] + power[1] + power[2]]
    after = [power[1] + power[2] + power[3], power[2] + power[3], power[3], jnp.zeros_like(power[0])]
    for which in range(FOLD):
        at = slice(which * rows, (which + 1) * rows)
        windows[at, :CLASS] = power[which].astype(bf16)
        windows[at, CLASS:2 * CLASS] = before[which].astype(bf16)
        windows[at, 2 * CLASS:] = after[which].astype(bf16)
    sums = jnp.dot(windows[...], band_ref[...], preferred_element_type=f32)
    weight = []
    for which in range(FOLD):
        bin_ = lax.broadcasted_iota(jnp.int32, (1, CLASS), 1) * FOLD + which
        within = jnp.minimum(bin_ + HW, NB - 1) - jnp.maximum(bin_ - HW, 0) + 1
        mean = sums[which * rows:(which + 1) * rows] * (1.0 / within.astype(f32))
        weight.append(lax.rsqrt(mean + EPSILON))
    for piece in range(SLICES):
        ref, column = holders[piece // 2]
        column += (piece % 2) * LANES
        scale = weight[piece // 2][:, (piece % 2) * LANES:(piece % 2 + 1) * LANES]
        real = (ref[:, column:column + LANES] * scale).astype(bf16)
        imag = (ref[:, CLASS + column:CLASS + column + LANES] * scale).astype(bf16)
        both = jnp.concatenate([real, imag], axis=1)
        for pair in range(rows // PAIR):
            sorted_ = jnp.dot(chosen, both[pair * PAIR:(pair + 1) * PAIR], preferred_element_type=f32).astype(bf16)
            head[piece, pair * kept:(pair + 1) * kept, :] = sorted_[:kept]
            start = kept
            for spare, tier in zip(spares, TIERS[1:]):
                spare[piece, pair * 2 * tier:(pair + 1) * 2 * tier, :] = sorted_[start:start + 2 * tier]
                start += 2 * tier
    if with_meta:
        tiles = owner_ref.shape[1]
        labels = (owner_ref[...] * BIN_DEV + bins_ref[...]).astype(f32)
        for piece in range(SLICES):
            at = pl.ds(rows // PAIR * kept, META)
            head[piece, at, :] = jnp.zeros((META, 2 * LANES), bf16)
            head[piece, at, :LANES] = jnp.broadcast_to(mask, (META, LANES)).astype(bf16)
            head[piece, at, LANES:LANES + tiles] = jnp.broadcast_to(labels, (META, tiles)).astype(bf16)
    if relative:
        for other in range(SLICES):
            out_refs[other][...] = head[lax.rem(here_ref[0] + other, SLICES)]


def spectra(traces, mask, owners, bins, first_row, rows, block, kept, here=None, with_meta=False):
    relative = here is not None
    table, band = jnp.asarray(forward_tables()), jnp.asarray(band_table())
    whole = lambda array: pl.BlockSpec(array.shape, lambda i, *_: (0, 0))
    in_place = pl.BlockSpec(memory_space=pl.ANY)
    f32, bf16 = jnp.float32, jnp.bfloat16
    pairs = block // PAIR
    scratch = [
        pltpu.VMEM((2, block, NT), bf16),
        pltpu.VMEM(table.shape, bf16),
        pltpu.VMEM(band.shape, bf16),
        pltpu.SemaphoreType.DMA((2,)),
        pltpu.SemaphoreType.DMA((3,)),
    ]
    scratch += [pltpu.VMEM((terms * block, QUARTER), bf16) for terms in (2, 2, 4)]
    scratch += [pltpu.VMEM((block, 4 * CLASS), f32)] * 2
    scratch += [pltpu.VMEM((FOLD * block, 3 * CLASS), bf16)]
    if relative:
        scratch = [pltpu.VMEM((SLICES, pairs * kept, 2 * LANES), bf16)] + scratch
        out_specs = [pl.BlockSpec((pairs * kept, 2 * LANES), lambda i, *_: (i, 0))] * SLICES
        out_shape = [jax.ShapeDtypeStruct((rows // PAIR * kept, 2 * LANES), bf16)] * SLICES
    else:
        extra = META if with_meta else 0
        out_specs = [pl.BlockSpec((SLICES, pairs * kept + extra, 2 * LANES), lambda i, *_: (0, i, 0))]
        out_shape = [jax.ShapeDtypeStruct((SLICES, rows // PAIR * kept + extra, 2 * LANES), bf16)]
    for tier in TIERS[1:] if kept < PAIR else ():
        out_specs.append(pl.BlockSpec((SLICES, pairs * 2 * tier, 2 * LANES), lambda i, *_: (0, i, 0)))
        out_shape.append(jax.ShapeDtypeStruct((SLICES, rows // LANES * tier, 2 * LANES), bf16))
    return pl.pallas_call(
        functools.partial(spectra_kernel, relative, with_meta, kept, first_row, rows == block),
        grid_spec=pltpu.PrefetchScalarGridSpec(
            num_scalar_prefetch=1 if relative else 0,
            grid=(rows // block,),
            in_specs=[in_place, whole(mask), whole(owners), whole(bins), in_place, in_place],
            out_specs=out_specs,
            scratch_shapes=scratch,
        ),
        out_shape=out_shape,
        compiler_params=pltpu.CompilerParams(vmem_limit_bytes=VMEM),
        cost_estimate=pl.CostEstimate(
            flops=14 * rows * NB * NB, bytes_accessed=rows * NT * 3 + 8 * NB * NB, transcendentals=rows * NB
        ),
        name="spectra",
    )(*([here] if relative else []), traces, mask, owners, bins, table, band)


def pair_sums(block_refs, pairs, steps, tiles):
    f32 = jnp.float32
    done = 0
    groups, current = [], []
    for pair in pairs:
        members = {m for p in current + [pair] for m in p}
        if current and 4 * (len(current) + 1) + 4 * len(members) > 60:
            groups.append(current)
            current = []
        current = current + [pair]
    groups.append(current)
    for group in groups:
        needed = sorted({m for pair in group for m in pair})

        def body(step, sums):
            at = pl.ds(pl.multiple_of(step * G, G), G)
            real = {m: block_refs[m][at, :LANES].astype(f32) for m in needed}
            imag = {m: block_refs[m][at, LANES:].astype(f32) for m in needed}
            new = []
            for (p, q), (re, im) in zip(group, sums):
                re = re + (real[p] * real[q] + imag[p] * imag[q])
                im = im + (imag[p] * real[q] - real[p] * imag[q])
                new.append((re, im))
            return tuple(new)

        zero = jnp.zeros((G, LANES), f32)
        sums = lax.fori_loop(0, steps, body, tuple((zero, zero) for _ in group), unroll=2)
        for re, im in sums:
            tiles[done:done + G, :LANES] = re
            tiles[done:done + G, LANES:] = im
            done += G


def place_rows(head_ref, spare_refs, first_pair, places, out_ref):
    for pair in range(out_ref.shape[0] // PAIR):
        rows = [head_ref[pair * KEPT:(pair + 1) * KEPT]]
        for spare_ref, tier in zip(spare_refs, TIERS[1:]):
            at = (first_pair + pair) * 2 * tier
            rows.append(spare_ref[at:at + 2 * tier])
        placed = jnp.dot(places, jnp.concatenate(rows, axis=0), preferred_element_type=jnp.float32)
        out_ref[pair * PAIR:(pair + 1) * PAIR, :] = placed.astype(out_ref.dtype)


def cross_kernel(plan, here_ref, *refs):
    f32 = jnp.float32
    refs = list(refs)
    take = lambda count: [refs.pop(0) for _ in range(count)]
    ready, heads = take(plan["ready"]), take(plan["heads"])
    *spare_refs, places_ref = take(len(TIERS)) if heads else [None]
    (rows_ref,) = take(1)
    before_ref = refs.pop(0) if plan["before"] else None
    out_ref = refs.pop(0)
    placed = take(len(plan["slots"])) if plan["hand_on"] else None
    tiles = refs.pop(0)
    if plan["stacked"]:
        source = heads[0] if heads else ready[0]
        count = source.shape[0]
        heads = [source.at[m] for m in range(count)] if heads else []
        ready = [] if heads else [source.at[m] for m in range(count)]
    if heads:
        if placed is None:
            (room,) = refs
            placed = [room.at[i] for i in range(len(heads))]
        for i, head in enumerate(heads):
            block = i if plan["stacked"] else lax.rem(here_ref[0] - plan["slots"][i] + SLICES, SLICES)
            spares = [spare_ref.at[block] for spare_ref in spare_refs]
            place_rows(head, spares, plan["first_pair"], places_ref[block], placed[i])
        ready = ready + placed
    pair_sums(ready, plan["pairs"], plan["steps"], tiles)
    bins, count = out_ref.shape[-2], tiles.shape[0]
    wanted = rows_ref[0:1, :] == lax.broadcasted_iota(jnp.int32, (bins, count), 0).astype(f32)
    high, low = two_terms(tiles[...])
    stacked = []
    for half in range(2):
        weights = jnp.where(wanted, jnp.broadcast_to(rows_ref[half + 1:half + 2, :], (bins, count)), 0.0)
        weights = jnp.concatenate(two_terms(weights), axis=0)
        at = slice(half * LANES, (half + 1) * LANES)
        both = jnp.dot(weights, high[:, at], preferred_element_type=f32)
        both = both[:bins] + both[bins:]
        stacked.append(both + jnp.dot(weights[:bins], low[:, at], preferred_element_type=f32))
    stacked = jnp.concatenate(stacked, axis=1)
    if before_ref is not None:
        stacked += before_ref[...]
    if len(out_ref.shape) == 2:
        out_ref[...] = stacked
    else:
        for copy in range(out_ref.shape[0]):
            out_ref[copy] = stacked.astype(out_ref.dtype)


def cross(here, pairs, steps, bins, weights, ready=(), heads=(), slots=(), spares=(), first_pair=0, places=None,
          before=None, copies=None, hand_on=False, stacked=False):
    shape = (bins, 2 * LANES)
    inputs = list(ready) + list(heads) + (list(spares) + [places] if heads else []) + [weights]
    if before is not None:
        inputs.append(before)
    if copies is None:
        out_shape = [jax.ShapeDtypeStruct(shape, jnp.float32)]
    else:
        out_shape = [jax.ShapeDtypeStruct((copies,) + shape, jnp.bfloat16)]
    scratch = [pltpu.VMEM((len(pairs) * G, 2 * LANES), jnp.float32)]
    if hand_on:
        out_shape += [jax.ShapeDtypeStruct((G * steps, 2 * LANES), jnp.bfloat16)] * len(heads)
    elif heads:
        count = heads[0].shape[0] if stacked else len(heads)
        scratch.append(pltpu.VMEM((count, G * steps, 2 * LANES), jnp.bfloat16))
    plan = dict(
        ready=len(ready), heads=len(heads), slots=slots, before=before is not None, hand_on=hand_on,
        stacked=stacked, first_pair=first_pair, pairs=pairs, steps=steps,
    )
    result = pl.pallas_call(
        functools.partial(cross_kernel, plan),
        in_specs=[pl.BlockSpec(memory_space=pltpu.SMEM)] + [pl.BlockSpec(memory_space=pltpu.VMEM)] * len(inputs),
        out_shape=out_shape,
        scratch_shapes=scratch,
        compiler_params=pltpu.CompilerParams(vmem_limit_bytes=VMEM if stacked and copies else VMEM_SMALL),
        cost_estimate=pl.CostEstimate(
            flops=8 * G * steps * LANES * len(pairs), bytes_accessed=4 * G * steps * LANES * len(pairs), transcendentals=0
        ),
        name="cross",
    )(here, *inputs)
    return result if hand_on else result[0]


def weights_kernel(blocks, total_segs, here_ref, meta_ref, *refs):
    f32, bf16 = jnp.float32, jnp.bfloat16
    meta = jnp.concatenate([meta_ref[b, 0:1, :] for b in range(blocks)], axis=0)
    masks, labels = meta[:, :LANES], meta[:, LANES:]
    empty = jnp.zeros((R, LANES), bf16)
    padded = jnp.concatenate([masks.astype(f32), empty.astype(f32)], axis=0)
    half = len(refs) // 2
    places_ref = refs[-1]
    in_place = place_order().astype(f32).astype(bf16)
    for b in range(blocks):
        rows = sorted_rows(masks[b:b + 1].astype(f32)).astype(f32).astype(bf16)
        places = lax.dot_general(in_place, rows, (((1,), (1,)), ((), ())), preferred_element_type=f32)
        places_ref[b] = places.astype(bf16)
    for ends_ref, out_ref in zip(refs[:half], refs[half:-1]):
        lanes = out_ref.shape[1]
        first, second = ends_ref[0:1, :], ends_ref[1:2, :]
        slots = first < 0
        held = [jnp.where(slots, lax.rem(here_ref[0] + end + 2 * blocks, blocks), end) for end in (first, second)]
        low, far = jnp.minimum(held[0], held[1]), jnp.abs(held[0] - held[1])
        sign = jnp.where(held[0] < held[1], 1.0, -1.0)
        block = lax.broadcasted_iota(jnp.int32, (blocks, lanes), 0)
        group = lax.broadcasted_iota(jnp.int32, (LANES, lanes), 1) % G
        place = lax.broadcasted_iota(jnp.int32, (LANES, lanes), 0)
        chosen = (place == (far - 1) * G + group).astype(f32).astype(bf16)
        label = jnp.dot(labels, chosen, preferred_element_type=f32)
        label = jnp.sum(jnp.where(block == low, label, 0.0), axis=0, keepdims=True)
        member = (place // (LANES // G) == group).astype(f32).astype(bf16)
        count = jnp.zeros((1, lanes), f32)
        for d in range(1, R + 1):
            both = (padded[:blocks] * padded[d:d + blocks]).astype(bf16)
            of_block = jnp.dot(both, member, preferred_element_type=f32)
            count += jnp.sum(jnp.where((block == low) & (far == d), of_block, 0.0), axis=0, keepdims=True)
        scale = jnp.where(far <= R, 1.0 / (total_segs * jnp.maximum(count, 1.0)), 0.0)
        out_ref[...] = jnp.concatenate([label, scale, scale * sign, jnp.zeros((5, lanes), f32)], axis=0)


def pair_weights(here, meta, at, total_segs, pair_lists):
    blocks = meta.shape[0]
    ends = [jnp.asarray(np.repeat(np.array(pairs, np.int32).T, G, axis=1)) for pairs in pair_lists]
    whole = lambda shape: pl.BlockSpec(shape, lambda i, *_: (0, 0))
    shapes = [(8, G * len(pairs)) for pairs in pair_lists]
    return pl.pallas_call(
        functools.partial(weights_kernel, blocks, total_segs),
        grid_spec=pltpu.PrefetchScalarGridSpec(
            num_scalar_prefetch=1,
            grid=(1,),
            in_specs=[pl.BlockSpec((blocks, META, 2 * LANES), lambda i, *_: (0, at // META, 0))]
            + [whole(end.shape) for end in ends],
            out_specs=[whole(shape) for shape in shapes]
            + [pl.BlockSpec((blocks, PAIR, PAIR), lambda i, *_: (0, 0, 0))],
        ),
        out_shape=[jax.ShapeDtypeStruct(shape, jnp.float32) for shape in shapes]
        + [jax.ShapeDtypeStruct((blocks, PAIR, PAIR), jnp.bfloat16)],
        compiler_params=pltpu.CompilerParams(vmem_limit_bytes=VMEM_SMALL),
        name="weights",
    )(here, meta, *ends)


def lags_kernel(stacks_ref, zero_ref, two_ref, odd_ref, out_ref):
    f32 = jnp.float32
    copies = stacks_ref.shape[0] // SLICES
    pieces = []
    for piece in range(SLICES):
        total = stacks_ref[piece].astype(f32)
        for copy in range(1, copies):
            total += stacks_ref[copy * SLICES + piece].astype(f32)
        pieces.append(total)

    def product(values, table):
        both = jnp.dot(jnp.concatenate(two_terms(values), axis=0), table, preferred_element_type=f32)
        return both[:BIN_DEV] + both[BIN_DEV:]

    zero = product(jnp.concatenate(pieces[0:2], axis=1), zero_ref[...])
    two = product(jnp.concatenate(pieces[4:6], axis=1), two_ref[...])
    odd = product(jnp.concatenate(pieces[2:4] + pieces[6:8], axis=1), odd_ref[...])
    plus, minus = zero + two, zero - two
    out_ref[:, :LAGQ] = plus + odd[:, :LAGQ]
    out_ref[:, LAGQ:2 * LAGQ] = minus + odd[:, LAGQ:]
    out_ref[:, 2 * LAGQ:3 * LAGQ] = plus - odd[:, :LAGQ]
    out_ref[:, 3 * LAGQ:] = minus - odd[:, LAGQ:]


def lags(stacks):
    tables = [jnp.asarray(table) for table in inverse_tables()]
    return pl.pallas_call(
        lags_kernel,
        out_shape=jax.ShapeDtypeStruct((BIN_DEV, NLAG), jnp.float32),
        compiler_params=pltpu.CompilerParams(vmem_limit_bytes=VMEM_SMALL),
        name="lags",
    )(stacks, *tables)


def fixed_pairs(blocks):
    return [(b, b + d) for b in range(blocks) for d in range(1, R + 1) if b + d < blocks]


def sent_along(x, mask, owners, bins, total_segs):
    seg_count = lax.axis_size("seg")
    count = lax.axis_size("chan")
    early = EARLY_SEGS * LANES
    late = x.shape[0] - early
    here = lax.axis_index("chan").astype(jnp.int32).reshape(1)
    first, *spare_early = spectra(x, mask, owners, bins, 0, early, early, KEPT, with_meta=True)
    first = lax.all_to_all(first, "chan", split_axis=0, concat_axis=0, tiled=True)
    second = list(spectra(x, mask, owners, bins, early, late, PAIR, KEPT, here=here))
    spare_late = second[SLICES:]
    at = early // PAIR * KEPT
    most = jnp.max(jnp.sum(first[:, at, :LANES].astype(jnp.float32), axis=1))
    spares, below = [], TIERS[0]
    for tier, *parts in zip(TIERS[1:], spare_early, spare_late):
        spares.append(lax.cond(
            most > below,
            lambda parts: lax.all_to_all(jnp.concatenate(parts, axis=1), "chan", split_axis=0, concat_axis=0, tiled=True),
            lambda parts: jnp.zeros((count, sum(part.shape[1] for part in parts), 2 * LANES), jnp.bfloat16),
            parts,
        ))
        below += tier

    *late_sent, _ = lax.optimization_barrier((second[SENT[-2]], second[SENT[-1]], tuple(spares)))
    second[SENT[-2]], second[SENT[-1]] = late_sent
    slots = {0: second[0]}
    for shift in SENT:
        slots[shift] = lax.ppermute(second[shift], "chan", [(i, (i + shift) % count) for i in range(count)])

    fixed = fixed_pairs(count)
    known = (0,) + SENT
    stages = [
        [(i, j) for j in range(start, end) for i in range(j)] for start, end in zip((1,) + STAGES, STAGES)
    ]
    as_slots = lambda pairs: [(-known[i] - count, -known[j] - count) for i, j in pairs]
    weights = pair_weights(here, first, at, total_segs, [fixed] + [as_slots(pairs) for pairs in stages])
    places = weights[-1]
    bins = count * BIN_DEV
    stacks = cross(
        here, fixed, early // G, bins, weights[0], heads=[first], spares=spares, places=places, stacked=True
    )
    ready, start = [], 0
    for end, pairs, weight in zip(STAGES, stages, weights[1:]):
        final = end == len(known)
        result = cross(
            here, pairs, late // G, bins, weight,
            ready=ready, heads=[slots[slot] for slot in known[start:end]], slots=known[start:end],
            spares=spares, first_pair=early // PAIR, places=places, before=stacks,
            copies=seg_count if final else None, hand_on=not final,
        )
        if final:
            return result
        stacks, ready, start = result[0], ready + list(result[1:]), end


def sent_at_once(x, mask, owners, bins, total_segs):
    seg_count = lax.axis_size("seg")
    count = lax.axis_size("chan")
    rows, chans = x.shape[0], mask.shape[1]
    narrow = NB // count
    splits = LANES // narrow
    here = lax.axis_index("chan").astype(jnp.int32).reshape(1)
    own = jnp.concatenate([mask, owners * BIN_DEV + bins], axis=1)
    every = lax.all_gather(own, "chan", axis=0, tiled=True).astype(jnp.bfloat16)
    every = jnp.pad(every, ((0, 0), (0, 2 * LANES - every.shape[1])))
    every = jnp.broadcast_to(every[:, None, :], (count, META, 2 * LANES))
    fixed = fixed_pairs(count)
    weights = pair_weights(here, every, 0, total_segs, [fixed])[:1]
    (outgoing,) = spectra(x, mask, owners, bins, 0, rows, PAIR, PAIR)
    outgoing = outgoing.reshape(SLICES, rows, 2, splits, narrow).transpose(0, 3, 1, 2, 4)
    outgoing = outgoing.reshape(count, rows, 2 * narrow)
    wide = lax.all_to_all(outgoing, "chan", split_axis=0, concat_axis=0, tiled=True)
    wide = jnp.pad(wide.reshape(count, rows, 2, narrow), ((0, 0), (0, 0), (0, 0), (0, LANES - narrow)))
    wide = wide.reshape(count, rows, 2 * LANES)
    stacks = cross(
        here, fixed, rows // G, count * BIN_DEV, weights[0], ready=[wide], copies=seg_count, stacked=True
    )
    return stacks.reshape(-1, 2, LANES)[..., :narrow]


def per_device(traces, channel_mask, owner_ids, local_bins):
    seg_count = lax.axis_size("seg")
    count = lax.axis_size("chan")
    segs, chans, length = traces.shape
    x = traces.reshape(segs * chans, length)
    mask = channel_mask.reshape(1, chans)
    owners = owner_ids.reshape(1, -1)
    if count == SLICES:
        stacks = sent_along(x, mask, owners, local_bins, segs * seg_count)
        stacks = stacks.reshape(seg_count * count, BIN_DEV, 2 * LANES)
        stacks = lax.all_to_all(stacks, ("seg", "chan"), split_axis=0, concat_axis=0, tiled=True)
    else:
        narrow = NB // count
        stacks = sent_at_once(x, mask, owners, local_bins, segs * seg_count)
        stacks = stacks.reshape(seg_count * count, BIN_DEV, 2 * narrow)
        stacks = lax.all_to_all(stacks, ("seg", "chan"), split_axis=0, concat_axis=0, tiled=True)
        stacks = stacks.reshape(seg_count, SLICES, count // SLICES, BIN_DEV, 2, narrow)
        stacks = stacks.transpose(0, 1, 3, 4, 2, 5).reshape(seg_count * SLICES, BIN_DEV, 2 * LANES)
    return lags(stacks)


def solution(mesh):
    in_specs = (P("seg", "chan", None), P("chan"), P("chan", None, None), P("chan", None))
    out_specs = P("chan", None)
    return jax.shard_map(
        per_device, mesh=mesh, in_specs=in_specs, out_specs=out_specs, check_vma=False
    )
```

```python
import functools
import math

import jax
import jax.numpy as jnp
import ml_dtypes
import numpy as np
from jax import lax
from jax.experimental import pallas as pl
from jax.experimental.pallas import tpu as pltpu
from jax.sharding import PartitionSpec as P

NT = 4096
DEC = 2
K0 = 8
HW = 64
R = 4
G = 16
BIN_DEV = 8
NB = 1024
NLAG = 2048
EPSILON = 1e-06

LANES = 128
SLICES = NB // LANES
FOLD = 4
CLASS = NB // FOLD
QUARTER = NT // FOLD
LAGQ = NLAG // FOLD
VMEM = 58 * 1024 * 1024
VMEM_SMALL = 20 * 1024 * 1024
META = 16
PAIR = 2 * LANES
TIERS = (104, 8, 16)
KEPT = 2 * TIERS[0]
EARLY_SEGS = 2

SENT = (4, 1, 7, 3, 5, 2, 6)
STAGES = (6, 8)


ORDER = np.arange(NB).reshape(LANES, 2, FOLD).transpose(2, 1, 0).reshape(-1)
EIGHTH = NT // (2 * FOLD)


def forward_tables():
    samples = np.arange(QUARTER, dtype=np.int64)
    freqs = K0 + ORDER.astype(np.int64)
    phase = samples[:, None] * freqs[None, :] % NT
    angle = (phase.astype(np.float32) * np.float32(2.0 * math.pi / NT)).astype(np.float64)
    cos = np.cos(angle).astype(np.float32).astype(ml_dtypes.bfloat16)
    sin = (-np.sin(angle)).astype(np.float32).astype(ml_dtypes.bfloat16)

    def part(which, rows, half=slice(0, CLASS)):
        columns = slice(which * CLASS + half.start, which * CLASS + half.stop)
        return [cos[:rows, columns], sin[:rows, columns]]

    halves = [part(0, EIGHTH, slice(at, at + LANES)) for at in (0, LANES)]
    zero, two = np.concatenate(halves[0] + halves[1], axis=1), np.concatenate(part(2, EIGHTH), axis=1)
    odd = np.concatenate(part(1, QUARTER) + part(3, QUARTER), axis=1)
    return np.stack([zero, two]), odd


def band_table():
    near = ORDER[:CLASS] // FOLD
    apart = FOLD * (near[:, None] - near[None, :])
    blocks = [np.abs(apart + shift) <= HW for shift in (0, -1, 1)]
    return np.concatenate(blocks, axis=0).astype(ml_dtypes.bfloat16)


def inverse_tables():
    freqs = K0 + ORDER.astype(np.int64)
    delays = (np.arange(2 * LAGQ, dtype=np.int64) - NLAG // 2) * DEC
    phase = np.mod(freqs[:, None] * delays[None, :], NT)
    angle = phase.astype(np.float64) * (2.0 * math.pi / NT)
    scale = 1.0 / math.sqrt(NB)
    real = (np.cos(angle) * scale).reshape(SLICES, 1, LANES, 2 * LAGQ)
    imag = (-np.sin(angle) * scale).reshape(SLICES, 1, LANES, 2 * LAGQ)
    rows = np.concatenate([real, imag], axis=1).reshape(FOLD, 2 * CLASS, 2 * LAGQ)
    zero = rows[0][:, :LAGQ]
    two = rows[2][:, :LAGQ]
    odd = np.concatenate([rows[1], rows[3]], axis=0)
    return [table.astype(np.float32).astype(ml_dtypes.bfloat16) for table in (zero, two, odd)]


def two_terms(values):
    high = values.astype(jnp.bfloat16)
    low = (values - high.astype(jnp.float32)).astype(jnp.bfloat16)
    return high, low


def two_term_dot(values_ref, table):
    rows = values_ref.shape[0] // 2
    both = jnp.dot(values_ref[...], table, preferred_element_type=jnp.float32)
    return both[:rows] + both[rows:]


def ranks(mask_row):
    shape = (LANES, LANES)
    upto = lax.broadcasted_iota(jnp.int32, shape, 0) <= lax.broadcasted_iota(jnp.int32, shape, 1)
    row = jnp.broadcast_to(mask_row, (META, LANES)).astype(jnp.bfloat16)
    count = jnp.dot(row, upto.astype(jnp.float32).astype(jnp.bfloat16), preferred_element_type=jnp.float32)
    return jnp.where(mask_row > 0, count[0:1] - 1.0, -1.0)


def sorted_rows(mask_row):
    rank = ranks(mask_row)
    rows = []
    for seg in range(2):
        row, below, done = jnp.full_like(rank, -1.0), 0, 0
        for tier in TIERS:
            inside = (rank >= below) & (rank < below + tier)
            row = jnp.where(inside, rank - below + done + seg * tier, row)
            below, done = below + tier, done + 2 * tier
        rows.append(row)
    rows = jnp.concatenate(rows, axis=1)
    return rows == lax.broadcasted_iota(jnp.int32, (PAIR, PAIR), 0).astype(jnp.float32)


def place_order():
    place = lax.broadcasted_iota(jnp.int32, (PAIR, PAIR), 0)
    row = lax.broadcasted_iota(jnp.int32, (PAIR, PAIR), 1)
    inside = place % LANES
    return (place // LANES) * LANES + (inside % G) * (LANES // G) + inside // G == row


def spectra_kernel(relative, with_meta, kept, skip, alone, *refs):
    f32, bf16 = jnp.float32, jnp.bfloat16
    refs = list(refs)
    here_ref = refs.pop(0) if relative else None
    x_any, mask_ref, owner_ref, bins_ref, even_any, odd_any, band_any = refs[:7]
    x_refs, even_ref, odd_ref, band_ref, x_came, arrived, plus, minus, v, ab, early, others, windows = refs[-13:]
    out_refs = refs[7:-14] if relative else refs[7:-13]
    head = refs[-14] if relative else out_refs[0]
    spares = out_refs[1 - len(TIERS):] if kept < PAIR else []
    step, steps = pl.program_id(0), pl.num_programs(0)
    first = step == 0
    rows = x_refs.shape[1]
    slot = 0 if alone else lax.rem(step, 2)
    at_first = (lambda act: act()) if alone else pl.when(first)
    moves = ((even_any, even_ref), (odd_any, odd_ref), (band_any, band_ref))
    copies = [pltpu.make_async_copy(source, into, arrived.at[i]) for i, (source, into) in enumerate(moves)]

    def trace_copy(block, slot):
        at = pl.ds(pl.multiple_of(block * rows + skip, LANES), rows)
        return pltpu.make_async_copy(x_any.at[at], x_refs.at[slot], x_came.at[slot])

    @at_first
    def start():
        trace_copy(0, 0).start()
        for copy in copies:
            copy.start()

    mask = mask_ref[...].astype(f32)
    if kept < PAIR:
        chosen = sorted_rows(mask)
    else:
        chosen = place_order() & (jnp.concatenate([mask, mask], axis=1) > 0)
    chosen = chosen.astype(f32).astype(bf16)

    trace_copy(step, slot).wait()

    if not alone:

        @pl.when(step + 1 < steps)
        def ahead():
            trace_copy(step + 1, 1 - slot).start()

    @at_first
    def table_waits():
        for copy in copies:
            copy.wait()

    x_ref = x_refs.at[slot]
    x = [x_ref[:, m * QUARTER:(m + 1) * QUARTER].astype(f32) for m in range(FOLD)]
    even, odd = x[0] + x[2], x[1] + x[3]
    u = even + odd
    plus[:rows], plus[rows:] = two_terms(u[:, :EIGHTH] + u[:, EIGHTH:])
    minus[:rows], minus[rows:] = two_terms(u[:, :EIGHTH] - u[:, EIGHTH:])
    u = even - odd
    v[:rows], v[rows:2 * rows] = two_terms(u[:, :EIGHTH])
    v[2 * rows:3 * rows], v[3 * rows:] = two_terms(u[:, EIGHTH:])
    ab[:rows], ab[rows:2 * rows] = two_terms(x[0] - x[2])
    ab[2 * rows:3 * rows], ab[3 * rows:] = two_terms(x[1] - x[3])

    for half, ref in enumerate((plus, minus)):
        both = two_term_dot(ref, even_ref[0, :, half * PAIR:(half + 1) * PAIR])
        early[:, half * LANES:(half + 1) * LANES] = both[:, :LANES]
        early[:, CLASS + half * LANES:CLASS + (half + 1) * LANES] = both[:, LANES:]
    turned = jnp.dot(v[...], even_ref[1], preferred_element_type=f32)
    straight = turned[:rows] + turned[rows:2 * rows]
    turned = turned[2 * rows:3 * rows] + turned[3 * rows:]
    lanes = [slice(i * LANES, (i + 1) * LANES) for i in range(4)]
    early[:, 2 * CLASS:2 * CLASS + LANES] = straight[:, lanes[0]] + turned[:, lanes[2]]
    early[:, 2 * CLASS + LANES:3 * CLASS] = straight[:, lanes[1]] - turned[:, lanes[3]]
    early[:, 3 * CLASS:3 * CLASS + LANES] = straight[:, lanes[2]] - turned[:, lanes[0]]
    early[:, 3 * CLASS + LANES:] = straight[:, lanes[3]] + turned[:, lanes[1]]
    turned = jnp.dot(ab[...], odd_ref[...], preferred_element_type=f32)
    straight = turned[:rows] + turned[rows:2 * rows]
    turned = turned[2 * rows:3 * rows] + turned[3 * rows:]
    columns = [slice(i * CLASS, (i + 1) * CLASS) for i in range(4)]
    others[:, columns[0]] = straight[:, columns[0]] + turned[:, columns[1]]
    others[:, columns[1]] = straight[:, columns[1]] - turned[:, columns[0]]
    others[:, columns[2]] = straight[:, columns[2]] - turned[:, columns[3]]
    others[:, columns[3]] = straight[:, columns[3]] + turned[:, columns[2]]

    holders = [(early, 0), (others, 0), (early, 2 * CLASS), (others, 2 * CLASS)]
    power = []
    for ref, start in holders:
        real, imag = ref[:, start:start + CLASS], ref[:, start + CLASS:start + 2 * CLASS]
        power.append(real * real + imag * imag)
    before = [jnp.zeros_like(power[0]), power[0], power[0] + power[1], power[0] + power[1] + power[2]]
    after = [power[1] + power[2] + power[3], power[2] + power[3], power[3], jnp.zeros_like(power[0])]
    for which in range(FOLD):
        at = slice(which * rows, (which + 1) * rows)
        windows[at, :CLASS] = power[which].astype(bf16)
        windows[at, CLASS:2 * CLASS] = before[which].astype(bf16)
        windows[at, 2 * CLASS:] = after[which].astype(bf16)
    sums = jnp.dot(windows[...], band_ref[...], preferred_element_type=f32)
    weight = []
    for which in range(FOLD):
        lane = lax.broadcasted_iota(jnp.int32, (1, CLASS), 1)
        bin_ = ((lane % LANES) * 2 + lane // LANES) * FOLD + which
        within = jnp.minimum(bin_ + HW, NB - 1) - jnp.maximum(bin_ - HW, 0) + 1
        mean = sums[which * rows:(which + 1) * rows] * (1.0 / within.astype(f32))
        weight.append(lax.rsqrt(mean + EPSILON))
    for piece in range(SLICES):
        ref, column = holders[piece // 2]
        column += (piece % 2) * LANES
        scale = weight[piece // 2][:, (piece % 2) * LANES:(piece % 2 + 1) * LANES]
        real = (ref[:, column:column + LANES] * scale).astype(bf16)
        imag = (ref[:, CLASS + column:CLASS + column + LANES] * scale).astype(bf16)
        both = jnp.concatenate([real, imag], axis=1)
        for pair in range(rows // PAIR):
            sorted_ = jnp.dot(chosen, both[pair * PAIR:(pair + 1) * PAIR], preferred_element_type=f32).astype(bf16)
            head[piece, pair * kept:(pair + 1) * kept, :] = sorted_[:kept]
            start = kept
            for spare, tier in zip(spares, TIERS[1:]):
                spare[piece, pair * 2 * tier:(pair + 1) * 2 * tier, :] = sorted_[start:start + 2 * tier]
                start += 2 * tier
    if with_meta:
        tiles = owner_ref.shape[1]
        labels = (owner_ref[...] * BIN_DEV + bins_ref[...]).astype(f32)
        for piece in range(SLICES):
            at = pl.ds(rows // PAIR * kept, META)
            head[piece, at, :] = jnp.zeros((META, 2 * LANES), bf16)
            head[piece, at, :LANES] = jnp.broadcast_to(mask, (META, LANES)).astype(bf16)
            head[piece, at, LANES:LANES + tiles] = jnp.broadcast_to(labels, (META, tiles)).astype(bf16)
    if relative:
        for other in range(SLICES):
            out_refs[other][...] = head[lax.rem(here_ref[0] + other, SLICES)]


def spectra(traces, mask, owners, bins, first_row, rows, block, kept, here=None, with_meta=False):
    relative = here is not None
    tables = [jnp.asarray(table) for table in forward_tables() + (band_table(),)]
    whole = lambda array: pl.BlockSpec(array.shape, lambda i, *_: (0, 0))
    in_place = pl.BlockSpec(memory_space=pl.ANY)
    f32, bf16 = jnp.float32, jnp.bfloat16
    pairs = block // PAIR
    scratch = [
        pltpu.VMEM((2, block, NT), bf16),
    ] + [pltpu.VMEM(table.shape, bf16) for table in tables] + [
        pltpu.SemaphoreType.DMA((2,)),
        pltpu.SemaphoreType.DMA((3,)),
    ]
    scratch += [pltpu.VMEM((terms * block, EIGHTH), bf16) for terms in (2, 2, 4)]
    scratch += [pltpu.VMEM((4 * block, QUARTER), bf16)]
    scratch += [pltpu.VMEM((block, 4 * CLASS), f32)] * 2
    scratch += [pltpu.VMEM((FOLD * block, 3 * CLASS), bf16)]
    if relative:
        scratch = [pltpu.VMEM((SLICES, pairs * kept, 2 * LANES), bf16)] + scratch
        out_specs = [pl.BlockSpec((pairs * kept, 2 * LANES), lambda i, *_: (i, 0))] * SLICES
        out_shape = [jax.ShapeDtypeStruct((rows // PAIR * kept, 2 * LANES), bf16)] * SLICES
    else:
        extra = META if with_meta else 0
        out_specs = [pl.BlockSpec((SLICES, pairs * kept + extra, 2 * LANES), lambda i, *_: (0, i, 0))]
        out_shape = [jax.ShapeDtypeStruct((SLICES, rows // PAIR * kept + extra, 2 * LANES), bf16)]
    for tier in TIERS[1:] if kept < PAIR else ():
        out_specs.append(pl.BlockSpec((SLICES, pairs * 2 * tier, 2 * LANES), lambda i, *_: (0, i, 0)))
        out_shape.append(jax.ShapeDtypeStruct((SLICES, rows // LANES * tier, 2 * LANES), bf16))
    return pl.pallas_call(
        functools.partial(spectra_kernel, relative, with_meta, kept, first_row, rows == block),
        grid_spec=pltpu.PrefetchScalarGridSpec(
            num_scalar_prefetch=1 if relative else 0,
            grid=(rows // block,),
            in_specs=[in_place, whole(mask), whole(owners), whole(bins)] + [in_place] * len(tables),
            out_specs=out_specs,
            scratch_shapes=scratch,
        ),
        out_shape=out_shape,
        compiler_params=pltpu.CompilerParams(vmem_limit_bytes=VMEM),
        cost_estimate=pl.CostEstimate(
            flops=14 * rows * NB * NB, bytes_accessed=rows * NT * 3 + 8 * NB * NB, transcendentals=rows * NB
        ),
        name="spectra",
    )(*([here] if relative else []), traces, mask, owners, bins, *tables)


def pair_sums(block_refs, pairs, steps, tiles):
    f32 = jnp.float32
    done = 0
    groups, current = [], []
    for pair in pairs:
        members = {m for p in current + [pair] for m in p}
        if current and 4 * (len(current) + 1) + 4 * len(members) > 60:
            groups.append(current)
            current = []
        current = current + [pair]
    groups.append(current)
    for group in groups:
        needed = sorted({m for pair in group for m in pair})

        def body(step, sums):
            at = pl.ds(pl.multiple_of(step * G, G), G)
            real = {m: block_refs[m][at, :LANES].astype(f32) for m in needed}
            imag = {m: block_refs[m][at, LANES:].astype(f32) for m in needed}
            new = []
            for (p, q), (re, im) in zip(group, sums):
                re = re + (real[p] * real[q] + imag[p] * imag[q])
                im = im + (imag[p] * real[q] - real[p] * imag[q])
                new.append((re, im))
            return tuple(new)

        zero = jnp.zeros((G, LANES), f32)
        sums = lax.fori_loop(0, steps, body, tuple((zero, zero) for _ in group), unroll=2)
        for re, im in sums:
            tiles[done:done + G, :LANES] = re
            tiles[done:done + G, LANES:] = im
            done += G


def place_rows(head_ref, spare_refs, first_pair, places, out_ref):
    for pair in range(out_ref.shape[0] // PAIR):
        rows = [head_ref[pair * KEPT:(pair + 1) * KEPT]]
        for spare_ref, tier in zip(spare_refs, TIERS[1:]):
            at = (first_pair + pair) * 2 * tier
            rows.append(spare_ref[at:at + 2 * tier])
        placed = jnp.dot(places, jnp.concatenate(rows, axis=0), preferred_element_type=jnp.float32)
        out_ref[pair * PAIR:(pair + 1) * PAIR, :] = placed.astype(out_ref.dtype)


def cross_kernel(plan, here_ref, *refs):
    f32 = jnp.float32
    refs = list(refs)
    take = lambda count: [refs.pop(0) for _ in range(count)]
    ready, heads = take(plan["ready"]), take(plan["heads"])
    *spare_refs, places_ref = take(len(TIERS)) if heads else [None]
    (rows_ref,) = take(1)
    before_ref = refs.pop(0) if plan["before"] else None
    out_ref = refs.pop(0)
    placed = take(len(plan["slots"])) if plan["hand_on"] else None
    tiles = refs.pop(0)
    if plan["stacked"]:
        source = heads[0] if heads else ready[0]
        count = source.shape[0]
        heads = [source.at[m] for m in range(count)] if heads else []
        ready = [] if heads else [source.at[m] for m in range(count)]
    if heads:
        if placed is None:
            (room,) = refs
            placed = [room.at[i] for i in range(len(heads))]
        for i, head in enumerate(heads):
            block = i if plan["stacked"] else lax.rem(here_ref[0] - plan["slots"][i] + SLICES, SLICES)
            spares = [spare_ref.at[block] for spare_ref in spare_refs]
            place_rows(head, spares, plan["first_pair"], places_ref[block], placed[i])
        ready = ready + placed
    pair_sums(ready, plan["pairs"], plan["steps"], tiles)
    bins, count = out_ref.shape[-2], tiles.shape[0]
    wanted = rows_ref[0:1, :] == lax.broadcasted_iota(jnp.int32, (bins, count), 0).astype(f32)
    high, low = two_terms(tiles[...])
    stacked = []
    for half in range(2):
        weights = jnp.where(wanted, jnp.broadcast_to(rows_ref[half + 1:half + 2, :], (bins, count)), 0.0)
        weights = jnp.concatenate(two_terms(weights), axis=0)
        at = slice(half * LANES, (half + 1) * LANES)
        both = jnp.dot(weights, high[:, at], preferred_element_type=f32)
        both = both[:bins] + both[bins:]
        stacked.append(both + jnp.dot(weights[:bins], low[:, at], preferred_element_type=f32))
    stacked = jnp.concatenate(stacked, axis=1)
    if before_ref is not None:
        stacked += before_ref[...]
    if len(out_ref.shape) == 2:
        out_ref[...] = stacked
    else:
        for copy in range(out_ref.shape[0]):
            out_ref[copy] = stacked.astype(out_ref.dtype)


def cross(here, pairs, steps, bins, weights, ready=(), heads=(), slots=(), spares=(), first_pair=0, places=None,
          before=None, copies=None, hand_on=False, stacked=False):
    shape = (bins, 2 * LANES)
    inputs = list(ready) + list(heads) + (list(spares) + [places] if heads else []) + [weights]
    if before is not None:
        inputs.append(before)
    if copies is None:
        out_shape = [jax.ShapeDtypeStruct(shape, jnp.float32)]
    else:
        out_shape = [jax.ShapeDtypeStruct((copies,) + shape, jnp.bfloat16)]
    scratch = [pltpu.VMEM((len(pairs) * G, 2 * LANES), jnp.float32)]
    if hand_on:
        out_shape += [jax.ShapeDtypeStruct((G * steps, 2 * LANES), jnp.bfloat16)] * len(heads)
    elif heads:
        count = heads[0].shape[0] if stacked else len(heads)
        scratch.append(pltpu.VMEM((count, G * steps, 2 * LANES), jnp.bfloat16))
    plan = dict(
        ready=len(ready), heads=len(heads), slots=slots, before=before is not None, hand_on=hand_on,
        stacked=stacked, first_pair=first_pair, pairs=pairs, steps=steps,
    )
    result = pl.pallas_call(
        functools.partial(cross_kernel, plan),
        in_specs=[pl.BlockSpec(memory_space=pltpu.SMEM)] + [pl.BlockSpec(memory_space=pltpu.VMEM)] * len(inputs),
        out_shape=out_shape,
        scratch_shapes=scratch,
        compiler_params=pltpu.CompilerParams(vmem_limit_bytes=VMEM if stacked and copies else VMEM_SMALL),
        cost_estimate=pl.CostEstimate(
            flops=8 * G * steps * LANES * len(pairs), bytes_accessed=4 * G * steps * LANES * len(pairs), transcendentals=0
        ),
        name="cross",
    )(here, *inputs)
    return result if hand_on else result[0]


def weights_kernel(blocks, total_segs, here_ref, meta_ref, *refs):
    f32, bf16 = jnp.float32, jnp.bfloat16
    meta = jnp.concatenate([meta_ref[b, 0:1, :] for b in range(blocks)], axis=0)
    masks, labels = meta[:, :LANES], meta[:, LANES:]
    empty = jnp.zeros((R, LANES), bf16)
    padded = jnp.concatenate([masks.astype(f32), empty.astype(f32)], axis=0)
    half = len(refs) // 2
    places_ref = refs[-1]
    in_place = place_order().astype(f32).astype(bf16)
    for b in range(blocks):
        rows = sorted_rows(masks[b:b + 1].astype(f32)).astype(f32).astype(bf16)
        places = lax.dot_general(in_place, rows, (((1,), (1,)), ((), ())), preferred_element_type=f32)
        places_ref[b] = places.astype(bf16)
    for ends_ref, out_ref in zip(refs[:half], refs[half:-1]):
        lanes = out_ref.shape[1]
        first, second = ends_ref[0:1, :], ends_ref[1:2, :]
        slots = first < 0
        held = [jnp.where(slots, lax.rem(here_ref[0] + end + 2 * blocks, blocks), end) for end in (first, second)]
        low, far = jnp.minimum(held[0], held[1]), jnp.abs(held[0] - held[1])
        sign = jnp.where(held[0] < held[1], 1.0, -1.0)
        block = lax.broadcasted_iota(jnp.int32, (blocks, lanes), 0)
        group = lax.broadcasted_iota(jnp.int32, (LANES, lanes), 1) % G
        place = lax.broadcasted_iota(jnp.int32, (LANES, lanes), 0)
        chosen = (place == (far - 1) * G + group).astype(f32).astype(bf16)
        label = jnp.dot(labels, chosen, preferred_element_type=f32)
        label = jnp.sum(jnp.where(block == low, label, 0.0), axis=0, keepdims=True)
        member = (place // (LANES // G) == group).astype(f32).astype(bf16)
        count = jnp.zeros((1, lanes), f32)
        for d in range(1, R + 1):
            both = (padded[:blocks] * padded[d:d + blocks]).astype(bf16)
            of_block = jnp.dot(both, member, preferred_element_type=f32)
            count += jnp.sum(jnp.where((block == low) & (far == d), of_block, 0.0), axis=0, keepdims=True)
        scale = jnp.where(far <= R, 1.0 / (total_segs * jnp.maximum(count, 1.0)), 0.0)
        out_ref[...] = jnp.concatenate([label, scale, scale * sign, jnp.zeros((5, lanes), f32)], axis=0)


def pair_weights(here, meta, at, total_segs, pair_lists):
    blocks = meta.shape[0]
    ends = [jnp.asarray(np.repeat(np.array(pairs, np.int32).T, G, axis=1)) for pairs in pair_lists]
    whole = lambda shape: pl.BlockSpec(shape, lambda i, *_: (0, 0))
    shapes = [(8, G * len(pairs)) for pairs in pair_lists]
    return pl.pallas_call(
        functools.partial(weights_kernel, blocks, total_segs),
        grid_spec=pltpu.PrefetchScalarGridSpec(
            num_scalar_prefetch=1,
            grid=(1,),
            in_specs=[pl.BlockSpec((blocks, META, 2 * LANES), lambda i, *_: (0, at // META, 0))]
            + [whole(end.shape) for end in ends],
            out_specs=[whole(shape) for shape in shapes]
            + [pl.BlockSpec((blocks, PAIR, PAIR), lambda i, *_: (0, 0, 0))],
        ),
        out_shape=[jax.ShapeDtypeStruct(shape, jnp.float32) for shape in shapes]
        + [jax.ShapeDtypeStruct((blocks, PAIR, PAIR), jnp.bfloat16)],
        compiler_params=pltpu.CompilerParams(vmem_limit_bytes=VMEM_SMALL),
        name="weights",
    )(here, meta, *ends)


def lags_kernel(stacks_ref, zero_ref, two_ref, odd_ref, out_ref):
    f32 = jnp.float32
    copies = stacks_ref.shape[0] // SLICES
    pieces = []
    for piece in range(SLICES):
        total = stacks_ref[piece].astype(f32)
        for copy in range(1, copies):
            total += stacks_ref[copy * SLICES + piece].astype(f32)
        pieces.append(total)

    def product(values, table):
        both = jnp.dot(jnp.concatenate(two_terms(values), axis=0), table, preferred_element_type=f32)
        return both[:BIN_DEV] + both[BIN_DEV:]

    zero = product(jnp.concatenate(pieces[0:2], axis=1), zero_ref[...])
    two = product(jnp.concatenate(pieces[4:6], axis=1), two_ref[...])
    odd = product(jnp.concatenate(pieces[2:4] + pieces[6:8], axis=1), odd_ref[...])
    plus, minus = zero + two, zero - two
    out_ref[:, :LAGQ] = plus + odd[:, :LAGQ]
    out_ref[:, LAGQ:2 * LAGQ] = minus + odd[:, LAGQ:]
    out_ref[:, 2 * LAGQ:3 * LAGQ] = plus - odd[:, :LAGQ]
    out_ref[:, 3 * LAGQ:] = minus - odd[:, LAGQ:]


def lags(stacks):
    tables = [jnp.asarray(table) for table in inverse_tables()]
    return pl.pallas_call(
        lags_kernel,
        out_shape=jax.ShapeDtypeStruct((BIN_DEV, NLAG), jnp.float32),
        compiler_params=pltpu.CompilerParams(vmem_limit_bytes=VMEM_SMALL),
        name="lags",
    )(stacks, *tables)


def fixed_pairs(blocks):
    return [(b, b + d) for b in range(blocks) for d in range(1, R + 1) if b + d < blocks]


def sent_along(x, mask, owners, bins, total_segs):
    seg_count = lax.axis_size("seg")
    count = lax.axis_size("chan")
    early = EARLY_SEGS * LANES
    late = x.shape[0] - early
    here = lax.axis_index("chan").astype(jnp.int32).reshape(1)
    first, *spare_early = spectra(x, mask, owners, bins, 0, early, early, KEPT, with_meta=True)
    first = lax.all_to_all(first, "chan", split_axis=0, concat_axis=0, tiled=True)
    second = list(spectra(x, mask, owners, bins, early, late, PAIR, KEPT, here=here))
    spare_late = second[SLICES:]
    at = early // PAIR * KEPT
    most = jnp.max(jnp.sum(first[:, at, :LANES].astype(jnp.float32), axis=1))
    spares, below = [], TIERS[0]
    for tier, *parts in zip(TIERS[1:], spare_early, spare_late):
        spares.append(lax.cond(
            most > below,
            lambda parts: lax.all_to_all(jnp.concatenate(parts, axis=1), "chan", split_axis=0, concat_axis=0, tiled=True),
            lambda parts: jnp.zeros((count, sum(part.shape[1] for part in parts), 2 * LANES), jnp.bfloat16),
            parts,
        ))
        below += tier

    *late_sent, _ = lax.optimization_barrier((second[SENT[-2]], second[SENT[-1]], tuple(spares)))
    second[SENT[-2]], second[SENT[-1]] = late_sent
    slots = {0: second[0]}
    for shift in SENT:
        slots[shift] = lax.ppermute(second[shift], "chan", [(i, (i + shift) % count) for i in range(count)])

    fixed = fixed_pairs(count)
    known = (0,) + SENT
    stages = [
        [(i, j) for j in range(start, end) for i in range(j)] for start, end in zip((1,) + STAGES, STAGES)
    ]
    as_slots = lambda pairs: [(-known[i] - count, -known[j] - count) for i, j in pairs]
    weights = pair_weights(here, first, at, total_segs, [fixed] + [as_slots(pairs) for pairs in stages])
    places = weights[-1]
    bins = count * BIN_DEV
    stacks = cross(
        here, fixed, early // G, bins, weights[0], heads=[first], spares=spares, places=places, stacked=True
    )
    ready, start = [], 0
    for end, pairs, weight in zip(STAGES, stages, weights[1:]):
        final = end == len(known)
        result = cross(
            here, pairs, late // G, bins, weight,
            ready=ready, heads=[slots[slot] for slot in known[start:end]], slots=known[start:end],
            spares=spares, first_pair=early // PAIR, places=places, before=stacks,
            copies=seg_count if final else None, hand_on=not final,
        )
        if final:
            return result
        stacks, ready, start = result[0], ready + list(result[1:]), end


def sent_at_once(x, mask, owners, bins, total_segs):
    seg_count = lax.axis_size("seg")
    count = lax.axis_size("chan")
    rows, chans = x.shape[0], mask.shape[1]
    narrow = NB // count
    splits = LANES // narrow
    here = lax.axis_index("chan").astype(jnp.int32).reshape(1)
    own = jnp.concatenate([mask, owners * BIN_DEV + bins], axis=1)
    every = lax.all_gather(own, "chan", axis=0, tiled=True).astype(jnp.bfloat16)
    every = jnp.pad(every, ((0, 0), (0, 2 * LANES - every.shape[1])))
    every = jnp.broadcast_to(every[:, None, :], (count, META, 2 * LANES))
    fixed = fixed_pairs(count)
    weights = pair_weights(here, every, 0, total_segs, [fixed])[:1]
    (outgoing,) = spectra(x, mask, owners, bins, 0, rows, PAIR, PAIR)
    outgoing = outgoing.reshape(SLICES, rows, 2, splits, narrow).transpose(0, 3, 1, 2, 4)
    outgoing = outgoing.reshape(count, rows, 2 * narrow)
    wide = lax.all_to_all(outgoing, "chan", split_axis=0, concat_axis=0, tiled=True)
    wide = jnp.pad(wide.reshape(count, rows, 2, narrow), ((0, 0), (0, 0), (0, 0), (0, LANES - narrow)))
    wide = wide.reshape(count, rows, 2 * LANES)
    stacks = cross(
        here, fixed, rows // G, count * BIN_DEV, weights[0], ready=[wide], copies=seg_count, stacked=True
    )
    return stacks.reshape(-1, 2, LANES)[..., :narrow]


def per_device(traces, channel_mask, owner_ids, local_bins):
    seg_count = lax.axis_size("seg")
    count = lax.axis_size("chan")
    segs, chans, length = traces.shape
    x = traces.reshape(segs * chans, length)
    mask = channel_mask.reshape(1, chans)
    owners = owner_ids.reshape(1, -1)
    if count == SLICES:
        stacks = sent_along(x, mask, owners, local_bins, segs * seg_count)
        stacks = stacks.reshape(seg_count * count, BIN_DEV, 2 * LANES)
        stacks = lax.all_to_all(stacks, ("seg", "chan"), split_axis=0, concat_axis=0, tiled=True)
    else:
        narrow = NB // count
        stacks = sent_at_once(x, mask, owners, local_bins, segs * seg_count)
        stacks = stacks.reshape(seg_count * count, BIN_DEV, 2 * narrow)
        stacks = lax.all_to_all(stacks, ("seg", "chan"), split_axis=0, concat_axis=0, tiled=True)
        stacks = stacks.reshape(seg_count, SLICES, count // SLICES, BIN_DEV, 2, narrow)
        stacks = stacks.transpose(0, 1, 3, 4, 2, 5).reshape(seg_count * SLICES, BIN_DEV, 2 * LANES)
    return lags(stacks)


def solution(mesh):
    in_specs = (P("seg", "chan", None), P("chan"), P("chan", None, None), P("chan", None))
    out_specs = P("chan", None)
    return jax.shard_map(
        per_device, mesh=mesh, in_specs=in_specs, out_specs=out_specs, check_vma=False
    )
```

```python
import functools
import math

import jax
import jax.numpy as jnp
import ml_dtypes
import numpy as np
from jax import lax
from jax.experimental import pallas as pl
from jax.experimental.pallas import tpu as pltpu
from jax.sharding import PartitionSpec as P

NT = 4096
DEC = 2
K0 = 8
HW = 64
R = 4
G = 16
BIN_DEV = 8
NB = 1024
NLAG = 2048
EPSILON = 1e-06

LANES = 128
SLICES = NB // LANES
FOLD = 4
CLASS = NB // FOLD
QUARTER = NT // FOLD
LAGQ = NLAG // FOLD
VMEM = 58 * 1024 * 1024
VMEM_SMALL = 20 * 1024 * 1024
META = 16
PAIR = 2 * LANES
TIERS = (104, 8, 16)
KEPT = 2 * TIERS[0]
EARLY_SEGS = 2

SENT = (4, 1, 7, 3, 5, 2, 6)
STAGES = (6, 8)


ORDER = np.arange(NB).reshape(LANES, 2, FOLD).transpose(2, 1, 0).reshape(-1)
EIGHTH = NT // (2 * FOLD)


def forward_tables():
    samples = np.arange(QUARTER, dtype=np.int64)
    freqs = K0 + ORDER.astype(np.int64)
    phase = samples[:, None] * freqs[None, :] % NT
    angle = (phase.astype(np.float32) * np.float32(2.0 * math.pi / NT)).astype(np.float64)
    cos = np.cos(angle).astype(np.float32).astype(ml_dtypes.bfloat16)
    sin = (-np.sin(angle)).astype(np.float32).astype(ml_dtypes.bfloat16)

    def part(which, rows, half=slice(0, CLASS)):
        columns = slice(which * CLASS + half.start, which * CLASS + half.stop)
        return [cos[:rows, columns], sin[:rows, columns]]

    halves = [part(0, EIGHTH, slice(at, at + LANES)) for at in (0, LANES)]
    zero, two = np.concatenate(halves[0] + halves[1], axis=1), np.concatenate(part(2, EIGHTH), axis=1)
    odd = np.concatenate(part(1, QUARTER) + part(3, QUARTER), axis=1)
    return np.stack([zero, two]), odd


def band_table():
    near = ORDER[:CLASS] // FOLD
    apart = FOLD * (near[:, None] - near[None, :])
    blocks = [np.abs(apart + shift) <= HW for shift in (0, -1, 1)]
    return np.concatenate(blocks, axis=0).astype(ml_dtypes.bfloat16)


def inverse_tables():
    freqs = K0 + ORDER.astype(np.int64)
    delays = (np.arange(2 * LAGQ, dtype=np.int64) - NLAG // 2) * DEC
    phase = np.mod(freqs[:, None] * delays[None, :], NT)
    angle = phase.astype(np.float64) * (2.0 * math.pi / NT)
    scale = 1.0 / math.sqrt(NB)
    real = (np.cos(angle) * scale).reshape(SLICES, 1, LANES, 2 * LAGQ)
    imag = (-np.sin(angle) * scale).reshape(SLICES, 1, LANES, 2 * LAGQ)
    rows = np.concatenate([real, imag], axis=1).reshape(FOLD, 2 * CLASS, 2 * LAGQ)
    zero = rows[0][:, :LAGQ]
    two = rows[2][:, :LAGQ]
    odd = np.concatenate([rows[1], rows[3]], axis=0)
    return [table.astype(np.float32).astype(ml_dtypes.bfloat16) for table in (zero, two, odd)]


def two_terms(values):
    high = values.astype(jnp.bfloat16)
    low = (values - high.astype(jnp.float32)).astype(jnp.bfloat16)
    return high, low


def two_term_dot(values_ref, table):
    rows = values_ref.shape[0] // 2
    both = jnp.dot(values_ref[...], table, preferred_element_type=jnp.float32)
    return both[:rows] + both[rows:]


def ranks(mask_row):
    shape = (LANES, LANES)
    upto = lax.broadcasted_iota(jnp.int32, shape, 0) <= lax.broadcasted_iota(jnp.int32, shape, 1)
    row = jnp.broadcast_to(mask_row, (META, LANES)).astype(jnp.bfloat16)
    count = jnp.dot(row, upto.astype(jnp.float32).astype(jnp.bfloat16), preferred_element_type=jnp.float32)
    return jnp.where(mask_row > 0, count[0:1] - 1.0, -1.0)


def sorted_rows(mask_row):
    rank = ranks(mask_row)
    rows = []
    for seg in range(2):
        row, below, done = jnp.full_like(rank, -1.0), 0, 0
        for tier in TIERS:
            inside = (rank >= below) & (rank < below + tier)
            row = jnp.where(inside, rank - below + done + seg * tier, row)
            below, done = below + tier, done + 2 * tier
        rows.append(row)
    rows = jnp.concatenate(rows, axis=1)
    return rows == lax.broadcasted_iota(jnp.int32, (PAIR, PAIR), 0).astype(jnp.float32)


def place_order():
    place = lax.broadcasted_iota(jnp.int32, (PAIR, PAIR), 0)
    row = lax.broadcasted_iota(jnp.int32, (PAIR, PAIR), 1)
    inside = place % LANES
    return (place // LANES) * LANES + (inside % G) * (LANES // G) + inside // G == row


def spectra_kernel(relative, with_meta, kept, skip, alone, *refs):
    f32, bf16 = jnp.float32, jnp.bfloat16
    refs = list(refs)
    here_ref = refs.pop(0) if relative else None
    x_any, mask_any, owner_any, bins_any, even_any, odd_any, band_any = refs[:7]
    x_refs, even_ref, odd_ref, band_ref, mask_ref, owner_ref, bins_ref = refs[-16:-9]
    x_came, arrived, plus, minus, v, ab, early, others, windows = refs[-9:]
    out_refs = refs[7:-17] if relative else refs[7:-16]
    head = refs[-17] if relative else out_refs[0]
    spares = out_refs[1 - len(TIERS):] if kept < PAIR else []
    step, steps = pl.program_id(0), pl.num_programs(0)
    first = step == 0
    rows = x_refs.shape[1]
    slot = 0 if alone else lax.rem(step, 2)
    at_first = (lambda act: act()) if alone else pl.when(first)
    moves = ((even_any, even_ref), (odd_any, odd_ref), (band_any, band_ref))
    moves += ((mask_any, mask_ref),)
    if with_meta:
        moves += ((owner_any, owner_ref), (bins_any, bins_ref))
    copies = [pltpu.make_async_copy(source, into, arrived.at[i]) for i, (source, into) in enumerate(moves)]

    def trace_copy(block, slot):
        at = pl.ds(pl.multiple_of(block * rows + skip, LANES), rows)
        return pltpu.make_async_copy(x_any.at[at], x_refs.at[slot], x_came.at[slot])

    @at_first
    def start():
        trace_copy(0, 0).start()
        for copy in copies:
            copy.start()

    @at_first
    def table_waits():
        for copy in copies:
            copy.wait()

    mask = mask_ref[...].astype(f32)
    if kept < PAIR:
        chosen = sorted_rows(mask)
    else:
        chosen = place_order() & (jnp.concatenate([mask, mask], axis=1) > 0)
    chosen = chosen.astype(f32).astype(bf16)

    trace_copy(step, slot).wait()

    if not alone:

        @pl.when(step + 1 < steps)
        def ahead():
            trace_copy(step + 1, 1 - slot).start()

    x_ref = x_refs.at[slot]
    x = [x_ref[:, m * QUARTER:(m + 1) * QUARTER].astype(f32) for m in range(FOLD)]
    even, odd = x[0] + x[2], x[1] + x[3]
    u = even + odd
    plus[:rows], plus[rows:] = two_terms(u[:, :EIGHTH] + u[:, EIGHTH:])
    minus[:rows], minus[rows:] = two_terms(u[:, :EIGHTH] - u[:, EIGHTH:])
    u = even - odd
    v[:rows], v[rows:2 * rows] = two_terms(u[:, :EIGHTH])
    v[2 * rows:3 * rows], v[3 * rows:] = two_terms(u[:, EIGHTH:])
    ab[:rows], ab[rows:2 * rows] = two_terms(x[0] - x[2])
    ab[2 * rows:3 * rows], ab[3 * rows:] = two_terms(x[1] - x[3])

    for half, ref in enumerate((plus, minus)):
        both = two_term_dot(ref, even_ref[0, :, half * PAIR:(half + 1) * PAIR])
        early[:, half * LANES:(half + 1) * LANES] = both[:, :LANES]
        early[:, CLASS + half * LANES:CLASS + (half + 1) * LANES] = both[:, LANES:]
    turned = jnp.dot(v[...], even_ref[1], preferred_element_type=f32)
    straight = turned[:rows] + turned[rows:2 * rows]
    turned = turned[2 * rows:3 * rows] + turned[3 * rows:]
    lanes = [slice(i * LANES, (i + 1) * LANES) for i in range(4)]
    early[:, 2 * CLASS:2 * CLASS + LANES] = straight[:, lanes[0]] + turned[:, lanes[2]]
    early[:, 2 * CLASS + LANES:3 * CLASS] = straight[:, lanes[1]] - turned[:, lanes[3]]
    early[:, 3 * CLASS:3 * CLASS + LANES] = straight[:, lanes[2]] - turned[:, lanes[0]]
    early[:, 3 * CLASS + LANES:] = straight[:, lanes[3]] + turned[:, lanes[1]]
    turned = jnp.dot(ab[...], odd_ref[...], preferred_element_type=f32)
    straight = turned[:rows] + turned[rows:2 * rows]
    turned = turned[2 * rows:3 * rows] + turned[3 * rows:]
    columns = [slice(i * CLASS, (i + 1) * CLASS) for i in range(4)]
    others[:, columns[0]] = straight[:, columns[0]] + turned[:, columns[1]]
    others[:, columns[1]] = straight[:, columns[1]] - turned[:, columns[0]]
    others[:, columns[2]] = straight[:, columns[2]] - turned[:, columns[3]]
    others[:, columns[3]] = straight[:, columns[3]] + turned[:, columns[2]]

    holders = [(early, 0), (others, 0), (early, 2 * CLASS), (others, 2 * CLASS)]
    power = []
    for ref, start in holders:
        real, imag = ref[:, start:start + CLASS], ref[:, start + CLASS:start + 2 * CLASS]
        power.append(real * real + imag * imag)
    before = [jnp.zeros_like(power[0]), power[0], power[0] + power[1], power[0] + power[1] + power[2]]
    after = [power[1] + power[2] + power[3], power[2] + power[3], power[3], jnp.zeros_like(power[0])]
    for which in range(FOLD):
        at = slice(which * rows, (which + 1) * rows)
        windows[at, :CLASS] = power[which].astype(bf16)
        windows[at, CLASS:2 * CLASS] = before[which].astype(bf16)
        windows[at, 2 * CLASS:] = after[which].astype(bf16)
    sums = jnp.dot(windows[...], band_ref[...], preferred_element_type=f32)
    weight = []
    for which in range(FOLD):
        lane = lax.broadcasted_iota(jnp.int32, (1, CLASS), 1)
        bin_ = ((lane % LANES) * 2 + lane // LANES) * FOLD + which
        within = jnp.minimum(bin_ + HW, NB - 1) - jnp.maximum(bin_ - HW, 0) + 1
        mean = sums[which * rows:(which + 1) * rows] * (1.0 / within.astype(f32))
        weight.append(lax.rsqrt(mean + EPSILON))
    for piece in range(SLICES):
        ref, column = holders[piece // 2]
        column += (piece % 2) * LANES
        scale = weight[piece // 2][:, (piece % 2) * LANES:(piece % 2 + 1) * LANES]
        real = (ref[:, column:column + LANES] * scale).astype(bf16)
        imag = (ref[:, CLASS + column:CLASS + column + LANES] * scale).astype(bf16)
        both = jnp.concatenate([real, imag], axis=1)
        for pair in range(rows // PAIR):
            sorted_ = jnp.dot(chosen, both[pair * PAIR:(pair + 1) * PAIR], preferred_element_type=f32).astype(bf16)
            head[piece, pair * kept:(pair + 1) * kept, :] = sorted_[:kept]
            start = kept
            for spare, tier in zip(spares, TIERS[1:]):
                spare[piece, pair * 2 * tier:(pair + 1) * 2 * tier, :] = sorted_[start:start + 2 * tier]
                start += 2 * tier
    if with_meta:
        tiles = owner_ref.shape[1]
        labels = (owner_ref[...] * BIN_DEV + bins_ref[...]).astype(f32)
        for piece in range(SLICES):
            at = pl.ds(rows // PAIR * kept, META)
            head[piece, at, :] = jnp.zeros((META, 2 * LANES), bf16)
            head[piece, at, :LANES] = jnp.broadcast_to(mask, (META, LANES)).astype(bf16)
            head[piece, at, LANES:LANES + tiles] = jnp.broadcast_to(labels, (META, tiles)).astype(bf16)
    if relative:
        for other in range(SLICES):
            out_refs[other][...] = head[lax.rem(here_ref[0] + other, SLICES)]


def spectra(traces, mask, owners, bins, first_row, rows, block, kept, here=None, with_meta=False):
    relative = here is not None
    tables = [jnp.asarray(table) for table in forward_tables() + (band_table(),)]
    in_place = pl.BlockSpec(memory_space=pl.ANY)
    f32, bf16 = jnp.float32, jnp.bfloat16
    pairs = block // PAIR
    scratch = [
        pltpu.VMEM((2, block, NT), bf16),
    ] + [pltpu.VMEM(array.shape, array.dtype) for array in (*tables, mask, owners, bins)] + [
        pltpu.SemaphoreType.DMA((2,)),
        pltpu.SemaphoreType.DMA((6,)),
    ]
    scratch += [pltpu.VMEM((terms * block, EIGHTH), bf16) for terms in (2, 2, 4)]
    scratch += [pltpu.VMEM((4 * block, QUARTER), bf16)]
    scratch += [pltpu.VMEM((block, 4 * CLASS), f32)] * 2
    scratch += [pltpu.VMEM((FOLD * block, 3 * CLASS), bf16)]
    if relative:
        scratch = [pltpu.VMEM((SLICES, pairs * kept, 2 * LANES), bf16)] + scratch
        out_specs = [pl.BlockSpec((pairs * kept, 2 * LANES), lambda i, *_: (i, 0))] * SLICES
        out_shape = [jax.ShapeDtypeStruct((rows // PAIR * kept, 2 * LANES), bf16)] * SLICES
    else:
        extra = META if with_meta else 0
        out_specs = [pl.BlockSpec((SLICES, pairs * kept + extra, 2 * LANES), lambda i, *_: (0, i, 0))]
        out_shape = [jax.ShapeDtypeStruct((SLICES, rows // PAIR * kept + extra, 2 * LANES), bf16)]
    for tier in TIERS[1:] if kept < PAIR else ():
        out_specs.append(pl.BlockSpec((SLICES, pairs * 2 * tier, 2 * LANES), lambda i, *_: (0, i, 0)))
        out_shape.append(jax.ShapeDtypeStruct((SLICES, rows // LANES * tier, 2 * LANES), bf16))
    return pl.pallas_call(
        functools.partial(spectra_kernel, relative, with_meta, kept, first_row, rows == block),
        grid_spec=pltpu.PrefetchScalarGridSpec(
            num_scalar_prefetch=1 if relative else 0,
            grid=(rows // block,),
            in_specs=[in_place] * (4 + len(tables)),
            out_specs=out_specs,
            scratch_shapes=scratch,
        ),
        out_shape=out_shape,
        compiler_params=pltpu.CompilerParams(vmem_limit_bytes=VMEM),
        cost_estimate=pl.CostEstimate(
            flops=14 * rows * NB * NB, bytes_accessed=rows * NT * 3 + 8 * NB * NB, transcendentals=rows * NB
        ),
        name="spectra",
    )(*([here] if relative else []), traces, mask, owners, bins, *tables)


def pair_sums(block_refs, pairs, steps, tiles):
    f32 = jnp.float32
    done = 0
    groups, current = [], []
    for pair in pairs:
        members = {m for p in current + [pair] for m in p}
        if current and 4 * (len(current) + 1) + 4 * len(members) > 60:
            groups.append(current)
            current = []
        current = current + [pair]
    groups.append(current)
    for group in groups:
        needed = sorted({m for pair in group for m in pair})

        def body(step, sums):
            at = pl.ds(pl.multiple_of(step * G, G), G)
            real = {m: block_refs[m][at, :LANES].astype(f32) for m in needed}
            imag = {m: block_refs[m][at, LANES:].astype(f32) for m in needed}
            new = []
            for (p, q), (re, im) in zip(group, sums):
                re = re + (real[p] * real[q] + imag[p] * imag[q])
                im = im + (imag[p] * real[q] - real[p] * imag[q])
                new.append((re, im))
            return tuple(new)

        zero = jnp.zeros((G, LANES), f32)
        sums = lax.fori_loop(0, steps, body, tuple((zero, zero) for _ in group), unroll=2)
        for re, im in sums:
            tiles[done:done + G, :LANES] = re
            tiles[done:done + G, LANES:] = im
            done += G


def place_rows(head_ref, spare_refs, first_pair, places, out_ref):
    for pair in range(out_ref.shape[0] // PAIR):
        rows = [head_ref[pair * KEPT:(pair + 1) * KEPT]]
        for spare_ref, tier in zip(spare_refs, TIERS[1:]):
            at = (first_pair + pair) * 2 * tier
            rows.append(spare_ref[at:at + 2 * tier])
        placed = jnp.dot(places, jnp.concatenate(rows, axis=0), preferred_element_type=jnp.float32)
        out_ref[pair * PAIR:(pair + 1) * PAIR, :] = placed.astype(out_ref.dtype)


def cross_kernel(plan, here_ref, *refs):
    f32 = jnp.float32
    refs = list(refs)
    take = lambda count: [refs.pop(0) for _ in range(count)]
    ready, heads = take(plan["ready"]), take(plan["heads"])
    *spare_refs, places_ref = take(len(TIERS)) if heads else [None]
    (rows_ref,) = take(1)
    before_ref = refs.pop(0) if plan["before"] else None
    out_ref = refs.pop(0)
    placed = take(len(plan["slots"])) if plan["hand_on"] else None
    tiles = refs.pop(0)
    if plan["stacked"]:
        source = heads[0] if heads else ready[0]
        count = source.shape[0]
        heads = [source.at[m] for m in range(count)] if heads else []
        ready = [] if heads else [source.at[m] for m in range(count)]
    if heads:
        if placed is None:
            (room,) = refs
            placed = [room.at[i] for i in range(len(heads))]
        for i, head in enumerate(heads):
            block = i if plan["stacked"] else lax.rem(here_ref[0] - plan["slots"][i] + SLICES, SLICES)
            spares = [spare_ref.at[block] for spare_ref in spare_refs]
            place_rows(head, spares, plan["first_pair"], places_ref[block], placed[i])
        ready = ready + placed
    pair_sums(ready, plan["pairs"], plan["steps"], tiles)
    bins, count = out_ref.shape[-2], tiles.shape[0]
    wanted = rows_ref[0:1, :] == lax.broadcasted_iota(jnp.int32, (bins, count), 0).astype(f32)
    high, low = two_terms(tiles[...])
    stacked = []
    for half in range(2):
        weights = jnp.where(wanted, jnp.broadcast_to(rows_ref[half + 1:half + 2, :], (bins, count)), 0.0)
        weights = jnp.concatenate(two_terms(weights), axis=0)
        at = slice(half * LANES, (half + 1) * LANES)
        both = jnp.dot(weights, high[:, at], preferred_element_type=f32)
        both = both[:bins] + both[bins:]
        stacked.append(both + jnp.dot(weights[:bins], low[:, at], preferred_element_type=f32))
    stacked = jnp.concatenate(stacked, axis=1)
    if before_ref is not None:
        stacked += before_ref[...]
    if len(out_ref.shape) == 2:
        out_ref[...] = stacked
    else:
        for copy in range(out_ref.shape[0]):
            out_ref[copy] = stacked.astype(out_ref.dtype)


def cross(here, pairs, steps, bins, weights, ready=(), heads=(), slots=(), spares=(), first_pair=0, places=None,
          before=None, copies=None, hand_on=False, stacked=False):
    shape = (bins, 2 * LANES)
    inputs = list(ready) + list(heads) + (list(spares) + [places] if heads else []) + [weights]
    if before is not None:
        inputs.append(before)
    if copies is None:
        out_shape = [jax.ShapeDtypeStruct(shape, jnp.float32)]
    else:
        out_shape = [jax.ShapeDtypeStruct((copies,) + shape, jnp.bfloat16)]
    scratch = [pltpu.VMEM((len(pairs) * G, 2 * LANES), jnp.float32)]
    if hand_on:
        out_shape += [jax.ShapeDtypeStruct((G * steps, 2 * LANES), jnp.bfloat16)] * len(heads)
    elif heads:
        count = heads[0].shape[0] if stacked else len(heads)
        scratch.append(pltpu.VMEM((count, G * steps, 2 * LANES), jnp.bfloat16))
    plan = dict(
        ready=len(ready), heads=len(heads), slots=slots, before=before is not None, hand_on=hand_on,
        stacked=stacked, first_pair=first_pair, pairs=pairs, steps=steps,
    )
    result = pl.pallas_call(
        functools.partial(cross_kernel, plan),
        in_specs=[pl.BlockSpec(memory_space=pltpu.SMEM)] + [pl.BlockSpec(memory_space=pltpu.VMEM)] * len(inputs),
        out_shape=out_shape,
        scratch_shapes=scratch,
        compiler_params=pltpu.CompilerParams(vmem_limit_bytes=VMEM if stacked and copies else VMEM_SMALL),
        cost_estimate=pl.CostEstimate(
            flops=8 * G * steps * LANES * len(pairs), bytes_accessed=4 * G * steps * LANES * len(pairs), transcendentals=0
        ),
        name="cross",
    )(here, *inputs)
    return result if hand_on else result[0]


def weights_kernel(blocks, total_segs, here_ref, meta_ref, *refs):
    f32, bf16 = jnp.float32, jnp.bfloat16
    meta = jnp.concatenate([meta_ref[b, 0:1, :] for b in range(blocks)], axis=0)
    masks, labels = meta[:, :LANES], meta[:, LANES:]
    empty = jnp.zeros((R, LANES), bf16)
    padded = jnp.concatenate([masks.astype(f32), empty.astype(f32)], axis=0)
    half = len(refs) // 2
    places_ref = refs[-1]
    in_place = place_order().astype(f32).astype(bf16)
    for b in range(blocks):
        rows = sorted_rows(masks[b:b + 1].astype(f32)).astype(f32).astype(bf16)
        places = lax.dot_general(in_place, rows, (((1,), (1,)), ((), ())), preferred_element_type=f32)
        places_ref[b] = places.astype(bf16)
    for ends_ref, out_ref in zip(refs[:half], refs[half:-1]):
        lanes = out_ref.shape[1]
        first, second = ends_ref[0:1, :], ends_ref[1:2, :]
        slots = first < 0
        held = [jnp.where(slots, lax.rem(here_ref[0] + end + 2 * blocks, blocks), end) for end in (first, second)]
        low, far = jnp.minimum(held[0], held[1]), jnp.abs(held[0] - held[1])
        sign = jnp.where(held[0] < held[1], 1.0, -1.0)
        block = lax.broadcasted_iota(jnp.int32, (blocks, lanes), 0)
        group = lax.broadcasted_iota(jnp.int32, (LANES, lanes), 1) % G
        place = lax.broadcasted_iota(jnp.int32, (LANES, lanes), 0)
        chosen = (place == (far - 1) * G + group).astype(f32).astype(bf16)
        label = jnp.dot(labels, chosen, preferred_element_type=f32)
        label = jnp.sum(jnp.where(block == low, label, 0.0), axis=0, keepdims=True)
        member = (place // (LANES // G) == group).astype(f32).astype(bf16)
        count = jnp.zeros((1, lanes), f32)
        for d in range(1, R + 1):
            both = (padded[:blocks] * padded[d:d + blocks]).astype(bf16)
            of_block = jnp.dot(both, member, preferred_element_type=f32)
            count += jnp.sum(jnp.where((block == low) & (far == d), of_block, 0.0), axis=0, keepdims=True)
        scale = jnp.where(far <= R, 1.0 / (total_segs * jnp.maximum(count, 1.0)), 0.0)
        out_ref[...] = jnp.concatenate([label, scale, scale * sign, jnp.zeros((5, lanes), f32)], axis=0)


def pair_weights(here, meta, at, total_segs, pair_lists):
    blocks = meta.shape[0]
    ends = [jnp.asarray(np.repeat(np.array(pairs, np.int32).T, G, axis=1)) for pairs in pair_lists]
    whole = lambda shape: pl.BlockSpec(shape, lambda i, *_: (0, 0))
    shapes = [(8, G * len(pairs)) for pairs in pair_lists]
    return pl.pallas_call(
        functools.partial(weights_kernel, blocks, total_segs),
        grid_spec=pltpu.PrefetchScalarGridSpec(
            num_scalar_prefetch=1,
            grid=(1,),
            in_specs=[pl.BlockSpec((blocks, META, 2 * LANES), lambda i, *_: (0, at // META, 0))]
            + [whole(end.shape) for end in ends],
            out_specs=[whole(shape) for shape in shapes]
            + [pl.BlockSpec((blocks, PAIR, PAIR), lambda i, *_: (0, 0, 0))],
        ),
        out_shape=[jax.ShapeDtypeStruct(shape, jnp.float32) for shape in shapes]
        + [jax.ShapeDtypeStruct((blocks, PAIR, PAIR), jnp.bfloat16)],
        compiler_params=pltpu.CompilerParams(vmem_limit_bytes=VMEM_SMALL),
        name="weights",
    )(here, meta, *ends)


def lags_kernel(stacks_ref, zero_ref, two_ref, odd_ref, out_ref):
    f32 = jnp.float32
    copies = stacks_ref.shape[0] // SLICES
    pieces = []
    for piece in range(SLICES):
        total = stacks_ref[piece].astype(f32)
        for copy in range(1, copies):
            total += stacks_ref[copy * SLICES + piece].astype(f32)
        pieces.append(total)

    def product(values, table):
        both = jnp.dot(jnp.concatenate(two_terms(values), axis=0), table, preferred_element_type=f32)
        return both[:BIN_DEV] + both[BIN_DEV:]

    zero = product(jnp.concatenate(pieces[0:2], axis=1), zero_ref[...])
    two = product(jnp.concatenate(pieces[4:6], axis=1), two_ref[...])
    odd = product(jnp.concatenate(pieces[2:4] + pieces[6:8], axis=1), odd_ref[...])
    plus, minus = zero + two, zero - two
    out_ref[:, :LAGQ] = plus + odd[:, :LAGQ]
    out_ref[:, LAGQ:2 * LAGQ] = minus + odd[:, LAGQ:]
    out_ref[:, 2 * LAGQ:3 * LAGQ] = plus - odd[:, :LAGQ]
    out_ref[:, 3 * LAGQ:] = minus - odd[:, LAGQ:]


def lags(stacks):
    tables = [jnp.asarray(table) for table in inverse_tables()]
    return pl.pallas_call(
        lags_kernel,
        out_shape=jax.ShapeDtypeStruct((BIN_DEV, NLAG), jnp.float32),
        compiler_params=pltpu.CompilerParams(vmem_limit_bytes=VMEM_SMALL),
        name="lags",
    )(stacks, *tables)


def fixed_pairs(blocks):
    return [(b, b + d) for b in range(blocks) for d in range(1, R + 1) if b + d < blocks]


def sent_along(x, mask, owners, bins, total_segs):
    seg_count = lax.axis_size("seg")
    count = lax.axis_size("chan")
    early = EARLY_SEGS * LANES
    late = x.shape[0] - early
    here = lax.axis_index("chan").astype(jnp.int32).reshape(1)
    first, *spare_early = spectra(x, mask, owners, bins, 0, early, early, KEPT, with_meta=True)
    first = lax.all_to_all(first, "chan", split_axis=0, concat_axis=0, tiled=True)
    second = list(spectra(x, mask, owners, bins, early, late, PAIR, KEPT, here=here))
    spare_late = second[SLICES:]
    at = early // PAIR * KEPT
    most = jnp.max(jnp.sum(first[:, at, :LANES].astype(jnp.float32), axis=1))
    spares, below = [], TIERS[0]
    for tier, *parts in zip(TIERS[1:], spare_early, spare_late):
        spares.append(lax.cond(
            most > below,
            lambda parts: lax.all_to_all(jnp.concatenate(parts, axis=1), "chan", split_axis=0, concat_axis=0, tiled=True),
            lambda parts: jnp.zeros((count, sum(part.shape[1] for part in parts), 2 * LANES), jnp.bfloat16),
            parts,
        ))
        below += tier

    *late_sent, _ = lax.optimization_barrier((second[SENT[-2]], second[SENT[-1]], tuple(spares)))
    second[SENT[-2]], second[SENT[-1]] = late_sent
    slots = {0: second[0]}
    for shift in SENT:
        slots[shift] = lax.ppermute(second[shift], "chan", [(i, (i + shift) % count) for i in range(count)])

    fixed = fixed_pairs(count)
    known = (0,) + SENT
    stages = [
        [(i, j) for j in range(start, end) for i in range(j)] for start, end in zip((1,) + STAGES, STAGES)
    ]
    as_slots = lambda pairs: [(-known[i] - count, -known[j] - count) for i, j in pairs]
    weights = pair_weights(here, first, at, total_segs, [fixed] + [as_slots(pairs) for pairs in stages])
    places = weights[-1]
    bins = count * BIN_DEV
    stacks = cross(
        here, fixed, early // G, bins, weights[0], heads=[first], spares=spares, places=places, stacked=True
    )
    ready, start = [], 0
    for end, pairs, weight in zip(STAGES, stages, weights[1:]):
        final = end == len(known)
        result = cross(
            here, pairs, late // G, bins, weight,
            ready=ready, heads=[slots[slot] for slot in known[start:end]], slots=known[start:end],
            spares=spares, first_pair=early // PAIR, places=places, before=stacks,
            copies=seg_count if final else None, hand_on=not final,
        )
        if final:
            return result
        stacks, ready, start = result[0], ready + list(result[1:]), end


def sent_at_once(x, mask, owners, bins, total_segs):
    seg_count = lax.axis_size("seg")
    count = lax.axis_size("chan")
    rows, chans = x.shape[0], mask.shape[1]
    narrow = NB // count
    splits = LANES // narrow
    here = lax.axis_index("chan").astype(jnp.int32).reshape(1)
    own = jnp.concatenate([mask, owners * BIN_DEV + bins], axis=1)
    every = lax.all_gather(own, "chan", axis=0, tiled=True).astype(jnp.bfloat16)
    every = jnp.pad(every, ((0, 0), (0, 2 * LANES - every.shape[1])))
    every = jnp.broadcast_to(every[:, None, :], (count, META, 2 * LANES))
    fixed = fixed_pairs(count)
    weights = pair_weights(here, every, 0, total_segs, [fixed])[:1]
    (outgoing,) = spectra(x, mask, owners, bins, 0, rows, PAIR, PAIR)
    outgoing = outgoing.reshape(SLICES, rows, 2, splits, narrow).transpose(0, 3, 1, 2, 4)
    outgoing = outgoing.reshape(count, rows, 2 * narrow)
    wide = lax.all_to_all(outgoing, "chan", split_axis=0, concat_axis=0, tiled=True)
    wide = jnp.pad(wide.reshape(count, rows, 2, narrow), ((0, 0), (0, 0), (0, 0), (0, LANES - narrow)))
    wide = wide.reshape(count, rows, 2 * LANES)
    stacks = cross(
        here, fixed, rows // G, count * BIN_DEV, weights[0], ready=[wide], copies=seg_count, stacked=True
    )
    return stacks.reshape(-1, 2, LANES)[..., :narrow]


def per_device(traces, channel_mask, owner_ids, local_bins):
    seg_count = lax.axis_size("seg")
    count = lax.axis_size("chan")
    segs, chans, length = traces.shape
    x = traces.reshape(segs * chans, length)
    mask = channel_mask.reshape(1, chans)
    owners = owner_ids.reshape(1, -1)
    if count == SLICES:
        stacks = sent_along(x, mask, owners, local_bins, segs * seg_count)
        stacks = stacks.reshape(seg_count * count, BIN_DEV, 2 * LANES)
        stacks = lax.all_to_all(stacks, ("seg", "chan"), split_axis=0, concat_axis=0, tiled=True)
    else:
        narrow = NB // count
        stacks = sent_at_once(x, mask, owners, local_bins, segs * seg_count)
        stacks = stacks.reshape(seg_count * count, BIN_DEV, 2 * narrow)
        stacks = lax.all_to_all(stacks, ("seg", "chan"), split_axis=0, concat_axis=0, tiled=True)
        stacks = stacks.reshape(seg_count, SLICES, count // SLICES, BIN_DEV, 2, narrow)
        stacks = stacks.transpose(0, 1, 3, 4, 2, 5).reshape(seg_count * SLICES, BIN_DEV, 2 * LANES)
    return lags(stacks)


def solution(mesh):
    in_specs = (P("seg", "chan", None), P("chan"), P("chan", None, None), P("chan", None))
    out_specs = P("chan", None)
    return jax.shard_map(
        per_device, mesh=mesh, in_specs=in_specs, out_specs=out_specs, check_vma=False
    )
```

```python
import functools
import math

import jax
import jax.numpy as jnp
import ml_dtypes
import numpy as np
from jax import lax
from jax.experimental import pallas as pl
from jax.experimental.pallas import tpu as pltpu
from jax.sharding import PartitionSpec as P

NT = 4096
DEC = 2
K0 = 8
HW = 64
R = 4
G = 16
BIN_DEV = 8
NB = 1024
NLAG = 2048
EPSILON = 1e-06

LANES = 128
SLICES = NB // LANES
FOLD = 4
CLASS = NB // FOLD
QUARTER = NT // FOLD
LAGQ = NLAG // FOLD
VMEM = 58 * 1024 * 1024
VMEM_SMALL = 20 * 1024 * 1024
META = 8
PAIR = 2 * LANES
TIERS = (104, 8, 16)
KEPT = 2 * TIERS[0]
EARLY_SEGS = 2

SENT = (4, 1, 7, 3, 5, 2, 6)
STAGES = (6, 8)


ORDER = np.arange(NB).reshape(LANES, 2, FOLD).transpose(2, 1, 0).reshape(-1)
EIGHTH = NT // (2 * FOLD)


def forward_tables():
    samples = np.arange(QUARTER, dtype=np.int64)
    freqs = K0 + ORDER.astype(np.int64)
    phase = samples[:, None] * freqs[None, :] % NT
    angle = (phase.astype(np.float32) * np.float32(2.0 * math.pi / NT)).astype(np.float64)
    cos = np.cos(angle).astype(np.float32).astype(ml_dtypes.bfloat16)
    sin = (-np.sin(angle)).astype(np.float32).astype(ml_dtypes.bfloat16)

    def part(which, rows, half=slice(0, CLASS)):
        columns = slice(which * CLASS + half.start, which * CLASS + half.stop)
        return [cos[:rows, columns], sin[:rows, columns]]

    halves = [part(0, EIGHTH, slice(at, at + LANES)) for at in (0, LANES)]
    zero, two = np.concatenate(halves[0] + halves[1], axis=1), np.concatenate(part(2, EIGHTH), axis=1)
    odd = np.concatenate(part(1, QUARTER) + part(3, QUARTER), axis=1)
    return np.stack([zero, two]), odd


def band_table():
    near = ORDER[:CLASS] // FOLD
    apart = FOLD * (near[:, None] - near[None, :])
    blocks = [np.abs(apart + shift) <= HW for shift in (0, -1, 1)]
    return np.concatenate(blocks, axis=0).astype(ml_dtypes.bfloat16)


def inverse_tables():
    freqs = K0 + ORDER.astype(np.int64)
    delays = (np.arange(2 * LAGQ, dtype=np.int64) - NLAG // 2) * DEC
    phase = np.mod(freqs[:, None] * delays[None, :], NT)
    angle = phase.astype(np.float64) * (2.0 * math.pi / NT)
    scale = 1.0 / math.sqrt(NB)
    real = (np.cos(angle) * scale).reshape(SLICES, 1, LANES, 2 * LAGQ)
    imag = (-np.sin(angle) * scale).reshape(SLICES, 1, LANES, 2 * LAGQ)
    rows = np.concatenate([real, imag], axis=1).reshape(FOLD, 2 * CLASS, 2 * LAGQ)
    zero = rows[0][:, :LAGQ]
    two = rows[2][:, :LAGQ]
    odd = np.concatenate([rows[1], rows[3]], axis=0)
    return [table.astype(np.float32).astype(ml_dtypes.bfloat16) for table in (zero, two, odd)]


def two_terms(values):
    high = values.astype(jnp.bfloat16)
    low = (values - high.astype(jnp.float32)).astype(jnp.bfloat16)
    return high, low


def two_term_dot(values_ref, table):
    rows = values_ref.shape[0] // 2
    both = jnp.dot(values_ref[...], table, preferred_element_type=jnp.float32)
    return both[:rows] + both[rows:]


def ranks(mask_row):
    shape = (LANES, LANES)
    upto = lax.broadcasted_iota(jnp.int32, shape, 0) <= lax.broadcasted_iota(jnp.int32, shape, 1)
    row = jnp.broadcast_to(mask_row, (META, LANES)).astype(jnp.bfloat16)
    count = jnp.dot(row, upto.astype(jnp.float32).astype(jnp.bfloat16), preferred_element_type=jnp.float32)
    return jnp.where(mask_row > 0, count[0:1] - 1.0, -1.0)


def sorted_rows(mask_row):
    rank = ranks(mask_row)
    rows = []
    for seg in range(2):
        row, below, done = jnp.full_like(rank, -1.0), 0, 0
        for tier in TIERS:
            inside = (rank >= below) & (rank < below + tier)
            row = jnp.where(inside, rank - below + done + seg * tier, row)
            below, done = below + tier, done + 2 * tier
        rows.append(row)
    rows = jnp.concatenate(rows, axis=1)
    return rows == lax.broadcasted_iota(jnp.int32, (PAIR, PAIR), 0).astype(jnp.float32)


def place_order():
    place = lax.broadcasted_iota(jnp.int32, (PAIR, PAIR), 0)
    row = lax.broadcasted_iota(jnp.int32, (PAIR, PAIR), 1)
    inside = place % LANES
    return (place // LANES) * LANES + (inside % G) * (LANES // G) + inside // G == row


def spectra_kernel(relative, with_meta, kept, skip, alone, *refs):
    f32, bf16 = jnp.float32, jnp.bfloat16
    refs = list(refs)
    here_ref = refs.pop(0) if relative else None
    x_any, mask_any, owner_any, bins_any, even_any, odd_any, band_any = refs[:7]
    x_refs, even_ref, odd_ref, band_ref, mask_ref, owner_ref, bins_ref = refs[-16:-9]
    x_came, arrived, plus, minus, v, ab, early, others, windows = refs[-9:]
    out_refs = refs[7:-17] if relative else refs[7:-16]
    head = refs[-17] if relative else out_refs[0]
    spares = out_refs[1 - len(TIERS):] if kept < PAIR else []
    step, steps = pl.program_id(0), pl.num_programs(0)
    first = step == 0
    rows = x_refs.shape[1]
    slot = 0 if alone else lax.rem(step, 2)
    at_first = (lambda act: act()) if alone else pl.when(first)
    moves = ((even_any, even_ref), (odd_any, odd_ref), (band_any, band_ref))
    moves += ((mask_any, mask_ref),)
    if with_meta:
        moves += ((owner_any, owner_ref), (bins_any, bins_ref))
    copies = [pltpu.make_async_copy(source, into, arrived.at[i]) for i, (source, into) in enumerate(moves)]

    def trace_copy(block, slot):
        at = pl.ds(pl.multiple_of(block * rows + skip, LANES), rows)
        return pltpu.make_async_copy(x_any.at[at], x_refs.at[slot], x_came.at[slot])

    @at_first
    def start():
        trace_copy(0, 0).start()
        for copy in copies:
            copy.start()

    @at_first
    def table_waits():
        for copy in copies:
            copy.wait()

    mask = mask_ref[...].astype(f32)
    if kept < PAIR:
        chosen = sorted_rows(mask)
    else:
        chosen = place_order() & (jnp.concatenate([mask, mask], axis=1) > 0)
    chosen = chosen.astype(f32).astype(bf16)

    trace_copy(step, slot).wait()

    if not alone:

        @pl.when(step + 1 < steps)
        def ahead():
            trace_copy(step + 1, 1 - slot).start()

    x_ref = x_refs.at[slot]
    x = [x_ref[:, m * QUARTER:(m + 1) * QUARTER].astype(f32) for m in range(FOLD)]
    even, odd = x[0] + x[2], x[1] + x[3]
    u = even + odd
    plus[:rows], plus[rows:] = two_terms(u[:, :EIGHTH] + u[:, EIGHTH:])
    minus[:rows], minus[rows:] = two_terms(u[:, :EIGHTH] - u[:, EIGHTH:])
    u = even - odd
    v[:rows], v[rows:2 * rows] = two_terms(u[:, :EIGHTH])
    v[2 * rows:3 * rows], v[3 * rows:] = two_terms(u[:, EIGHTH:])
    ab[:rows], ab[rows:2 * rows] = two_terms(x[0] - x[2])
    ab[2 * rows:3 * rows], ab[3 * rows:] = two_terms(x[1] - x[3])

    for half, ref in enumerate((plus, minus)):
        both = two_term_dot(ref, even_ref[0, :, half * PAIR:(half + 1) * PAIR])
        early[:, half * LANES:(half + 1) * LANES] = both[:, :LANES]
        early[:, CLASS + half * LANES:CLASS + (half + 1) * LANES] = both[:, LANES:]
    turned = jnp.dot(v[...], even_ref[1], preferred_element_type=f32)
    straight = turned[:rows] + turned[rows:2 * rows]
    turned = turned[2 * rows:3 * rows] + turned[3 * rows:]
    lanes = [slice(i * LANES, (i + 1) * LANES) for i in range(4)]
    early[:, 2 * CLASS:2 * CLASS + LANES] = straight[:, lanes[0]] + turned[:, lanes[2]]
    early[:, 2 * CLASS + LANES:3 * CLASS] = straight[:, lanes[1]] - turned[:, lanes[3]]
    early[:, 3 * CLASS:3 * CLASS + LANES] = straight[:, lanes[2]] - turned[:, lanes[0]]
    early[:, 3 * CLASS + LANES:] = straight[:, lanes[3]] + turned[:, lanes[1]]
    turned = jnp.dot(ab[...], odd_ref[...], preferred_element_type=f32)
    straight = turned[:rows] + turned[rows:2 * rows]
    turned = turned[2 * rows:3 * rows] + turned[3 * rows:]
    columns = [slice(i * CLASS, (i + 1) * CLASS) for i in range(4)]
    others[:, columns[0]] = straight[:, columns[0]] + turned[:, columns[1]]
    others[:, columns[1]] = straight[:, columns[1]] - turned[:, columns[0]]
    others[:, columns[2]] = straight[:, columns[2]] - turned[:, columns[3]]
    others[:, columns[3]] = straight[:, columns[3]] + turned[:, columns[2]]

    holders = [(early, 0), (others, 0), (early, 2 * CLASS), (others, 2 * CLASS)]
    power = []
    for ref, start in holders:
        real, imag = ref[:, start:start + CLASS], ref[:, start + CLASS:start + 2 * CLASS]
        power.append(real * real + imag * imag)
    before = [jnp.zeros_like(power[0]), power[0], power[0] + power[1], power[0] + power[1] + power[2]]
    after = [power[1] + power[2] + power[3], power[2] + power[3], power[3], jnp.zeros_like(power[0])]
    for which in range(FOLD):
        at = slice(which * rows, (which + 1) * rows)
        windows[at, :CLASS] = power[which].astype(bf16)
        windows[at, CLASS:2 * CLASS] = before[which].astype(bf16)
        windows[at, 2 * CLASS:] = after[which].astype(bf16)
    sums = jnp.dot(windows[...], band_ref[...], preferred_element_type=f32)
    weight = []
    for which in range(FOLD):
        lane = lax.broadcasted_iota(jnp.int32, (1, CLASS), 1)
        bin_ = ((lane % LANES) * 2 + lane // LANES) * FOLD + which
        within = jnp.minimum(bin_ + HW, NB - 1) - jnp.maximum(bin_ - HW, 0) + 1
        mean = sums[which * rows:(which + 1) * rows] * (1.0 / within.astype(f32))
        weight.append(lax.rsqrt(mean + EPSILON))
    for piece in range(SLICES):
        ref, column = holders[piece // 2]
        column += (piece % 2) * LANES
        scale = weight[piece // 2][:, (piece % 2) * LANES:(piece % 2 + 1) * LANES]
        real = (ref[:, column:column + LANES] * scale).astype(bf16)
        imag = (ref[:, CLASS + column:CLASS + column + LANES] * scale).astype(bf16)
        both = jnp.concatenate([real, imag], axis=1)
        for pair in range(rows // PAIR):
            sorted_ = jnp.dot(chosen, both[pair * PAIR:(pair + 1) * PAIR], preferred_element_type=f32).astype(bf16)
            head[piece, pair * kept:(pair + 1) * kept, :] = sorted_[:kept]
            start = kept
            for spare, tier in zip(spares, TIERS[1:]):
                spare[piece, pair * 2 * tier:(pair + 1) * 2 * tier, :] = sorted_[start:start + 2 * tier]
                start += 2 * tier
    if with_meta:
        tiles = owner_ref.shape[1]
        labels = (owner_ref[...] * BIN_DEV + bins_ref[...]).astype(f32)
        for piece in range(SLICES):
            at = pl.ds(rows // PAIR * kept, META)
            head[piece, at, :] = jnp.zeros((META, 2 * LANES), bf16)
            head[piece, at, :LANES] = jnp.broadcast_to(mask, (META, LANES)).astype(bf16)
            head[piece, at, LANES:LANES + tiles] = jnp.broadcast_to(labels, (META, tiles)).astype(bf16)
    if relative:
        for other in range(SLICES):
            out_refs[other][...] = head[lax.rem(here_ref[0] + other, SLICES)]


def spectra(traces, mask, owners, bins, first_row, rows, block, kept, here=None, with_meta=False):
    relative = here is not None
    tables = [jnp.asarray(table) for table in forward_tables() + (band_table(),)]
    in_place = pl.BlockSpec(memory_space=pl.ANY)
    f32, bf16 = jnp.float32, jnp.bfloat16
    pairs = block // PAIR
    scratch = [
        pltpu.VMEM((2, block, NT), bf16),
    ] + [pltpu.VMEM(array.shape, array.dtype) for array in (*tables, mask, owners, bins)] + [
        pltpu.SemaphoreType.DMA((2,)),
        pltpu.SemaphoreType.DMA((6,)),
    ]
    scratch += [pltpu.VMEM((terms * block, EIGHTH), bf16) for terms in (2, 2, 4)]
    scratch += [pltpu.VMEM((4 * block, QUARTER), bf16)]
    scratch += [pltpu.VMEM((block, 4 * CLASS), f32)] * 2
    scratch += [pltpu.VMEM((FOLD * block, 3 * CLASS), bf16)]
    if relative:
        scratch = [pltpu.VMEM((SLICES, pairs * kept, 2 * LANES), bf16)] + scratch
        out_specs = [pl.BlockSpec((pairs * kept, 2 * LANES), lambda i, *_: (i, 0))] * SLICES
        out_shape = [jax.ShapeDtypeStruct((rows // PAIR * kept, 2 * LANES), bf16)] * SLICES
    else:
        extra = META if with_meta else 0
        out_specs = [pl.BlockSpec((SLICES, pairs * kept + extra, 2 * LANES), lambda i, *_: (0, i, 0))]
        out_shape = [jax.ShapeDtypeStruct((SLICES, rows // PAIR * kept + extra, 2 * LANES), bf16)]
    for tier in TIERS[1:] if kept < PAIR else ():
        out_specs.append(pl.BlockSpec((SLICES, pairs * 2 * tier, 2 * LANES), lambda i, *_: (0, i, 0)))
        out_shape.append(jax.ShapeDtypeStruct((SLICES, rows // LANES * tier, 2 * LANES), bf16))
    return pl.pallas_call(
        functools.partial(spectra_kernel, relative, with_meta, kept, first_row, rows == block),
        grid_spec=pltpu.PrefetchScalarGridSpec(
            num_scalar_prefetch=1 if relative else 0,
            grid=(rows // block,),
            in_specs=[in_place] * (4 + len(tables)),
            out_specs=out_specs,
            scratch_shapes=scratch,
        ),
        out_shape=out_shape,
        compiler_params=pltpu.CompilerParams(vmem_limit_bytes=VMEM),
        cost_estimate=pl.CostEstimate(
            flops=14 * rows * NB * NB, bytes_accessed=rows * NT * 3 + 8 * NB * NB, transcendentals=rows * NB
        ),
        name="spectra",
    )(*([here] if relative else []), traces, mask, owners, bins, *tables)


def pair_sums(block_refs, pairs, steps, tiles):
    f32 = jnp.float32
    done = 0
    groups, current = [], []
    for pair in pairs:
        members = {m for p in current + [pair] for m in p}
        if current and 4 * (len(current) + 1) + 4 * len(members) > 72:
            groups.append(current)
            current = []
        current = current + [pair]
    groups.append(current)
    for group in groups:
        needed = sorted({m for pair in group for m in pair})

        def body(step, sums):
            at = pl.ds(pl.multiple_of(step * G, G), G)
            real = {m: block_refs[m][at, :LANES].astype(f32) for m in needed}
            imag = {m: block_refs[m][at, LANES:].astype(f32) for m in needed}
            new = []
            for (p, q), (re, im) in zip(group, sums):
                re = re + (real[p] * real[q] + imag[p] * imag[q])
                im = im + (imag[p] * real[q] - real[p] * imag[q])
                new.append((re, im))
            return tuple(new)

        zero = jnp.zeros((G, LANES), f32)
        sums = lax.fori_loop(0, steps, body, tuple((zero, zero) for _ in group), unroll=4)
        for re, im in sums:
            tiles[done:done + G, :LANES] = re
            tiles[done:done + G, LANES:] = im
            done += G


def place_rows(head_ref, spare_refs, first_pair, places, out_ref):
    for pair in range(out_ref.shape[0] // PAIR):
        rows = [head_ref[pair * KEPT:(pair + 1) * KEPT]]
        for spare_ref, tier in zip(spare_refs, TIERS[1:]):
            at = (first_pair + pair) * 2 * tier
            rows.append(spare_ref[at:at + 2 * tier])
        placed = jnp.dot(places, jnp.concatenate(rows, axis=0), preferred_element_type=jnp.float32)
        out_ref[pair * PAIR:(pair + 1) * PAIR, :] = placed.astype(out_ref.dtype)


def cross_kernel(plan, here_ref, *refs):
    f32 = jnp.float32
    refs = list(refs)
    take = lambda count: [refs.pop(0) for _ in range(count)]
    ready, heads = take(plan["ready"]), take(plan["heads"])
    *spare_refs, places_ref = take(len(TIERS)) if heads else [None]
    (rows_ref,) = take(1)
    before_ref = refs.pop(0) if plan["before"] else None
    out_ref = refs.pop(0)
    placed = take(len(plan["slots"])) if plan["hand_on"] else None
    tiles = refs.pop(0)
    if plan["stacked"]:
        source = heads[0] if heads else ready[0]
        count = source.shape[0]
        heads = [source.at[m] for m in range(count)] if heads else []
        ready = [] if heads else [source.at[m] for m in range(count)]
    if heads:
        if placed is None:
            (room,) = refs
            placed = [room.at[i] for i in range(len(heads))]
        for i, head in enumerate(heads):
            block = i if plan["stacked"] else lax.rem(here_ref[0] - plan["slots"][i] + SLICES, SLICES)
            spares = [spare_ref.at[block] for spare_ref in spare_refs]
            place_rows(head, spares, plan["first_pair"], places_ref[block], placed[i])
        ready = ready + placed
    pair_sums(ready, plan["pairs"], plan["steps"], tiles)
    bins, count = out_ref.shape[-2], tiles.shape[0]
    wanted = rows_ref[0:1, :] == lax.broadcasted_iota(jnp.int32, (bins, count), 0).astype(f32)
    high, low = two_terms(tiles[...])
    stacked = []
    for half in range(2):
        weights = jnp.where(wanted, jnp.broadcast_to(rows_ref[half + 1:half + 2, :], (bins, count)), 0.0)
        weights = jnp.concatenate(two_terms(weights), axis=0)
        at = slice(half * LANES, (half + 1) * LANES)
        both = jnp.dot(weights, high[:, at], preferred_element_type=f32)
        both = both[:bins] + both[bins:]
        stacked.append(both + jnp.dot(weights[:bins], low[:, at], preferred_element_type=f32))
    stacked = jnp.concatenate(stacked, axis=1)
    if before_ref is not None:
        stacked += before_ref[...]
    if len(out_ref.shape) == 2:
        out_ref[...] = stacked
    else:
        for copy in range(out_ref.shape[0]):
            out_ref[copy] = stacked.astype(out_ref.dtype)


def cross(here, pairs, steps, bins, weights, ready=(), heads=(), slots=(), spares=(), first_pair=0, places=None,
          before=None, copies=None, hand_on=False, stacked=False):
    shape = (bins, 2 * LANES)
    inputs = list(ready) + list(heads) + (list(spares) + [places] if heads else []) + [weights]
    if before is not None:
        inputs.append(before)
    if copies is None:
        out_shape = [jax.ShapeDtypeStruct(shape, jnp.float32)]
    else:
        out_shape = [jax.ShapeDtypeStruct((copies,) + shape, jnp.bfloat16)]
    scratch = [pltpu.VMEM((len(pairs) * G, 2 * LANES), jnp.float32)]
    if hand_on:
        out_shape += [jax.ShapeDtypeStruct((G * steps, 2 * LANES), jnp.bfloat16)] * len(heads)
    elif heads:
        count = heads[0].shape[0] if stacked else len(heads)
        scratch.append(pltpu.VMEM((count, G * steps, 2 * LANES), jnp.bfloat16))
    plan = dict(
        ready=len(ready), heads=len(heads), slots=slots, before=before is not None, hand_on=hand_on,
        stacked=stacked, first_pair=first_pair, pairs=pairs, steps=steps,
    )
    result = pl.pallas_call(
        functools.partial(cross_kernel, plan),
        in_specs=[pl.BlockSpec(memory_space=pltpu.SMEM)] + [pl.BlockSpec(memory_space=pltpu.VMEM)] * len(inputs),
        out_shape=out_shape,
        scratch_shapes=scratch,
        compiler_params=pltpu.CompilerParams(vmem_limit_bytes=VMEM if stacked and copies else VMEM_SMALL),
        cost_estimate=pl.CostEstimate(
            flops=8 * G * steps * LANES * len(pairs), bytes_accessed=4 * G * steps * LANES * len(pairs), transcendentals=0
        ),
        name="cross",
    )(here, *inputs)
    return result if hand_on else result[0]


def weights_kernel(blocks, total_segs, here_ref, meta_ref, *refs):
    f32, bf16 = jnp.float32, jnp.bfloat16
    meta = jnp.concatenate([meta_ref[b, 0:1, :] for b in range(blocks)], axis=0)
    masks, labels = meta[:, :LANES], meta[:, LANES:]
    empty = jnp.zeros((R, LANES), bf16)
    padded = jnp.concatenate([masks.astype(f32), empty.astype(f32)], axis=0)
    half = len(refs) // 2
    places_ref = refs[-1]
    in_place = place_order().astype(f32).astype(bf16)
    for b in range(blocks):
        rows = sorted_rows(masks[b:b + 1].astype(f32)).astype(f32).astype(bf16)
        places = lax.dot_general(in_place, rows, (((1,), (1,)), ((), ())), preferred_element_type=f32)
        places_ref[b] = places.astype(bf16)
    for ends_ref, out_ref in zip(refs[:half], refs[half:-1]):
        lanes = out_ref.shape[1]
        first, second = ends_ref[0:1, :], ends_ref[1:2, :]
        slots = first < 0
        held = [jnp.where(slots, lax.rem(here_ref[0] + end + 2 * blocks, blocks), end) for end in (first, second)]
        low, far = jnp.minimum(held[0], held[1]), jnp.abs(held[0] - held[1])
        sign = jnp.where(held[0] < held[1], 1.0, -1.0)
        block = lax.broadcasted_iota(jnp.int32, (blocks, lanes), 0)
        group = lax.broadcasted_iota(jnp.int32, (LANES, lanes), 1) % G
        place = lax.broadcasted_iota(jnp.int32, (LANES, lanes), 0)
        chosen = (place == (far - 1) * G + group).astype(f32).astype(bf16)
        label = jnp.dot(labels, chosen, preferred_element_type=f32)
        label = jnp.sum(jnp.where(block == low, label, 0.0), axis=0, keepdims=True)
        member = (place // (LANES // G) == group).astype(f32).astype(bf16)
        count = jnp.zeros((1, lanes), f32)
        for d in range(1, R + 1):
            both = (padded[:blocks] * padded[d:d + blocks]).astype(bf16)
            of_block = jnp.dot(both, member, preferred_element_type=f32)
            count += jnp.sum(jnp.where((block == low) & (far == d), of_block, 0.0), axis=0, keepdims=True)
        scale = jnp.where(far <= R, 1.0 / (total_segs * jnp.maximum(count, 1.0)), 0.0)
        out_ref[...] = jnp.concatenate([label, scale, scale * sign, jnp.zeros((5, lanes), f32)], axis=0)


def pair_weights(here, meta, at, total_segs, pair_lists):
    blocks = meta.shape[0]
    ends = [jnp.asarray(np.repeat(np.array(pairs, np.int32).T, G, axis=1)) for pairs in pair_lists]
    whole = lambda shape: pl.BlockSpec(shape, lambda i, *_: (0, 0))
    shapes = [(8, G * len(pairs)) for pairs in pair_lists]
    return pl.pallas_call(
        functools.partial(weights_kernel, blocks, total_segs),
        grid_spec=pltpu.PrefetchScalarGridSpec(
            num_scalar_prefetch=1,
            grid=(1,),
            in_specs=[pl.BlockSpec((blocks, META, 2 * LANES), lambda i, *_: (0, at // META, 0))]
            + [whole(end.shape) for end in ends],
            out_specs=[whole(shape) for shape in shapes]
            + [pl.BlockSpec((blocks, PAIR, PAIR), lambda i, *_: (0, 0, 0))],
        ),
        out_shape=[jax.ShapeDtypeStruct(shape, jnp.float32) for shape in shapes]
        + [jax.ShapeDtypeStruct((blocks, PAIR, PAIR), jnp.bfloat16)],
        compiler_params=pltpu.CompilerParams(vmem_limit_bytes=VMEM_SMALL),
        name="weights",
    )(here, meta, *ends)


def lags_kernel(stacks_ref, zero_ref, two_ref, odd_ref, out_ref):
    f32 = jnp.float32
    copies = stacks_ref.shape[0] // SLICES
    pieces = []
    for piece in range(SLICES):
        total = stacks_ref[piece].astype(f32)
        for copy in range(1, copies):
            total += stacks_ref[copy * SLICES + piece].astype(f32)
        pieces.append(total)

    def product(values, table):
        both = jnp.dot(jnp.concatenate(two_terms(values), axis=0), table, preferred_element_type=f32)
        return both[:BIN_DEV] + both[BIN_DEV:]

    zero = product(jnp.concatenate(pieces[0:2], axis=1), zero_ref[...])
    two = product(jnp.concatenate(pieces[4:6], axis=1), two_ref[...])
    odd = product(jnp.concatenate(pieces[2:4] + pieces[6:8], axis=1), odd_ref[...])
    plus, minus = zero + two, zero - two
    out_ref[:, :LAGQ] = plus + odd[:, :LAGQ]
    out_ref[:, LAGQ:2 * LAGQ] = minus + odd[:, LAGQ:]
    out_ref[:, 2 * LAGQ:3 * LAGQ] = plus - odd[:, :LAGQ]
    out_ref[:, 3 * LAGQ:] = minus - odd[:, LAGQ:]


def lags(stacks):
    tables = [jnp.asarray(table) for table in inverse_tables()]
    return pl.pallas_call(
        lags_kernel,
        out_shape=jax.ShapeDtypeStruct((BIN_DEV, NLAG), jnp.float32),
        compiler_params=pltpu.CompilerParams(vmem_limit_bytes=VMEM_SMALL),
        name="lags",
    )(stacks, *tables)


def fixed_pairs(blocks):
    return [(b, b + d) for b in range(blocks) for d in range(1, R + 1) if b + d < blocks]


def sent_along(x, mask, owners, bins, total_segs):
    seg_count = lax.axis_size("seg")
    count = lax.axis_size("chan")
    early = EARLY_SEGS * LANES
    late = x.shape[0] - early
    here = lax.axis_index("chan").astype(jnp.int32).reshape(1)
    first, *spare_early = spectra(x, mask, owners, bins, 0, early, early, KEPT, with_meta=True)
    first = lax.all_to_all(first, "chan", split_axis=0, concat_axis=0, tiled=True)
    second = list(spectra(x, mask, owners, bins, early, late, PAIR, KEPT, here=here))
    spare_late = second[SLICES:]
    at = early // PAIR * KEPT
    most = jnp.max(jnp.sum(first[:, at, :LANES].astype(jnp.float32), axis=1))
    spares, below = [], TIERS[0]
    for tier, *parts in zip(TIERS[1:], spare_early, spare_late):
        spares.append(lax.cond(
            most > below,
            lambda parts: lax.all_to_all(jnp.concatenate(parts, axis=1), "chan", split_axis=0, concat_axis=0, tiled=True),
            lambda parts: jnp.zeros((count, sum(part.shape[1] for part in parts), 2 * LANES), jnp.bfloat16),
            parts,
        ))
        below += tier

    *late_sent, _ = lax.optimization_barrier((second[SENT[-2]], second[SENT[-1]], tuple(spares)))
    second[SENT[-2]], second[SENT[-1]] = late_sent
    slots = {0: second[0]}
    for shift in SENT:
        slots[shift] = lax.ppermute(second[shift], "chan", [(i, (i + shift) % count) for i in range(count)])

    fixed = fixed_pairs(count)
    known = (0,) + SENT
    stages = [
        [(i, j) for j in range(start, end) for i in range(j)] for start, end in zip((1,) + STAGES, STAGES)
    ]
    as_slots = lambda pairs: [(-known[i] - count, -known[j] - count) for i, j in pairs]
    weights = pair_weights(here, first, at, total_segs, [fixed] + [as_slots(pairs) for pairs in stages])
    places = weights[-1]
    bins = count * BIN_DEV
    stacks = cross(
        here, fixed, early // G, bins, weights[0], heads=[first], spares=spares, places=places, stacked=True
    )
    ready, start = [], 0
    for end, pairs, weight in zip(STAGES, stages, weights[1:]):
        final = end == len(known)
        result = cross(
            here, pairs, late // G, bins, weight,
            ready=ready, heads=[slots[slot] for slot in known[start:end]], slots=known[start:end],
            spares=spares, first_pair=early // PAIR, places=places, before=stacks,
            copies=seg_count if final else None, hand_on=not final,
        )
        if final:
            return result
        stacks, ready, start = result[0], ready + list(result[1:]), end


def sent_at_once(x, mask, owners, bins, total_segs):
    seg_count = lax.axis_size("seg")
    count = lax.axis_size("chan")
    rows, chans = x.shape[0], mask.shape[1]
    narrow = NB // count
    splits = LANES // narrow
    here = lax.axis_index("chan").astype(jnp.int32).reshape(1)
    own = jnp.concatenate([mask, owners * BIN_DEV + bins], axis=1)
    every = lax.all_gather(own, "chan", axis=0, tiled=True).astype(jnp.bfloat16)
    every = jnp.pad(every, ((0, 0), (0, 2 * LANES - every.shape[1])))
    every = jnp.broadcast_to(every[:, None, :], (count, META, 2 * LANES))
    fixed = fixed_pairs(count)
    weights = pair_weights(here, every, 0, total_segs, [fixed])[:1]
    (outgoing,) = spectra(x, mask, owners, bins, 0, rows, PAIR, PAIR)
    outgoing = outgoing.reshape(SLICES, rows, 2, splits, narrow).transpose(0, 3, 1, 2, 4)
    outgoing = outgoing.reshape(count, rows, 2 * narrow)
    wide = lax.all_to_all(outgoing, "chan", split_axis=0, concat_axis=0, tiled=True)
    wide = jnp.pad(wide.reshape(count, rows, 2, narrow), ((0, 0), (0, 0), (0, 0), (0, LANES - narrow)))
    wide = wide.reshape(count, rows, 2 * LANES)
    stacks = cross(
        here, fixed, rows // G, count * BIN_DEV, weights[0], ready=[wide], copies=seg_count, stacked=True
    )
    return stacks.reshape(-1, 2, LANES)[..., :narrow]


def per_device(traces, channel_mask, owner_ids, local_bins):
    seg_count = lax.axis_size("seg")
    count = lax.axis_size("chan")
    segs, chans, length = traces.shape
    x = traces.reshape(segs * chans, length)
    mask = channel_mask.reshape(1, chans)
    owners = owner_ids.reshape(1, -1)
    if count == SLICES:
        stacks = sent_along(x, mask, owners, local_bins, segs * seg_count)
        stacks = stacks.reshape(seg_count * count, BIN_DEV, 2 * LANES)
        stacks = lax.all_to_all(stacks, ("seg", "chan"), split_axis=0, concat_axis=0, tiled=True)
    else:
        narrow = NB // count
        stacks = sent_at_once(x, mask, owners, local_bins, segs * seg_count)
        stacks = stacks.reshape(seg_count * count, BIN_DEV, 2 * narrow)
        stacks = lax.all_to_all(stacks, ("seg", "chan"), split_axis=0, concat_axis=0, tiled=True)
        stacks = stacks.reshape(seg_count, SLICES, count // SLICES, BIN_DEV, 2, narrow)
        stacks = stacks.transpose(0, 1, 3, 4, 2, 5).reshape(seg_count * SLICES, BIN_DEV, 2 * LANES)
    return lags(stacks)


def solution(mesh):
    in_specs = (P("seg", "chan", None), P("chan"), P("chan", None, None), P("chan", None))
    out_specs = P("chan", None)
    return jax.shard_map(
        per_device, mesh=mesh, in_specs=in_specs, out_specs=out_specs, check_vma=False
    )
```
